128 devices in a mesh: memory: 4 (over z), context: 16 (over x, y), dp: 2 (over core).
Axes of the slice: x: 4, y: 4, z: 4, core: 2. Of those that a mesh axis runs over, the one named last changes fastest.
Arguments:
- hidden: bfloat16 [32, 512, 4096], P(('context', 'dp'), 'memory'), may hold values from -6 to 6
- queries: bfloat16 [32, 512, 2048], P(('context', 'dp'), 'memory'), may hold values from -6 to 6
- route_ids: int32 [32, 512, 2], P(('context', 'dp'), 'memory'), may hold values from 0 to 3, all different within a row; in each aligned block of 128 rows (0 to 127, 128 to 255, ..., all dimensions but the last counted through in order) at most 80 rows name the same one
- router_weight: bfloat16 [4096, 4], replicated, may hold values from -0.09375 to 0.09375
- key_weight: bfloat16 [4, 4096, 2048], P('memory', None, 'dp'), may hold values from -0.09375 to 0.09375
- value_weight: bfloat16 [4, 4096, 2048], P('memory', None, 'dp'), may hold values from -0.09375 to 0.09375
- decay_weight: bfloat16 [4, 4096, 16], P('memory', None, 'dp'), may hold values from -0.046875 to 0.046875
- decay_bias: float32 [4, 16], P('memory', 'dp'), may hold values from 3 to 14
- norm_gain: float32 [2048], replicated, may hold values from 0.5 to 1.5
Outputs:
- mixed: bfloat16 [32, 512, 2048], P(('context', 'dp'), 'memory')
The draws below stay inside these ranges and needn't reach their ends.
Inputs may be any that keep to these rules, and one draw needn't show every extreme that they name: `route_ids`: each token names 2 different memories. Within the tokens of one device (aligned blocks of 128 tokens in token order) no memory is named by more than 80 tokens, and in some such block one memory is named exactly 80 times.
All inputs are finite; a program needn't handle non-finite values.
Results may differ from the reference program's by a relative error of at most 0.0085.
Values may be sent and summed in bfloat16 or wider, within the bound.
No kernel may reach another device: no remote copies, remote signals or barrier semaphores. Data moves between devices by JAX's collectives and lax.ppermute only.
A program may use at most 128 MiB of HBM per device.

```python
import math
import jax
import jax.numpy as jnp
import numpy as np
from jax import lax

D = 4096
HEADS = 16
HEAD_DIM = 128
TOP = 2
BLOCK = 64
ROWS = 128
CAP = 80
MEMORIES = 4
HK = 2048
SEGS = 32
SEG_LEN = 512
TOKENS = 16384


def shard_levels(stream_key, shape, split, smallest, top_value):
    factor_of, own = 1.0, jax.random.fold_in(stream_key, 6)
    for axis_at, blocks in split:
        steps = jnp.exp(jax.random.uniform(jax.random.fold_in(own, axis_at), (blocks,), jnp.float32, smallest / len(split), top_value / len(split)))
        factor_of = factor_of * jnp.repeat(steps, shape[axis_at] // blocks).reshape([-1 if axis == axis_at else 1 for axis in range(len(shape))])
    return factor_of


def assign_block(rng, own, number, rows, amount, top, limit, lean):
    ranking = jax.random.permutation(rng, amount)
    packed, usual = shares(amount, rows * top, limit, lean, True), shares(amount, rows * top, limit, lean, False)
    places = jnp.arange(amount)

    def named(sizes, rotation):
        used = int((sizes > 0).sum())
        fixed = max(1, used // 4)
        passed = fixed + (places - fixed + rotation * (used - fixed)) % max(1, amount - fixed)
        return jnp.zeros((amount,), jnp.int32).at[ranking[jnp.where(places < fixed, places, passed)]].set(jnp.asarray(sizes, jnp.int32))

    sizes = jnp.where(number % 4 == 0, named(packed, number // 4), named(usual, number - number // 4 - 1))
    mixed = jax.random.permutation(jax.random.fold_in(own, 3), amount)
    source_of, receiver = mixed[0:amount // 2 * 2:2], mixed[1:amount // 2 * 2:2]
    margin = jnp.minimum(sizes[source_of] - 1, limit - sizes[receiver]) // 2
    margin = jnp.where((source_of == ranking[0]) | (receiver == ranking[0]) | (sizes[receiver] == 0), 0, jnp.maximum(margin, 0))
    passed = jax.random.randint(jax.random.fold_in(own, 4), (amount // 2,), 0, 1 << 20) % (margin + 1)
    sizes = sizes.at[source_of].add(-passed).at[receiver].add(passed)
    labels = jnp.searchsorted(jnp.cumsum(sizes), jnp.arange(rows * top), side="right").astype(jnp.int32)
    listing = labels.reshape(top, rows).T
    listing = listing[jax.random.permutation(jax.random.fold_in(own, 1), rows)]
    rotation = jax.random.randint(jax.random.fold_in(own, 2), (rows, 1), 0, top)
    return jnp.take_along_axis(listing, (jnp.arange(top)[None, :] + rotation) % top, axis=1)


def shares(amount, total, bound, slope, full):
    portions = [(1 << 20) // math.isqrt(grade ** slope) + 1 for grade in range(1, amount + 1)]
    largest = bound if full else min(bound, max(-(-total // amount), total * portions[0] // sum(portions)))
    least = 1 if total - largest >= amount - 1 else 0
    given, rest = [largest] + [least] * (amount - 1), total - largest - least * (amount - 1)
    while rest > 0:
        movable = [i for i in range(1, amount) if given[i] < largest] or [i for i in range(1, amount) if given[i] < bound]
        pool, left = sum([portions[i] for i in movable]), rest
        for i in movable:
            more = min(bound - given[i], max(1, left * portions[i] // pool), rest)
            given[i] = given[i] + more
            rest = rest - more
    return np.array(given)


def bell_draw(stream_key, shape, deviation, most, shards=(), dtype=jnp.bfloat16):
    drawn = deviation * jax.random.normal(stream_key, shape, jnp.float32)
    if shards:
        drawn = drawn * shard_levels(stream_key, shape, shards, -0.22, 0.18)
    return jnp.clip(drawn, -most, most).astype(dtype)


def setup_inputs(seed: int = 0) -> dict:
    keys = jax.random.split(jax.random.key(seed), 10)
    hidden = bell_draw(keys[0], (SEGS, SEG_LEN, D), 1.0, 6.0, ((0, 32), (1, 4)))
    queries = bell_draw(keys[1], (SEGS, SEG_LEN, HK), 1.0, 6.0, ((0, 32), (1, 4)))
    route_ids_keys = jax.random.split(jax.random.fold_in(keys[2], 1), SEGS * SEG_LEN // ROWS)
    route_ids_turns = jax.random.permutation(jax.random.fold_in(keys[2], 3), SEGS * SEG_LEN // ROWS)
    route_ids = jax.vmap(lambda own, number: assign_block(jax.random.fold_in(keys[2], 2), own, number, ROWS, MEMORIES, TOP, CAP, 2))(route_ids_keys, route_ids_turns).reshape((SEGS, SEG_LEN, TOP))
    router_weight = bell_draw(keys[3], (D, MEMORIES), D ** -0.5, 0.09375)
    key_weight = bell_draw(keys[4], (MEMORIES, D, HK), D ** -0.5, 0.09375, ((0, 4), (2, 2)))
    value_weight = bell_draw(keys[5], (MEMORIES, D, HK), D ** -0.5, 0.09375, ((0, 4), (2, 2)))
    decay_weight = bell_draw(keys[6], (MEMORIES, D, HEADS), (4 * D) ** -0.5, 0.046875, ((0, 4), (2, 2)))
    decay_bias = jnp.clip(3.0 + 11.0 * jax.random.uniform(keys[7], (MEMORIES, HEADS), jnp.float32) ** shard_levels(keys[7], (MEMORIES, HEADS), ((0, 4), (1, 2)), -0.2, 0.2), 3.0, 14.0)
    norm_gain = jnp.clip(1.0 + 0.1 * jax.random.normal(keys[8], (HK,), jnp.float32), 0.5, 1.5)
    return dict(hidden=hidden, queries=queries, route_ids=route_ids, router_weight=router_weight, key_weight=key_weight, value_weight=value_weight, decay_weight=decay_weight, decay_bias=decay_bias, norm_gain=norm_gain)


HIGHEST = lax.Precision.HIGHEST

def block_scan(query_all, unit_all, value_all, decay_all):
    seq_len, head_count, head_width = query_all.shape
    block_count = seq_len // BLOCK

    def shaped(tensor):
        return tensor.reshape((block_count, BLOCK) + tensor.shape[1:])
    causal = jnp.arange(BLOCK)[:, None] >= jnp.arange(BLOCK)[None, :]

    def advance(carry, pieces):
        memory_state, running = carry
        query_blk, unit_blk, value_blk, decay_blk = pieces
        query_wide = query_blk.astype(jnp.float32)
        unit_wide = unit_blk.astype(jnp.float32)
        value_wide = value_blk.astype(jnp.float32)
        cumulative = jnp.cumsum(decay_blk, axis=0)
        spread = cumulative[:, None, :] - cumulative[None, :, :]
        weights = jnp.exp(jnp.where(causal[:, :, None], spread, -1e+30))
        scores = jnp.einsum('ihd,jhd->ijh', query_wide, unit_wide, precision=HIGHEST) * weights
        scores = scores.astype(jnp.bfloat16).astype(jnp.float32)
        inner = jnp.einsum('ijh,jhe->ihe', scores, value_wide, precision=HIGHEST)
        carried = jnp.exp(cumulative)[:, :, None] * jnp.einsum('ihd,hde->ihe', query_wide, memory_state, precision=HIGHEST)
        last_sum = cumulative[-1]
        faded = jnp.exp(last_sum[None, :] - cumulative)[:, :, None] * unit_wide
        memory_state = jnp.exp(last_sum)[:, None, None] * memory_state + jnp.einsum('jhd,jhe->hde', faded, value_wide, precision=HIGHEST)
        return ((memory_state, running + last_sum), (inner + carried, running[None, :] + cumulative))
    start_state = jnp.zeros((head_count, head_width, head_width), jnp.float32)
    start_total = jnp.zeros((head_count,), jnp.float32)
    pieces = (shaped(query_all), shaped(unit_all), shaped(value_all), shaped(decay_all))
    (end_state, end_total), (outputs, positions) = lax.scan(advance, (start_state, start_total), pieces)
    return (outputs.reshape(seq_len, head_count, head_width), positions.reshape(seq_len, head_count), end_state, end_total)

def project_rows(hidden_rows, key_matrix, value_matrix, decay_matrix, decay_shift, live_slots):
    seq_len = hidden_rows.shape[0]
    head_count = decay_matrix.shape[1]
    keys_low = jnp.dot(hidden_rows, key_matrix, preferred_element_type=jnp.float32).astype(jnp.bfloat16)
    values_low = jnp.dot(hidden_rows, value_matrix, preferred_element_type=jnp.float32).astype(jnp.bfloat16)
    gate_logit = jnp.dot(hidden_rows, decay_matrix, preferred_element_type=jnp.float32) + decay_shift[None, :]
    decays = jax.nn.log_sigmoid(gate_logit) * live_slots[:, None]
    keys_full = keys_low.astype(jnp.float32).reshape(seq_len, head_count, HEAD_DIM)
    unit_keys = keys_full * lax.rsqrt(lax.optimization_barrier(jnp.sum(keys_full * keys_full, axis=-1, keepdims=True)) + 1e-06)
    unit_keys = (unit_keys * live_slots[:, None, None]).astype(jnp.bfloat16)
    values_out = values_low.reshape(seq_len, head_count, HEAD_DIM)
    return (unit_keys, values_out, decays)

def reference(hidden, queries, route_ids, router_weight, key_weight, value_weight, decay_weight, decay_bias, norm_gain):
    tokens_flat = hidden.reshape(TOKENS, D)
    query_flat = queries.reshape(TOKENS, HK)
    route_flat = route_ids.reshape(TOKENS, TOP)
    router = jnp.dot(tokens_flat, router_weight, preferred_element_type=jnp.float32)
    chosen = jax.nn.sigmoid(jnp.take_along_axis(router, route_flat, axis=1))
    gates = chosen / lax.optimization_barrier(jnp.sum(chosen, axis=1, keepdims=True))
    mixture = jnp.zeros((TOKENS, HK), jnp.float32)
    slot_total = SEGS * MEMORIES * CAP
    for memory in range(MEMORIES):
        named = route_flat == memory
        member = jnp.any(named, axis=1)
        ordering = jnp.argsort(jnp.where(member, 0, 1).astype(jnp.int32), stable=True)[:slot_total].astype(jnp.int32)
        live_slots = member[ordering].astype(jnp.float32)
        unit_keys, values_out, decays = project_rows(tokens_flat[ordering], key_weight[memory], value_weight[memory], decay_weight[memory], decay_bias[memory], live_slots)
        query_rows = query_flat[ordering].reshape(slot_total, HEADS, HEAD_DIM)
        outputs = block_scan(query_rows, unit_keys, values_out, decays)[0]
        reads = outputs.reshape(slot_total, HK).astype(jnp.bfloat16).astype(jnp.float32)
        placed = jnp.zeros((TOKENS, HK), jnp.float32).at[ordering].set(reads * live_slots[:, None])
        weight_here = lax.optimization_barrier(jnp.sum(gates * named.astype(jnp.float32), axis=1))
        mixture = mixture + weight_here[:, None] * placed
    per_head = mixture.reshape(TOKENS, HEADS, HEAD_DIM)
    per_head = per_head * lax.rsqrt(lax.optimization_barrier(jnp.mean(per_head * per_head, axis=-1, keepdims=True)) + 1e-05)
    result = per_head * norm_gain.reshape(HEADS, HEAD_DIM)[None]
    return result.reshape(SEGS, SEG_LEN, HK).astype(jnp.bfloat16)
```

```python
import functools

import jax
import jax.numpy as jnp
from jax import lax
from jax.experimental import pallas as pl
from jax.experimental.pallas import tpu as pltpu
from jax.sharding import PartitionSpec as P

D = 4096
HEAD_DIM = 128
CAP = 80
ROWS = 128
OWNERS = 4
CHUNKS = 8
SLOTS = CHUNKS * CAP
HALF = 1024
HEADS = HALF // HEAD_DIM
CONTEXTS = 16
LIVE = 128
PIECE = HALF // CONTEXTS
TAIL = 16
F32 = jnp.float32
BF16 = jnp.bfloat16
MIB = 1 << 20


def iota(shape, axis):
    return lax.broadcasted_iota(jnp.int32, shape, axis)


def dot(a, b):
    return jnp.dot(a, b, preferred_element_type=F32)


def source(owner, shift):
    return (owner + OWNERS - shift) & (OWNERS - 1)


def position(shift, partner, owner, core):
    return (core ^ partner) * OWNERS + source(owner, shift)


def membership(route):
    lane = iota((ROWS, 128), 1)
    named = ((route[:, 0:1] == lane) | (route[:, 1:2] == lane)).astype(F32)
    before = (iota((ROWS, ROWS), 0) > iota((ROWS, ROWS), 1)).astype(F32).astype(BF16)
    return named, dot(before, named.astype(BF16))


def pick_lane(table, lane_at):
    return jnp.sum(jnp.where(iota(table.shape, 1) == lane_at, table, 0.0), axis=1, keepdims=True)


def one_hot(named, slot, memory):
    live = pick_lane(named, memory) > 0.0
    place = pick_lane(slot, memory)
    match = (iota((ROWS, 128), 1).astype(F32) == place) & live
    return match.astype(F32)


def pack_rows_kernel(route_ref, rows_ref, *out_refs):
    owner = lax.axis_index("memory")
    named, slot = membership(route_ref[...])
    picks = [
        one_hot(named, slot, (owner + shift) & (OWNERS - 1)).T.astype(BF16)[:CAP]
        for shift in range(OWNERS)
    ]
    pick = jnp.concatenate(picks, axis=0)
    width = 512
    for column in range(0, D, width):
        part = dot(pick, rows_ref[:, column : column + width]).astype(BF16)
        for shift in range(OWNERS):
            out_refs[shift][:, column : column + width] = part[shift * CAP : (shift + 1) * CAP]
    live = dot(pick, jnp.ones((ROWS, LIVE), BF16)).astype(BF16)
    for shift in range(OWNERS):
        out_refs[shift][:, D:] = live[shift * CAP : (shift + 1) * CAP]


def pack_rows(route, rows):
    return pl.pallas_call(
        pack_rows_kernel,
        out_shape=[jax.ShapeDtypeStruct((CAP, D + LIVE), BF16)] * OWNERS,
        compiler_params=pltpu.CompilerParams(vmem_limit_bytes=24 * MIB),
        cost_estimate=pl.CostEstimate(
            flops=2 * 320 * 128 * D, bytes_accessed=4 * MIB, transcendentals=0
        ),
        name="pack_rows",
    )(route, rows)


def pack_queries_kernel(
    route_ref, other_route_ref, query_ref, other_query_ref, rows_ref, router_ref, *out_refs
):
    owner, core = lax.axis_index("memory"), lax.axis_index("dp")
    gates_ref = out_refs[OWNERS]
    mine = pl.multiple_of(core * HALF, HALF)
    for place, (routes, queries) in enumerate(
        ((route_ref, query_ref), (other_route_ref, other_query_ref))
    ):
        named, slot = membership(routes[...])
        picks = [
            one_hot(named, slot, (owner + shift) & (OWNERS - 1)).T.astype(BF16)[:CAP]
            for shift in range(OWNERS)
        ]
        pick = jnp.concatenate(picks, axis=0)
        part = dot(pick, queries[:, pl.ds(mine, HALF)]).astype(BF16)
        for shift in range(OWNERS):
            out_refs[shift][core ^ place] = part[shift * CAP : (shift + 1) * CAP]
        if place == 0:
            score = dot(rows_ref[...], router_ref[...])
            chosen = jax.nn.sigmoid(score) * named[:, :OWNERS]
            gates_ref[...] = jnp.zeros((ROWS, 128), F32)
            gates_ref[:, :OWNERS] = chosen / jnp.sum(chosen, axis=1, keepdims=True)


def pack_queries(route, other_route, queries, other_queries, rows, router_weight):
    return pl.pallas_call(
        pack_queries_kernel,
        out_shape=[jax.ShapeDtypeStruct((2, CAP, HALF), BF16)] * OWNERS
        + [jax.ShapeDtypeStruct((ROWS, 128), F32)],
        compiler_params=pltpu.CompilerParams(vmem_limit_bytes=24 * MIB),
        cost_estimate=pl.CostEstimate(
            flops=2 * 640 * 128 * HALF, bytes_accessed=4 * MIB, transcendentals=0
        ),
        name="pack_queries",
    )(route, other_route, queries, other_queries, rows, router_weight)


def log_sigmoid(x):
    small = jnp.exp(-jnp.abs(x))
    near = 1.0 + small
    log1p = jnp.where(near == 1.0, small, jnp.log(near) * (small / jnp.where(near == 1.0, 1.0, near - 1.0)))
    return jnp.minimum(x, 0.0) - log1p


def project_kernel(count, *refs):
    row_refs = refs[:count]
    key_ref, value_ref, decay_ref, bias_ref, unit_out, value_out, decay_out, held = refs[count:]

    @pl.when(pl.program_id(0) == 0)
    def _():
        for at in range(count):
            held[at * CAP : (at + 1) * CAP] = row_refs[at][:, :D]
        gate = dot(held[...], decay_ref[...]) + bias_ref[...]
        decay = log_sigmoid(gate)
        decay_out[...] = jnp.zeros_like(decay_out)
        for at in range(count):
            live = row_refs[at][:, D : D + HEADS].astype(F32)
            decay_out[at, :, :HEADS] = decay[at * CAP : (at + 1) * CAP] * live

    keys = dot(held[...], key_ref[...]).astype(BF16).astype(F32)
    width = keys.shape[1]
    for head in range(width // HEAD_DIM):
        columns = slice(head * HEAD_DIM, (head + 1) * HEAD_DIM)
        key = keys[:, columns]
        unit = key * lax.rsqrt(jnp.sum(key * key, axis=1, keepdims=True) + 1e-06)
        unit_out[:, :, columns] = unit.astype(BF16).reshape(count, CAP, HEAD_DIM)
    values = dot(held[...], value_ref[...]).astype(BF16)
    value_out[...] = values.reshape(count, CAP, width)


def project(row_parts, key_weight, value_weight, decay_weight, decay_bias):
    count = len(row_parts)
    width = 256
    whole = lambda shape: pl.BlockSpec(shape, lambda n: (0,) * len(shape))
    return pl.pallas_call(
        functools.partial(project_kernel, count),
        grid=(HALF // width,),
        in_specs=[whole((CAP, D + LIVE))] * count
        + [
            pl.BlockSpec((D, width), lambda n: (0, n)),
            pl.BlockSpec((D, width), lambda n: (0, n)),
            whole((D, HEADS)),
            whole((1, HEADS)),
        ],
        out_specs=[
            pl.BlockSpec((count, CAP, width), lambda n: (0, 0, n)),
            pl.BlockSpec((count, CAP, width), lambda n: (0, 0, n)),
            whole((count, CAP, 128)),
        ],
        out_shape=[
            jax.ShapeDtypeStruct((count, CAP, HALF), BF16),
            jax.ShapeDtypeStruct((count, CAP, HALF), BF16),
            jax.ShapeDtypeStruct((count, CAP, 128), F32),
        ],
        scratch_shapes=[pltpu.VMEM((count * CAP, D), BF16)],
        compiler_params=pltpu.CompilerParams(vmem_limit_bytes=30 * MIB),
        cost_estimate=pl.CostEstimate(
            flops=2 * count * CAP * D * 2 * HALF, bytes_accessed=18 * MIB, transcendentals=0
        ),
        name=f"project_{count}",
    )(*row_parts, key_weight, value_weight, decay_weight, decay_bias)


GROUPS = (((0, 0), (0, 1)), ((1, 0), (1, 1), (3, 0), (3, 1)), ((2, 0), (2, 1)))


def gather_order(refs, held, columns=slice(None)):
    owner, core = lax.axis_index("memory"), lax.axis_index("dp")
    for group, ref in zip(GROUPS, refs):
        for at, (shift, partner) in enumerate(group):
            held[position(shift, partner, owner, core)] = ref[at, :, columns]


def state_kernel(*refs):
    unit_refs, value_refs, decay_refs = refs[0:3], refs[3:6], refs[6:9]
    message, column_out, row_out, units, values, decays = refs[9:]
    step = pl.program_id(0)

    @pl.when(step == 0)
    def _():
        gather_order(decay_refs, decays)
        total = decays[...].reshape(SLOTS, 128).T[:HEADS]
        lane = iota((HEADS, SLOTS), 1)
        reach = 1
        while reach < SLOTS:
            total = total + jnp.where(lane >= reach, pltpu.roll(total, reach, 1), 0.0)
            reach *= 2
        row_out[...] = total
        column_out[...] = jnp.concatenate(
            [total, jnp.zeros((128 - HEADS, SLOTS), F32)], axis=0
        ).T

    gather_order(unit_refs, units)
    gather_order(value_refs, values)
    for at in range(2):
        head = step * 2 + at
        columns = slice(at * HEAD_DIM, (at + 1) * HEAD_DIM)
        running = pick_lane(column_out[...], head)
        last = running[SLOTS - 1 : SLOTS]
        unit = units[:, :, columns].reshape(SLOTS, HEAD_DIM).astype(F32)
        faded = (unit * jnp.exp(last - running)).astype(BF16)
        value = values[:, :, columns].reshape(SLOTS, HEAD_DIM)
        state = lax.dot_general(
            faded, value, (((0,), (0,)), ((), ())), preferred_element_type=F32
        ).astype(BF16)
        high = jnp.broadcast_to(last, (TAIL, 128)).astype(BF16).astype(F32)
        low = jnp.broadcast_to(last, (TAIL, 128)) - high
        tail = jnp.where(iota((TAIL, 128), 0) < TAIL // 2, high, low).astype(BF16)
        for part in range(2):
            message[at * 2 + part, :PIECE] = state[part * PIECE : (part + 1) * PIECE]
            message[at * 2 + part, PIECE:] = tail


def block_state(units, values, decays):
    whole = lambda shape: pl.BlockSpec(shape, lambda n: (0,) * len(shape))
    chunked = [pl.BlockSpec((len(group), CAP, 256), lambda n: (0, 0, n)) for group in GROUPS]
    return pl.pallas_call(
        state_kernel,
        grid=(HEADS // 2,),
        in_specs=chunked * 2 + [whole((len(group), CAP, 128)) for group in GROUPS],
        out_specs=[
            pl.BlockSpec((4, PIECE + TAIL, 128), lambda n: (n, 0, 0)),
            whole((SLOTS, 128)),
            whole((HEADS, SLOTS)),
        ],
        out_shape=[
            jax.ShapeDtypeStruct((CONTEXTS, PIECE + TAIL, 128), BF16),
            jax.ShapeDtypeStruct((SLOTS, 128), F32),
            jax.ShapeDtypeStruct((HEADS, SLOTS), F32),
        ],
        scratch_shapes=[
            pltpu.VMEM((CHUNKS, CAP, 256), BF16),
            pltpu.VMEM((CHUNKS, CAP, 256), BF16),
            pltpu.VMEM((CHUNKS, CAP, 128), F32),
        ],
        compiler_params=pltpu.CompilerParams(vmem_limit_bytes=24 * MIB),
        cost_estimate=pl.CostEstimate(
            flops=2 * SLOTS * HALF * 128, bytes_accessed=4 * MIB, transcendentals=SLOTS * HEADS
        ),
        name="block_state",
    )(*units, *values, *decays)


def prefix_kernel(message, entry):
    before = jnp.zeros((PIECE, 128), F32)
    for context in range(CONTEXTS):
        entry[context] = before.astype(BF16)
        high = message[context, PIECE : PIECE + 1].astype(F32)
        low = message[context, PIECE + TAIL // 2 : PIECE + TAIL // 2 + 1].astype(F32)
        before = jnp.exp(high + low) * before + message[context, :PIECE].astype(F32)


def prefix(message):
    return pl.pallas_call(
        prefix_kernel,
        out_shape=jax.ShapeDtypeStruct((CONTEXTS, PIECE, 128), BF16),
        cost_estimate=pl.CostEstimate(flops=1 << 20, bytes_accessed=1 << 20, transcendentals=0),
        name="prefix",
    )(message)


def inner_kernel(*refs):
    unit_refs, value_refs, query_refs = refs[0:3], refs[3:6], refs[6:10]
    column_ref, row_ref, inner, units, values, queries = refs[10:]
    step = pl.program_id(0)
    owner = lax.axis_index("memory")
    gather_order(unit_refs, units)
    gather_order(value_refs, values)
    for shift in range(OWNERS):
        for core in range(2):
            queries[core * OWNERS + source(owner, shift)] = query_refs[shift][core]
    tile = 2 * CAP
    for at in range(2):
        head = step * 2 + at
        columns = slice(at * HEAD_DIM, (at + 1) * HEAD_DIM)
        running = pick_lane(column_ref[...], head)
        running_row = row_ref[pl.ds(head, 1), :]
        unit = units[:, :, columns].reshape(SLOTS, HEAD_DIM)
        value = values[:, :, columns].reshape(SLOTS, HEAD_DIM)
        for block in range(SLOTS // tile):
            reach = -(-((block + 1) * tile) // 128) * 128
            query = queries[2 * block : 2 * block + 2, :, columns].reshape(tile, HEAD_DIM)
            score = lax.dot_general(
                query, unit[:reach], (((1,), (1,)), ((), ())), preferred_element_type=F32
            )
            spread = running[block * tile : (block + 1) * tile] - running_row[:, :reach]
            causal = iota((tile, reach), 0) + block * tile >= iota((tile, reach), 1)
            score = (score * jnp.exp(jnp.where(causal, spread, -1e30))).astype(BF16)
            result = dot(score, value[:reach])
            inner[2 * block : 2 * block + 2, :, columns] = result.reshape(2, CAP, HEAD_DIM)


def inner_reads(units, values, queries, column, row):
    whole = lambda shape: pl.BlockSpec(shape, lambda n: (0,) * len(shape))
    chunked = [pl.BlockSpec((len(group), CAP, 256), lambda n: (0, 0, n)) for group in GROUPS]
    return pl.pallas_call(
        inner_kernel,
        grid=(HEADS // 2,),
        in_specs=chunked * 2
        + [pl.BlockSpec((2, CAP, 256), lambda n: (0, 0, n))] * OWNERS
        + [whole((SLOTS, 128)), whole((HEADS, SLOTS))],
        out_specs=pl.BlockSpec((CHUNKS, CAP, 256), lambda n: (0, 0, n)),
        out_shape=jax.ShapeDtypeStruct((CHUNKS, CAP, HALF), F32),
        scratch_shapes=[pltpu.VMEM((CHUNKS, CAP, 256), BF16)] * 3,
        compiler_params=pltpu.CompilerParams(vmem_limit_bytes=24 * MIB),
        cost_estimate=pl.CostEstimate(
            flops=4 * SLOTS * SLOTS * HALF, bytes_accessed=8 * MIB, transcendentals=SLOTS * SLOTS * 4
        ),
        name="inner_reads",
    )(*units, *values, *queries, column, row)


def read_kernel(*refs):
    query_refs = refs[0:4]
    inner, column_ref, entry = refs[4:7]
    out_refs = refs[7:11]
    queries, reads = refs[11:]
    step = pl.program_id(0)
    owner = lax.axis_index("memory")
    for shift in range(OWNERS):
        for core in range(2):
            queries[core * OWNERS + source(owner, shift)] = query_refs[shift][core]
    for at in range(2):
        head = step * 2 + at
        columns = slice(at * HEAD_DIM, (at + 1) * HEAD_DIM)
        fade = jnp.exp(pick_lane(column_ref[...], head))
        carried = dot(queries[:, :, columns].reshape(SLOTS, HEAD_DIM), entry[at])
        result = inner[:, :, columns].reshape(SLOTS, HEAD_DIM) + fade * carried
        reads[:, :, columns] = result.astype(BF16).reshape(CHUNKS, CAP, HEAD_DIM)
    for shift in range(OWNERS):
        for core in range(2):
            out_refs[shift][core] = reads[core * OWNERS + source(owner, shift)]


def read_out(queries, inner, column, entry):
    whole = lambda shape: pl.BlockSpec(shape, lambda n: (0,) * len(shape))
    return pl.pallas_call(
        read_kernel,
        grid=(HEADS // 2,),
        in_specs=[pl.BlockSpec((2, CAP, 256), lambda n: (0, 0, n))] * OWNERS
        + [
            pl.BlockSpec((CHUNKS, CAP, 256), lambda n: (0, 0, n)),
            whole((SLOTS, 128)),
            pl.BlockSpec((2, 128, 128), lambda n: (n, 0, 0)),
        ],
        out_specs=[pl.BlockSpec((2, CAP, 256), lambda n: (0, 0, n))] * OWNERS,
        out_shape=[jax.ShapeDtypeStruct((2, CAP, HALF), BF16)] * OWNERS,
        scratch_shapes=[pltpu.VMEM((CHUNKS, CAP, 256), BF16)] * 2,
        compiler_params=pltpu.CompilerParams(vmem_limit_bytes=24 * MIB),
        cost_estimate=pl.CostEstimate(
            flops=2 * SLOTS * HALF * 128, bytes_accessed=6 * MIB, transcendentals=SLOTS * HEADS
        ),
        name="read_out",
    )(*queries, inner, column, entry)


def mix_kernel(route_ref, gates_ref, gain_ref, *refs):
    own_refs, other_refs, out_ref = refs[0:4], refs[4:8], refs[8]
    owner, core = lax.axis_index("memory"), lax.axis_index("dp")
    named, slot = membership(route_ref[...])
    picks, gates = [], []
    for shift in range(OWNERS):
        memory = (owner + shift) & (OWNERS - 1)
        picks.append(one_hot(named, slot, memory).astype(BF16)[:, :CAP])
        gates.append(pick_lane(gates_ref[...], memory))
    for place, reads in enumerate((own_refs, other_refs)):
        start = (core ^ place) * HALF
        mixture = jnp.zeros((ROWS, HALF), F32)
        for shift in range(OWNERS):
            mixture = mixture + gates[shift] * dot(picks[shift], reads[shift][core])
        for head in range(HEADS):
            columns = pl.ds(pl.multiple_of(start + head * HEAD_DIM, HEAD_DIM), HEAD_DIM)
            mix = mixture[:, head * HEAD_DIM : (head + 1) * HEAD_DIM]
            scale = lax.rsqrt(jnp.mean(mix * mix, axis=1, keepdims=True) + 1e-05)
            out_ref[:, columns] = (mix * scale * gain_ref[:, columns]).astype(BF16)


def mix_reads(route, gates, gain, own, other):
    return pl.pallas_call(
        mix_kernel,
        out_shape=jax.ShapeDtypeStruct((ROWS, 2 * HALF), BF16),
        compiler_params=pltpu.CompilerParams(vmem_limit_bytes=24 * MIB),
        cost_estimate=pl.CostEstimate(
            flops=2 * ROWS * 320 * 2 * HALF, bytes_accessed=4 * MIB, transcendentals=0
        ),
        name="mix_reads",
    )(route, gates, gain, *own, *other)


def hop(array, shift):
    return lax.ppermute(array, "memory", [(i, (i + shift) % OWNERS) for i in range(OWNERS)])


def swap(array):
    return lax.ppermute(array, "dp", [(0, 1), (1, 0)])


def shards(
    hidden,
    queries,
    route_ids,
    router_weight,
    key_weight,
    value_weight,
    decay_weight,
    decay_bias,
    norm_gain,
):
    rows, query_rows, route = hidden[0], queries[0], route_ids[0]
    weights = (key_weight[0], value_weight[0], decay_weight[0], decay_bias)

    packed = pack_rows(route, rows)
    arrived = {0: packed[0]}
    for shift in (1, 3, 2):
        arrived[shift] = hop(packed[shift], shift)
    other_route, other_query = swap(route), swap(query_rows)
    packed_query = pack_queries(route, other_route, query_rows, other_query, rows, router_weight)
    gates = packed_query[OWNERS]

    projected = []
    for group in GROUPS:
        parts = [swap(arrived[shift]) if partner else arrived[shift] for shift, partner in group]
        projected.append(project(parts, *weights))
    units, values, decays = zip(*projected)

    query_in = [packed_query[0]] + [hop(packed_query[shift], shift) for shift in (1, 2, 3)]
    message, column, row = block_state(units, values, decays)
    slices = lax.all_to_all(message, "context", 0, 0, tiled=True)
    entry = lax.all_to_all(prefix(slices), "context", 0, 0, tiled=True)
    inner = inner_reads(units, values, query_in, column, row)
    reads = read_out(query_in, inner, column, entry.reshape(HEADS, HEAD_DIM, HEAD_DIM))

    own = [reads[0]] + [hop(reads[shift], -shift) for shift in (1, 2, 3)]
    other = [swap(part) for part in own]
    return mix_reads(route, gates, norm_gain[None], own, other)[None]


def solution(mesh):
    in_specs = (
        P(("context", "dp"), "memory", None),
        P(("context", "dp"), "memory", None),
        P(("context", "dp"), "memory", None),
        P(),
        P("memory", None, "dp"),
        P("memory", None, "dp"),
        P("memory", None, "dp"),
        P("memory", "dp"),
        P(),
    )
    out_specs = P(("context", "dp"), "memory", None)
    return jax.shard_map(shards, mesh=mesh, in_specs=in_specs, out_specs=out_specs, check_vma=False)
```

```python
import functools

import jax
import jax.numpy as jnp
from jax import lax
from jax.experimental import pallas as pl
from jax.experimental.pallas import tpu as pltpu
from jax.sharding import PartitionSpec as P

D = 4096
HEAD_DIM = 128
CAP = 80
ROWS = 128
OWNERS = 4
CHUNKS = 8
SLOTS = CHUNKS * CAP
HALF = 1024
HEADS = HALF // HEAD_DIM
CONTEXTS = 16
LIVE = 128
PIECE = HALF // CONTEXTS
TAIL = 16
F32 = jnp.float32
BF16 = jnp.bfloat16
MIB = 1 << 20
VMEM = 60 * MIB


def iota(shape, axis):
    return lax.broadcasted_iota(jnp.int32, shape, axis)


def dot(a, b):
    return jnp.dot(a, b, preferred_element_type=F32)


def source(owner, shift):
    return (owner + OWNERS - shift) & (OWNERS - 1)


def position(shift, partner, owner, core):
    return (core ^ partner) * OWNERS + source(owner, shift)


def membership(route):
    lane = iota((ROWS, 128), 1)
    named = ((route[:, 0:1] == lane) | (route[:, 1:2] == lane)).astype(F32)
    before = (iota((ROWS, ROWS), 0) > iota((ROWS, ROWS), 1)).astype(F32).astype(BF16)
    return named, dot(before, named.astype(BF16))


def pick_lane(table, lane_at):
    return jnp.sum(jnp.where(iota(table.shape, 1) == lane_at, table, 0.0), axis=1, keepdims=True)


def one_hot(named, slot, memory):
    live = pick_lane(named, memory) > 0.0
    place = pick_lane(slot, memory)
    match = (iota((ROWS, 128), 1).astype(F32) == place) & live
    return match.astype(F32)


def pack_rows_kernel(route_ref, rows_ref, *out_refs):
    owner = lax.axis_index("memory")
    named, slot = membership(route_ref[...])
    picks = [
        one_hot(named, slot, (owner + shift) & (OWNERS - 1)).T.astype(BF16)[:CAP]
        for shift in range(OWNERS)
    ]
    pick = jnp.concatenate(picks, axis=0)
    width = 512
    for column in range(0, D, width):
        part = dot(pick, rows_ref[:, column : column + width]).astype(BF16)
        for shift in range(OWNERS):
            out_refs[shift][:, column : column + width] = part[shift * CAP : (shift + 1) * CAP]
    live = dot(pick, jnp.ones((ROWS, LIVE), BF16)).astype(BF16)
    for shift in range(OWNERS):
        out_refs[shift][:, D:] = live[shift * CAP : (shift + 1) * CAP]


def pack_rows(route, rows):
    return pl.pallas_call(
        pack_rows_kernel,
        out_shape=[jax.ShapeDtypeStruct((CAP, D + LIVE), BF16)] * OWNERS,
        compiler_params=pltpu.CompilerParams(vmem_limit_bytes=VMEM),
        cost_estimate=pl.CostEstimate(
            flops=2 * 320 * 128 * D, bytes_accessed=4 * MIB, transcendentals=0
        ),
        name="pack_rows",
    )(route, rows)


def pack_queries_kernel(
    route_ref, other_route_ref, query_ref, other_query_ref, rows_ref, router_ref, *out_refs
):
    owner, core = lax.axis_index("memory"), lax.axis_index("dp")
    gates_ref = out_refs[OWNERS]
    mine = pl.multiple_of(core * HALF, HALF)
    for place, (routes, queries) in enumerate(
        ((route_ref, query_ref), (other_route_ref, other_query_ref))
    ):
        named, slot = membership(routes[...])
        picks = [
            one_hot(named, slot, (owner + shift) & (OWNERS - 1)).T.astype(BF16)[:CAP]
            for shift in range(OWNERS)
        ]
        pick = jnp.concatenate(picks, axis=0)
        part = dot(pick, queries[:, pl.ds(mine, HALF)]).astype(BF16)
        for shift in range(OWNERS):
            out_refs[shift][core ^ place] = part[shift * CAP : (shift + 1) * CAP]
        if place == 0:
            score = dot(rows_ref[...], router_ref[...])
            chosen = jax.nn.sigmoid(score) * named[:, :OWNERS]
            gates_ref[...] = jnp.zeros((ROWS, 128), F32)
            gates_ref[:, :OWNERS] = chosen / jnp.sum(chosen, axis=1, keepdims=True)


def pack_queries(route, other_route, queries, other_queries, rows, router_weight):
    return pl.pallas_call(
        pack_queries_kernel,
        out_shape=[jax.ShapeDtypeStruct((2, CAP, HALF), BF16)] * OWNERS
        + [jax.ShapeDtypeStruct((ROWS, 128), F32)],
        compiler_params=pltpu.CompilerParams(vmem_limit_bytes=VMEM),
        cost_estimate=pl.CostEstimate(
            flops=2 * 640 * 128 * HALF, bytes_accessed=4 * MIB, transcendentals=0
        ),
        name="pack_queries",
    )(route, other_route, queries, other_queries, rows, router_weight)


def log_sigmoid(x):
    small = jnp.exp(-jnp.abs(x))
    near = 1.0 + small
    log1p = jnp.where(near == 1.0, small, jnp.log(near) * (small / jnp.where(near == 1.0, 1.0, near - 1.0)))
    return jnp.minimum(x, 0.0) - log1p


def project_kernel(count, *refs):
    row_refs = refs[:count]
    key_ref, value_ref, decay_ref, bias_ref, unit_out, value_out, decay_out, held = refs[count:]

    @pl.when(pl.program_id(0) == 0)
    def _():
        for at in range(count):
            held[at * CAP : (at + 1) * CAP] = row_refs[at][:, :D]
        gate = dot(held[...], decay_ref[...]) + bias_ref[...]
        decay = log_sigmoid(gate)
        decay_out[...] = jnp.zeros_like(decay_out)
        for at in range(count):
            live = row_refs[at][:, D : D + HEADS].astype(F32)
            decay_out[at, :, :HEADS] = decay[at * CAP : (at + 1) * CAP] * live

    keys = dot(held[...], key_ref[...]).astype(BF16).astype(F32)
    width = keys.shape[1]
    for head in range(width // HEAD_DIM):
        columns = slice(head * HEAD_DIM, (head + 1) * HEAD_DIM)
        key = keys[:, columns]
        unit = key * lax.rsqrt(jnp.sum(key * key, axis=1, keepdims=True) + 1e-06)
        unit_out[:, :, columns] = unit.astype(BF16).reshape(count, CAP, HEAD_DIM)
    values = dot(held[...], value_ref[...]).astype(BF16)
    value_out[...] = values.reshape(count, CAP, width)


def project(row_parts, key_weight, value_weight, decay_weight, decay_bias):
    count = len(row_parts)
    width = 256
    whole = lambda shape: pl.BlockSpec(shape, lambda n: (0,) * len(shape))
    return pl.pallas_call(
        functools.partial(project_kernel, count),
        grid=(HALF // width,),
        in_specs=[whole((CAP, D + LIVE))] * count
        + [
            pl.BlockSpec((D, width), lambda n: (0, n)),
            pl.BlockSpec((D, width), lambda n: (0, n)),
            whole((D, HEADS)),
            whole((1, HEADS)),
        ],
        out_specs=[
            pl.BlockSpec((count, CAP, width), lambda n: (0, 0, n)),
            pl.BlockSpec((count, CAP, width), lambda n: (0, 0, n)),
            whole((count, CAP, 128)),
        ],
        out_shape=[
            jax.ShapeDtypeStruct((count, CAP, HALF), BF16),
            jax.ShapeDtypeStruct((count, CAP, HALF), BF16),
            jax.ShapeDtypeStruct((count, CAP, 128), F32),
        ],
        scratch_shapes=[pltpu.VMEM((count * CAP, D), BF16)],
        compiler_params=pltpu.CompilerParams(vmem_limit_bytes=VMEM),
        cost_estimate=pl.CostEstimate(
            flops=2 * count * CAP * D * 2 * HALF, bytes_accessed=18 * MIB, transcendentals=0
        ),
        name=f"project_{count}",
    )(*row_parts, key_weight, value_weight, decay_weight, decay_bias)


GROUPS = (((0, 0), (0, 1)), ((1, 0), (1, 1), (3, 0), (3, 1)), ((2, 0), (2, 1)))


def gather_order(refs, held, columns=slice(None)):
    owner, core = lax.axis_index("memory"), lax.axis_index("dp")
    for group, ref in zip(GROUPS, refs):
        for at, (shift, partner) in enumerate(group):
            held[position(shift, partner, owner, core)] = ref[at, :, columns]


def state_kernel(*refs):
    unit_refs, value_refs, decay_refs = refs[0:3], refs[3:6], refs[6:9]
    message, column_out, row_out, units, values, decays = refs[9:]
    step = pl.program_id(0)

    @pl.when(step == 0)
    def _():
        gather_order(decay_refs, decays)
        total = decays[...].reshape(SLOTS, 128).T[:HEADS]
        lane = iota((HEADS, SLOTS), 1)
        reach = 1
        while reach < SLOTS:
            total = total + jnp.where(lane >= reach, pltpu.roll(total, reach, 1), 0.0)
            reach *= 2
        row_out[...] = total
        column_out[...] = jnp.concatenate(
            [total, jnp.zeros((128 - HEADS, SLOTS), F32)], axis=0
        ).T

    gather_order(unit_refs, units)
    gather_order(value_refs, values)
    for at in range(2):
        head = step * 2 + at
        columns = slice(at * HEAD_DIM, (at + 1) * HEAD_DIM)
        running = pick_lane(column_out[...], head)
        last = running[SLOTS - 1 : SLOTS]
        unit = units[:, :, columns].reshape(SLOTS, HEAD_DIM).astype(F32)
        faded = (unit * jnp.exp(last - running)).astype(BF16)
        value = values[:, :, columns].reshape(SLOTS, HEAD_DIM)
        state = lax.dot_general(
            faded, value, (((0,), (0,)), ((), ())), preferred_element_type=F32
        ).astype(BF16)
        high = jnp.broadcast_to(last, (TAIL, 128)).astype(BF16).astype(F32)
        low = jnp.broadcast_to(last, (TAIL, 128)) - high
        tail = jnp.where(iota((TAIL, 128), 0) < TAIL // 2, high, low).astype(BF16)
        for part in range(2):
            message[at * 2 + part, :PIECE] = state[part * PIECE : (part + 1) * PIECE]
            message[at * 2 + part, PIECE:] = tail


def block_state(units, values, decays):
    whole = lambda shape: pl.BlockSpec(shape, lambda n: (0,) * len(shape))
    chunked = [pl.BlockSpec((len(group), CAP, 256), lambda n: (0, 0, n)) for group in GROUPS]
    return pl.pallas_call(
        state_kernel,
        grid=(HEADS // 2,),
        in_specs=chunked * 2 + [whole((len(group), CAP, 128)) for group in GROUPS],
        out_specs=[
            pl.BlockSpec((4, PIECE + TAIL, 128), lambda n: (n, 0, 0)),
            whole((SLOTS, 128)),
            whole((HEADS, SLOTS)),
        ],
        out_shape=[
            jax.ShapeDtypeStruct((CONTEXTS, PIECE + TAIL, 128), BF16),
            jax.ShapeDtypeStruct((SLOTS, 128), F32),
            jax.ShapeDtypeStruct((HEADS, SLOTS), F32),
        ],
        scratch_shapes=[
            pltpu.VMEM((CHUNKS, CAP, 256), BF16),
            pltpu.VMEM((CHUNKS, CAP, 256), BF16),
            pltpu.VMEM((CHUNKS, CAP, 128), F32),
        ],
        compiler_params=pltpu.CompilerParams(vmem_limit_bytes=VMEM),
        cost_estimate=pl.CostEstimate(
            flops=2 * SLOTS * HALF * 128, bytes_accessed=4 * MIB, transcendentals=SLOTS * HEADS
        ),
        name="block_state",
    )(*units, *values, *decays)


def prefix_kernel(message, entry):
    before = jnp.zeros((PIECE, 128), F32)
    for context in range(CONTEXTS):
        entry[context] = before.astype(BF16)
        high = message[context, PIECE : PIECE + 1].astype(F32)
        low = message[context, PIECE + TAIL // 2 : PIECE + TAIL // 2 + 1].astype(F32)
        before = jnp.exp(high + low) * before + message[context, :PIECE].astype(F32)


def prefix(message):
    return pl.pallas_call(
        prefix_kernel,
        out_shape=jax.ShapeDtypeStruct((CONTEXTS, PIECE, 128), BF16),
        compiler_params=pltpu.CompilerParams(vmem_limit_bytes=VMEM),
        cost_estimate=pl.CostEstimate(flops=1 << 20, bytes_accessed=1 << 20, transcendentals=0),
        name="prefix",
    )(message)


def inner_kernel(*refs):
    unit_refs, value_refs, query_refs = refs[0:3], refs[3:6], refs[6:10]
    column_ref, row_ref, inner, units, values, queries = refs[10:]
    step = pl.program_id(0)
    owner = lax.axis_index("memory")
    gather_order(unit_refs, units)
    gather_order(value_refs, values)
    for shift in range(OWNERS):
        for core in range(2):
            queries[core * OWNERS + source(owner, shift)] = query_refs[shift][core]
    tile = 2 * CAP
    for at in range(2):
        head = step * 2 + at
        columns = slice(at * HEAD_DIM, (at + 1) * HEAD_DIM)
        running = pick_lane(column_ref[...], head)
        running_row = row_ref[pl.ds(head, 1), :]
        unit = units[:, :, columns].reshape(SLOTS, HEAD_DIM)
        value = values[:, :, columns].reshape(SLOTS, HEAD_DIM)
        for block in range(SLOTS // tile):
            reach = -(-((block + 1) * tile) // 128) * 128
            query = queries[2 * block : 2 * block + 2, :, columns].reshape(tile, HEAD_DIM)
            score = lax.dot_general(
                query, unit[:reach], (((1,), (1,)), ((), ())), preferred_element_type=F32
            )
            spread = running[block * tile : (block + 1) * tile] - running_row[:, :reach]
            causal = iota((tile, reach), 0) + block * tile >= iota((tile, reach), 1)
            score = (score * jnp.exp(jnp.where(causal, spread, -1e30))).astype(BF16)
            result = dot(score, value[:reach])
            inner[2 * block : 2 * block + 2, :, columns] = result.reshape(2, CAP, HEAD_DIM)


def inner_reads(units, values, queries, column, row):
    whole = lambda shape: pl.BlockSpec(shape, lambda n: (0,) * len(shape))
    chunked = [pl.BlockSpec((len(group), CAP, 256), lambda n: (0, 0, n)) for group in GROUPS]
    return pl.pallas_call(
        inner_kernel,
        grid=(HEADS // 2,),
        in_specs=chunked * 2
        + [pl.BlockSpec((2, CAP, 256), lambda n: (0, 0, n))] * OWNERS
        + [whole((SLOTS, 128)), whole((HEADS, SLOTS))],
        out_specs=pl.BlockSpec((CHUNKS, CAP, 256), lambda n: (0, 0, n)),
        out_shape=jax.ShapeDtypeStruct((CHUNKS, CAP, HALF), F32),
        scratch_shapes=[pltpu.VMEM((CHUNKS, CAP, 256), BF16)] * 3,
        compiler_params=pltpu.CompilerParams(vmem_limit_bytes=VMEM),
        cost_estimate=pl.CostEstimate(
            flops=4 * SLOTS * SLOTS * HALF, bytes_accessed=8 * MIB, transcendentals=SLOTS * SLOTS * 4
        ),
        name="inner_reads",
    )(*units, *values, *queries, column, row)


def read_kernel(*refs):
    query_refs = refs[0:4]
    inner, column_ref, entry = refs[4:7]
    out_refs = refs[7:11]
    queries, reads = refs[11:]
    step = pl.program_id(0)
    owner = lax.axis_index("memory")
    for shift in range(OWNERS):
        for core in range(2):
            queries[core * OWNERS + source(owner, shift)] = query_refs[shift][core]
    for at in range(2):
        head = step * 2 + at
        columns = slice(at * HEAD_DIM, (at + 1) * HEAD_DIM)
        fade = jnp.exp(pick_lane(column_ref[...], head))
        carried = dot(queries[:, :, columns].reshape(SLOTS, HEAD_DIM), entry[at])
        result = inner[:, :, columns].reshape(SLOTS, HEAD_DIM) + fade * carried
        reads[:, :, columns] = result.astype(BF16).reshape(CHUNKS, CAP, HEAD_DIM)
    for shift in range(OWNERS):
        for core in range(2):
            out_refs[shift][core] = reads[core * OWNERS + source(owner, shift)]


def read_out(queries, inner, column, entry):
    whole = lambda shape: pl.BlockSpec(shape, lambda n: (0,) * len(shape))
    return pl.pallas_call(
        read_kernel,
        grid=(HEADS // 2,),
        in_specs=[pl.BlockSpec((2, CAP, 256), lambda n: (0, 0, n))] * OWNERS
        + [
            pl.BlockSpec((CHUNKS, CAP, 256), lambda n: (0, 0, n)),
            whole((SLOTS, 128)),
            pl.BlockSpec((2, 128, 128), lambda n: (n, 0, 0)),
        ],
        out_specs=[pl.BlockSpec((2, CAP, 256), lambda n: (0, 0, n))] * OWNERS,
        out_shape=[jax.ShapeDtypeStruct((2, CAP, HALF), BF16)] * OWNERS,
        scratch_shapes=[pltpu.VMEM((CHUNKS, CAP, 256), BF16)] * 2,
        compiler_params=pltpu.CompilerParams(vmem_limit_bytes=VMEM),
        cost_estimate=pl.CostEstimate(
            flops=2 * SLOTS * HALF * 128, bytes_accessed=6 * MIB, transcendentals=SLOTS * HEADS
        ),
        name="read_out",
    )(*queries, inner, column, entry)


def mix_kernel(route_ref, gates_ref, gain_ref, *refs):
    own_refs, other_refs, out_ref = refs[0:4], refs[4:8], refs[8]
    owner, core = lax.axis_index("memory"), lax.axis_index("dp")
    named, slot = membership(route_ref[...])
    picks, gates = [], []
    for shift in range(OWNERS):
        memory = (owner + shift) & (OWNERS - 1)
        picks.append(one_hot(named, slot, memory).astype(BF16)[:, :CAP])
        gates.append(pick_lane(gates_ref[...], memory))
    for place, reads in enumerate((own_refs, other_refs)):
        start = (core ^ place) * HALF
        mixture = jnp.zeros((ROWS, HALF), F32)
        for shift in range(OWNERS):
            mixture = mixture + gates[shift] * dot(picks[shift], reads[shift][core])
        for head in range(HEADS):
            columns = pl.ds(pl.multiple_of(start + head * HEAD_DIM, HEAD_DIM), HEAD_DIM)
            mix = mixture[:, head * HEAD_DIM : (head + 1) * HEAD_DIM]
            scale = lax.rsqrt(jnp.mean(mix * mix, axis=1, keepdims=True) + 1e-05)
            out_ref[:, columns] = (mix * scale * gain_ref[:, columns]).astype(BF16)


def mix_reads(route, gates, gain, own, other):
    return pl.pallas_call(
        mix_kernel,
        out_shape=jax.ShapeDtypeStruct((ROWS, 2 * HALF), BF16),
        compiler_params=pltpu.CompilerParams(vmem_limit_bytes=VMEM),
        cost_estimate=pl.CostEstimate(
            flops=2 * ROWS * 320 * 2 * HALF, bytes_accessed=4 * MIB, transcendentals=0
        ),
        name="mix_reads",
    )(route, gates, gain, *own, *other)


def after(array, *first):
    return lax.optimization_barrier((array, *first))[0]


def hop(array, shift):
    return lax.ppermute(array, "memory", [(i, (i + shift) % OWNERS) for i in range(OWNERS)])


def swap(array):
    return lax.ppermute(array, "dp", [(0, 1), (1, 0)])


def shards(
    hidden,
    queries,
    route_ids,
    router_weight,
    key_weight,
    value_weight,
    decay_weight,
    decay_bias,
    norm_gain,
):
    rows, query_rows, route = hidden[0], queries[0], route_ids[0]
    weights = (key_weight[0], value_weight[0], decay_weight[0], decay_bias)

    packed = pack_rows(route, rows)
    arrived = {0: packed[0]}
    for shift in (1, 3, 2):
        arrived[shift] = hop(packed[shift], shift)
    other = {0: swap(packed[0])}
    other_route, other_query = swap(route), swap(query_rows)
    first = project([arrived[0], other[0]], *weights)
    packed_query = pack_queries(
        after(route, first[2]), other_route, query_rows, other_query, rows, router_weight
    )
    gates = packed_query[OWNERS]
    for shift in (1, 3):
        arrived[shift] = after(arrived[shift], gates)
        other[shift] = swap(arrived[shift])
    second = project([arrived[1], other[1], arrived[3], other[3]], *weights)
    arrived[2] = after(arrived[2], second[2])
    other[2] = swap(arrived[2])
    query_in = [packed_query[0]]
    query_in += [hop(after(packed_query[shift], arrived[2]), shift) for shift in (1, 2, 3)]
    third = project([arrived[2], other[2]], *weights)
    units, values, decays = zip(first, second, third)

    message, column, row = block_state(units, values, decays)
    slices = lax.all_to_all(message, "context", 0, 0, tiled=True)
    entry = lax.all_to_all(prefix(slices), "context", 0, 0, tiled=True)
    inner = inner_reads(units, values, query_in, column, row)
    reads = read_out(query_in, inner, column, entry.reshape(HEADS, HEAD_DIM, HEAD_DIM))

    own = [reads[0]] + [hop(reads[shift], -shift) for shift in (1, 2, 3)]
    paired = [swap(part) for part in own]
    return mix_reads(route, gates, norm_gain[None], own, paired)[None]


def solution(mesh):
    in_specs = (
        P(("context", "dp"), "memory", None),
        P(("context", "dp"), "memory", None),
        P(("context", "dp"), "memory", None),
        P(),
        P("memory", None, "dp"),
        P("memory", None, "dp"),
        P("memory", None, "dp"),
        P("memory", "dp"),
        P(),
    )
    out_specs = P(("context", "dp"), "memory", None)
    return jax.shard_map(shards, mesh=mesh, in_specs=in_specs, out_specs=out_specs, check_vma=False)
```

```python
import functools

import jax
import jax.numpy as jnp
from jax import lax
from jax.experimental import pallas as pl
from jax.experimental.pallas import tpu as pltpu
from jax.sharding import PartitionSpec as P

D = 4096
HEAD_DIM = 128
CAP = 80
ROWS = 128
OWNERS = 4
CHUNKS = 8
SLOTS = CHUNKS * CAP
HALF = 1024
HEADS = HALF // HEAD_DIM
CONTEXTS = 16
LIVE = 128
PIECE = HALF // CONTEXTS
TAIL = 16
F32 = jnp.float32
BF16 = jnp.bfloat16
MIB = 1 << 20


def iota(shape, axis):
    return lax.broadcasted_iota(jnp.int32, shape, axis)


def dot(a, b):
    return jnp.dot(a, b, preferred_element_type=F32)


def dot_rows(a, b):
    return lax.dot_general(a, b, (((1,), (1,)), ((), ())), preferred_element_type=F32)


def dot_columns(a, b):
    return lax.dot_general(a, b, (((0,), (0,)), ((), ())), preferred_element_type=F32)


def source(owner, shift):
    return (owner + OWNERS - shift) & (OWNERS - 1)


def position(shift, partner, owner, core):
    return (core ^ partner) * OWNERS + source(owner, shift)


def membership(route):
    memory = iota((8, ROWS), 0)
    named = ((route[0:1] == memory) | (route[1:2] == memory)).astype(F32)
    before = (iota((ROWS, ROWS), 0) < iota((ROWS, ROWS), 1)).astype(F32).astype(BF16)
    slot = dot(named.astype(BF16), before)
    return named, jnp.where(named > 0.0, slot, -1.0)


def one_hot(place, memory, slots=CAP):
    mine = jnp.sum(jnp.where(iota(place.shape, 0) == memory, place, 0.0), axis=0, keepdims=True)
    return (iota((slots, ROWS), 0).astype(F32) == mine).astype(F32)


def kernel_call(kernel, name, out_shape, scratch, limit, cost, *operands, hbm=()):
    spaces = [pltpu.HBM if at in hbm else pltpu.VMEM for at in range(len(operands))]
    return pl.pallas_call(
        kernel,
        out_shape=out_shape,
        in_specs=[pl.BlockSpec(memory_space=space) for space in spaces],
        out_specs=jax.tree.map(lambda _: pl.BlockSpec(memory_space=pltpu.VMEM), out_shape),
        scratch_shapes=scratch,
        compiler_params=pltpu.CompilerParams(vmem_limit_bytes=limit * MIB),
        cost_estimate=pl.CostEstimate(
            flops=cost[0], bytes_accessed=cost[1], transcendentals=0
        ),
        name=name,
    )(*operands)


def pack_rows_kernel(route_ref, rows_ref, *out_refs):
    owner = lax.axis_index("memory")
    place = membership(route_ref[...])[1]
    pick = jnp.concatenate(
        [one_hot(place, (owner + shift) & (OWNERS - 1)) for shift in range(OWNERS)], axis=0
    ).astype(BF16)
    width = 512
    for column in range(0, D, width):
        part = dot(pick, rows_ref[:, column : column + width]).astype(BF16)
        for shift in range(OWNERS):
            out_refs[shift][:, column : column + width] = part[shift * CAP : (shift + 1) * CAP]
    live = dot(pick, jnp.ones((ROWS, LIVE), BF16)).astype(BF16)
    for shift in range(OWNERS):
        out_refs[shift][:, D:] = live[shift * CAP : (shift + 1) * CAP]


def pack_rows(route, rows):
    out = [jax.ShapeDtypeStruct((CAP, D + LIVE), BF16)] * OWNERS
    cost = (2 * 320 * 128 * D, 4 * MIB)
    return kernel_call(pack_rows_kernel, "pack_rows", out, (), 12, cost, route, rows)


def pack_queries_kernel(
    route_ref, other_route_ref, query_ref, other_query_ref, rows_ref, router_ref, *out_refs
):
    owner, core = lax.axis_index("memory"), lax.axis_index("dp")
    gates_ref = out_refs[OWNERS]
    mine = pl.multiple_of(core * HALF, HALF)
    for side, (routes, queries) in enumerate(
        ((route_ref, query_ref), (other_route_ref, other_query_ref))
    ):
        named, place = membership(routes[...])
        pick = jnp.concatenate(
            [one_hot(place, (owner + shift) & (OWNERS - 1)) for shift in range(OWNERS)], axis=0
        ).astype(BF16)
        part = dot(pick, queries[:, pl.ds(mine, HALF)]).astype(BF16)
        for shift in range(OWNERS):
            out_refs[shift][core ^ side] = part[shift * CAP : (shift + 1) * CAP]
        if side == 0:
            score = dot_rows(router_ref[...], rows_ref[...])
            chosen = jax.nn.sigmoid(score) * named[:OWNERS]
            gates = chosen / jnp.sum(chosen, axis=0, keepdims=True)
            gates_ref[...] = jnp.concatenate(
                [gates, jnp.zeros((128 - OWNERS, ROWS), F32)], axis=0
            ).T


def pack_queries(route, other_route, queries, other_queries, rows, router_weight):
    out = [jax.ShapeDtypeStruct((2, CAP, HALF), BF16)] * OWNERS
    out = out + [jax.ShapeDtypeStruct((ROWS, 128), F32)]
    cost = (2 * 640 * 128 * HALF, 4 * MIB)
    operands = (route, other_route, queries, other_queries, rows, router_weight)
    return kernel_call(pack_queries_kernel, "pack_queries", out, (), 12, cost, *operands)


def log_sigmoid(x):
    small = jnp.exp(-jnp.abs(x))
    near = 1.0 + small
    tiny = near == 1.0
    log1p = jnp.where(tiny, small, jnp.log(near) * (small / jnp.where(tiny, 1.0, near - 1.0)))
    return jnp.minimum(x, 0.0) - log1p


WIDTH = 512


def project_parts(row_refs, decay_ref, bias_ref, outs, key_ref, value_ref, held, ready):
    count = len(row_refs)
    unit_out, value_out, decay_out = outs
    for at in range(count):
        held[at * CAP : (at + 1) * CAP] = row_refs[at][:, :D]
    decay = log_sigmoid(dot_rows(held[...], decay_ref[...]) + bias_ref[...])
    decay_out[...] = jnp.zeros_like(decay_out)
    for at in range(count):
        live = row_refs[at][:, D : D + HEADS].astype(F32)
        decay_out[at, :, :HEADS] = decay[at * CAP : (at + 1) * CAP] * live
    for start in range(0, HALF, WIDTH):
        ready(start // WIDTH)
        columns = slice(start, start + WIDTH)
        keys = dot(held[...], key_ref[:, columns]).astype(BF16).astype(F32)
        for head in range(0, WIDTH, HEAD_DIM):
            key = keys[:, head : head + HEAD_DIM]
            unit = key * lax.rsqrt(jnp.sum(key * key, axis=1, keepdims=True) + 1e-06)
            unit_out[:, :, start + head : start + head + HEAD_DIM] = unit.astype(BF16).reshape(
                count, CAP, HEAD_DIM
            )
        values = dot(held[...], value_ref[:, columns]).astype(BF16)
        value_out[:, :, columns] = values.reshape(count, CAP, WIDTH)


def project_first_kernel(count, *refs):
    key_hbm, value_hbm, decay_ref, bias_ref = refs[count : count + 4]
    outs, (key_ref, value_ref, held, sems) = refs[count + 4 : count + 7], refs[count + 7 :]
    copies = []
    for at, start in enumerate(range(0, HALF, WIDTH)):
        columns = slice(start, start + WIDTH)
        for side, (far, near) in enumerate(((key_hbm, key_ref), (value_hbm, value_ref))):
            copies.append(
                pltpu.make_async_copy(far.at[:, columns], near.at[:, columns], sems.at[side, at])
            )
    for copy in copies:
        copy.start()

    def ready(at):
        copies[2 * at].wait()
        copies[2 * at + 1].wait()

    project_parts(refs[:count], decay_ref, bias_ref, outs, key_ref, value_ref, held, ready)


def project_next_kernel(count, *refs):
    key_ref, value_ref, decay_ref, bias_ref = refs[count : count + 4]
    outs, held = refs[count + 4 : count + 7], refs[count + 7]
    project_parts(
        refs[:count], decay_ref, bias_ref, outs, key_ref, value_ref, held, lambda at: None
    )


def project(row_parts, key_weight, value_weight, decay_weight, decay_bias, first=False):
    count = len(row_parts)
    out = [jax.ShapeDtypeStruct((count, CAP, HALF), BF16)] * 2
    out = out + [jax.ShapeDtypeStruct((count, CAP, 128), F32)]
    scratch = [pltpu.VMEM((count * CAP, D), BF16)]
    cost = (2 * count * CAP * D * 2 * HALF, 18 * MIB)
    kernel = project_first_kernel if first else project_next_kernel
    if first:
        out = out + [pltpu.VMEM((D, HALF), BF16)] * 2
        scratch = scratch + [pltpu.SemaphoreType.DMA((2, HALF // WIDTH))]
    return kernel_call(
        functools.partial(kernel, count),
        f"project_{count}",
        out,
        scratch,
        40 if first else 12,
        cost,
        *row_parts,
        key_weight,
        value_weight,
        decay_weight,
        decay_bias,
        hbm=(count, count + 1) if first else (),
    )


GROUPS = (((0, 0), (0, 1)), ((1, 0), (1, 1), (3, 0), (3, 1)), ((2, 0), (2, 1)))


def token_order(refs, held):
    owner, core = lax.axis_index("memory"), lax.axis_index("dp")
    for group, ref in zip(GROUPS, refs):
        for at, (shift, partner) in enumerate(group):
            held[position(shift, partner, owner, core)] = ref[at]


def head_columns(head):
    return slice(head * HEAD_DIM, (head + 1) * HEAD_DIM)


def state_kernel(*refs):
    unit_refs, value_refs, decay_refs = refs[0:3], refs[3:6], refs[6:9]
    message, column_out, row_out, units, values, decays = refs[9:]
    token_order(decay_refs, decays)
    total = decays[...].reshape(SLOTS, 128).T[:HEADS]
    lane = iota((HEADS, SLOTS), 1)
    reach = 1
    while reach < SLOTS:
        total = total + jnp.where(lane >= reach, pltpu.roll(total, reach, 1), 0.0)
        reach *= 2
    row_out[...] = total
    running = jnp.concatenate([total, jnp.zeros((128 - HEADS, SLOTS), F32)], axis=0).T
    column_out[...] = running
    token_order(unit_refs, units)
    token_order(value_refs, values)
    last = running[SLOTS - 1 : SLOTS]
    fade = jnp.exp(last - running)
    for head in range(HEADS):
        unit = units[:, :, head_columns(head)].reshape(SLOTS, HEAD_DIM).astype(F32)
        faded = (unit * fade[:, head : head + 1]).astype(BF16)
        value = values[:, :, head_columns(head)].reshape(SLOTS, HEAD_DIM)
        state = dot_columns(faded, value).astype(BF16)
        ended = jnp.broadcast_to(last[:, head : head + 1], (TAIL, 128))
        high = ended.astype(BF16).astype(F32)
        tail = jnp.where(iota((TAIL, 128), 0) < TAIL // 2, high, ended - high).astype(BF16)
        for part in range(2):
            message[head * 2 + part, :PIECE] = state[part * PIECE : (part + 1) * PIECE]
            message[head * 2 + part, PIECE:] = tail


def block_state(units, values, decays):
    out = [
        jax.ShapeDtypeStruct((CONTEXTS, PIECE + TAIL, 128), BF16),
        jax.ShapeDtypeStruct((SLOTS, 128), F32),
        jax.ShapeDtypeStruct((HEADS, SLOTS), F32),
    ]
    scratch = [
        pltpu.VMEM((CHUNKS, CAP, HALF), BF16),
        pltpu.VMEM((CHUNKS, CAP, HALF), BF16),
        pltpu.VMEM((CHUNKS, CAP, 128), F32),
    ]
    cost = (2 * SLOTS * HALF * 128, 4 * MIB)
    return kernel_call(
        state_kernel, "block_state", out, scratch, 12, cost, *units, *values, *decays
    )


def prefix_kernel(message, entry):
    before = jnp.zeros((PIECE, 128), F32)
    for context in range(CONTEXTS):
        entry[context] = before.astype(BF16)
        high = message[context, PIECE : PIECE + 1].astype(F32)
        low = message[context, PIECE + TAIL // 2 : PIECE + TAIL // 2 + 1].astype(F32)
        before = jnp.exp(high + low) * before + message[context, :PIECE].astype(F32)


def prefix(message):
    out = jax.ShapeDtypeStruct((CONTEXTS, PIECE, 128), BF16)
    return kernel_call(prefix_kernel, "prefix", out, (), 4, (MIB, MIB), message)


def order_queries(query_refs, held):
    owner = lax.axis_index("memory")
    for shift in range(OWNERS):
        for core in range(2):
            held[core * OWNERS + source(owner, shift)] = query_refs[shift][core]


def inner_kernel(*refs):
    unit_refs, value_refs, query_refs = refs[0:3], refs[3:6], refs[6:10]
    column_ref, row_ref, inner, units, values, queries = refs[10:]
    token_order(unit_refs, units)
    token_order(value_refs, values)
    order_queries(query_refs, queries)
    tile = 2 * CAP
    for head in range(HEADS):
        columns = head_columns(head)
        running = column_ref[:, head : head + 1]
        running_row = row_ref[head : head + 1]
        unit = units[:, :, columns].reshape(SLOTS, HEAD_DIM)
        value = values[:, :, columns].reshape(SLOTS, HEAD_DIM)
        for block in range(SLOTS // tile):
            reach = -(-((block + 1) * tile) // 128) * 128
            query = queries[2 * block : 2 * block + 2, :, columns].reshape(tile, HEAD_DIM)
            score = dot_rows(query, unit[:reach])
            spread = running[block * tile : (block + 1) * tile] - running_row[:, :reach]
            causal = iota((tile, reach), 0) + block * tile >= iota((tile, reach), 1)
            score = (score * jnp.exp(jnp.where(causal, spread, -1e30))).astype(BF16)
            result = dot(score, value[:reach])
            inner[2 * block : 2 * block + 2, :, columns] = result.reshape(2, CAP, HEAD_DIM)


def inner_reads(units, values, queries, column, row):
    out = jax.ShapeDtypeStruct((CHUNKS, CAP, HALF), F32)
    scratch = [pltpu.VMEM((CHUNKS, CAP, HALF), BF16)] * 3
    cost = (4 * SLOTS * SLOTS * HALF, 8 * MIB)
    operands = (*units, *values, *queries, column, row)
    return kernel_call(inner_kernel, "inner_reads", out, scratch, 16, cost, *operands)


def read_kernel(*refs):
    query_refs = refs[0:4]
    inner, column_ref, entry = refs[4:7]
    out_refs = refs[7:11]
    queries, reads = refs[11:]
    owner = lax.axis_index("memory")
    order_queries(query_refs, queries)
    fade = jnp.exp(column_ref[...])
    for head in range(HEADS):
        columns = head_columns(head)
        carried = dot(queries[:, :, columns].reshape(SLOTS, HEAD_DIM), entry[head])
        result = inner[:, :, columns].reshape(SLOTS, HEAD_DIM) + fade[:, head : head + 1] * carried
        reads[:, :, columns] = result.astype(BF16).reshape(CHUNKS, CAP, HEAD_DIM)
    for shift in range(OWNERS):
        for core in range(2):
            out_refs[shift][core] = reads[core * OWNERS + source(owner, shift)]


def read_out(queries, inner, column, entry):
    out = [jax.ShapeDtypeStruct((2, CAP, HALF), BF16)] * OWNERS
    scratch = [pltpu.VMEM((CHUNKS, CAP, HALF), BF16)] * 2
    cost = (2 * SLOTS * HALF * 128, 6 * MIB)
    return kernel_call(
        read_kernel, "read_out", out, scratch, 12, cost, *queries, inner, column, entry
    )


def mix_kernel(route_ref, gates_ref, gain_ref, *refs):
    own_refs, other_refs, out_ref = refs[0:4], refs[4:8], refs[8]
    owner, core = lax.axis_index("memory"), lax.axis_index("dp")
    place = membership(route_ref[...])[1]
    picks, gates = [], []
    lane = iota((ROWS, 128), 1)
    for shift in range(OWNERS):
        memory = (owner + shift) & (OWNERS - 1)
        picks.append(one_hot(place, memory, 128).T.astype(BF16)[:, :CAP])
        gate = jnp.where(lane == memory, gates_ref[...], 0.0)
        gates.append(jnp.sum(gate, axis=1, keepdims=True))
    for side, reads in enumerate((own_refs, other_refs)):
        start = (core ^ side) * HALF
        mixture = jnp.zeros((ROWS, HALF), F32)
        for shift in range(OWNERS):
            mixture = mixture + gates[shift] * dot(picks[shift], reads[shift][core])
        for head in range(HEADS):
            columns = pl.ds(pl.multiple_of(start + head * HEAD_DIM, HEAD_DIM), HEAD_DIM)
            mix = mixture[:, head_columns(head)]
            scale = lax.rsqrt(jnp.mean(mix * mix, axis=1, keepdims=True) + 1e-05)
            out_ref[:, columns] = (mix * scale * gain_ref[:, columns]).astype(BF16)


def mix_reads(route, gates, gain, own, other):
    out = jax.ShapeDtypeStruct((ROWS, 2 * HALF), BF16)
    cost = (2 * ROWS * 320 * 2 * HALF, 4 * MIB)
    return kernel_call(
        mix_kernel, "mix_reads", out, (), 12, cost, route, gates, gain, *own, *other
    )


def after(array, *first):
    return lax.optimization_barrier((array, *first))[0]


def hop(array, shift):
    return lax.ppermute(array, "memory", [(i, (i + shift) % OWNERS) for i in range(OWNERS)])


def swap(array):
    return lax.ppermute(array, "dp", [(0, 1), (1, 0)])


def shards(
    hidden,
    queries,
    route_ids,
    router_weight,
    key_weight,
    value_weight,
    decay_weight,
    decay_bias,
    norm_gain,
):
    rows, query_rows, route = hidden[0], queries[0], route_ids[0].T
    weights = (key_weight[0], value_weight[0], decay_weight[0].T, decay_bias)

    packed = pack_rows(route, rows)
    arrived = {0: packed[0]}
    for shift in (1, 3, 2):
        arrived[shift] = hop(packed[shift], shift)
    other = {0: swap(packed[0])}
    other_route, other_query = swap(route), swap(query_rows)
    first = project([arrived[0], other[0]], *weights, first=True)
    weights = (first[3], first[4], *weights[2:])
    packed_query = pack_queries(
        after(route, first[2]), other_route, query_rows, other_query, rows, router_weight.T
    )
    gates = packed_query[OWNERS]
    for shift in (1, 3):
        arrived[shift] = after(arrived[shift], gates)
        other[shift] = swap(arrived[shift])
    second = project([arrived[1], other[1], arrived[3], other[3]], *weights)
    arrived[2] = after(arrived[2], second[2])
    other[2] = swap(arrived[2])
    query_in = [packed_query[0]]
    query_in += [hop(after(packed_query[shift], arrived[2]), shift) for shift in (1, 2, 3)]
    third = project([arrived[2], other[2]], *weights)
    units, values, decays = zip(first[:3], second, third)

    message, column, row = block_state(units, values, decays)
    slices = lax.all_to_all(message, "context", 0, 0, tiled=True)
    entry = lax.all_to_all(prefix(slices), "context", 0, 0, tiled=True)
    inner = inner_reads(units, values, query_in, column, row)
    reads = read_out(query_in, inner, column, entry.reshape(HEADS, HEAD_DIM, HEAD_DIM))

    own = [reads[0]] + [hop(reads[shift], -shift) for shift in (1, 2, 3)]
    paired = [swap(part) for part in own]
    return mix_reads(route, gates, norm_gain[None], own, paired)[None]


def solution(mesh):
    in_specs = (
        P(("context", "dp"), "memory", None),
        P(("context", "dp"), "memory", None),
        P(("context", "dp"), "memory", None),
        P(),
        P("memory", None, "dp"),
        P("memory", None, "dp"),
        P("memory", None, "dp"),
        P("memory", "dp"),
        P(),
    )
    out_specs = P(("context", "dp"), "memory", None)
    return jax.shard_map(shards, mesh=mesh, in_specs=in_specs, out_specs=out_specs, check_vma=False)
```

```python
import functools

import jax
import jax.numpy as jnp
from jax import lax
from jax.experimental import pallas as pl
from jax.experimental.pallas import tpu as pltpu
from jax.sharding import PartitionSpec as P

D = 4096
HEAD_DIM = 128
CAP = 80
ROWS = 128
OWNERS = 4
CHUNKS = 8
SLOTS = CHUNKS * CAP
HALF = 1024
HEADS = HALF // HEAD_DIM
EMPTY = 64.0
PAD = 128
PACKS = 4
RING = 4
PIECE = HALF // RING
TAIL = 16
F32 = jnp.float32
BF16 = jnp.bfloat16
MIB = 1 << 20


def iota(shape, axis):
    return lax.broadcasted_iota(jnp.int32, shape, axis)


def dot(a, b):
    return jnp.dot(a, b, preferred_element_type=F32)


def dot_rows(a, b):
    return lax.dot_general(a, b, (((1,), (1,)), ((), ())), preferred_element_type=F32)


def dot_columns(a, b):
    return lax.dot_general(a, b, (((0,), (0,)), ((), ())), preferred_element_type=F32)


def near(shape, dtype):
    return pltpu.VMEM(shape, dtype)


def position(shift, partner, owner, core):
    return (core ^ partner) * OWNERS + (owner ^ shift)


def membership(route):
    memory = iota((8, ROWS), 0)
    named = ((route[0:1] == memory) | (route[1:2] == memory)).astype(F32)
    before = (iota((ROWS, ROWS), 0) < iota((ROWS, ROWS), 1)).astype(F32).astype(BF16)
    slot = dot(named.astype(BF16), before)
    return named, jnp.where(named > 0.0, slot, -1.0)


def one_hot(place, memory, slots=CAP):
    mine = jnp.sum(jnp.where(iota(place.shape, 0) == memory, place, 0.0), axis=0, keepdims=True)
    return (iota((slots, ROWS), 0).astype(F32) == mine).astype(F32)


def kernel_call(kernel, name, out_shape, scratch, limit, *operands, hbm=(), moved=1):
    spaces = [pltpu.HBM if at in hbm else pltpu.VMEM for at in range(len(operands))]
    return pl.pallas_call(
        kernel,
        out_shape=out_shape,
        in_specs=[pl.BlockSpec(memory_space=space) for space in spaces],
        out_specs=jax.tree.map(lambda _: pl.BlockSpec(memory_space=pltpu.VMEM), out_shape),
        scratch_shapes=scratch,
        compiler_params=pltpu.CompilerParams(vmem_limit_bytes=limit * MIB),
        cost_estimate=pl.CostEstimate(flops=1, bytes_accessed=moved, transcendentals=0),
        name=name,
    )(*operands)


def pack_rows_kernel(route_hbm, rows_hbm, *refs):
    out_refs, (route_ref, rows_ref, sems) = refs[:OWNERS], refs[OWNERS:]
    owner = lax.axis_index("memory")
    width = D // PACKS
    route_copy = pltpu.make_async_copy(route_hbm, route_ref, sems.at[PACKS])
    route_copy.start()
    copies = []
    for at in range(PACKS):
        columns = slice(at * width, (at + 1) * width)
        copies.append(
            pltpu.make_async_copy(rows_hbm.at[:, columns], rows_ref.at[:, columns], sems.at[at])
        )
        copies[at].start()
    route_copy.wait()
    place = membership(route_ref[...])[1]
    pick = jnp.concatenate([one_hot(place, owner ^ shift) for shift in range(OWNERS)], axis=0)
    empty = jnp.sum(pick, axis=1, keepdims=True) == 0.0
    pick = pick.astype(BF16)
    first_lane = iota((OWNERS * CAP, HEAD_DIM), 1) == 0
    for at in range(PACKS):
        copies[at].wait()
        part = dot(pick, rows_ref[:, at * width : (at + 1) * width])
        if at == 0:
            marked = jnp.where(first_lane & empty, EMPTY, part[:, :HEAD_DIM])
            part = jnp.concatenate([marked, part[:, HEAD_DIM:]], axis=1)
        part = part.astype(BF16)
        for shift in range(OWNERS):
            out_refs[shift][:, at * width : (at + 1) * width] = part[
                shift * CAP : (shift + 1) * CAP
            ]
    out_refs[2][:, D:] = jnp.zeros((CAP, PAD), BF16)


def pack_rows(route, rows):
    out = [near((CAP, D + PAD * (shift == 2)), BF16) for shift in range(OWNERS)]
    scratch = [
        pltpu.VMEM((2, ROWS), jnp.int32),
        pltpu.VMEM((ROWS, D), BF16),
        pltpu.SemaphoreType.DMA((PACKS + 1,)),
    ]
    return kernel_call(pack_rows_kernel, "pack_rows", out, scratch, 56, route, rows, hbm=(0, 1))


def pack_queries_kernel(
    route_ref, other_route_ref, query_ref, other_query_ref, rows_ref, router_ref, *out_refs
):
    owner, core = lax.axis_index("memory"), lax.axis_index("dp")
    gates_ref = out_refs[OWNERS]
    mine = pl.multiple_of(core * HALF, HALF)
    for side, (routes, queries) in enumerate(
        ((route_ref, query_ref), (other_route_ref, other_query_ref))
    ):
        named, place = membership(routes[...])
        pick = jnp.concatenate(
            [one_hot(place, owner ^ shift) for shift in range(OWNERS)], axis=0
        ).astype(BF16)
        part = dot(pick, queries[:, pl.ds(mine, HALF)]).astype(BF16)
        for shift in range(OWNERS):
            out_refs[shift][core ^ side] = part[shift * CAP : (shift + 1) * CAP]
        if side == 0:
            score = dot_rows(router_ref[...], rows_ref[...])
            chosen = jax.nn.sigmoid(score) * named[:OWNERS]
            gates = chosen / jnp.sum(chosen, axis=0, keepdims=True)
            gates_ref[...] = jnp.concatenate(
                [gates, jnp.zeros((128 - OWNERS, ROWS), F32)], axis=0
            ).T


def pack_queries(route, other_route, queries, other_queries, rows, router_weight):
    out = [near((2, CAP, HALF), BF16)] * OWNERS
    out = out + [near((ROWS, 128), F32)]
    operands = (route, other_route, queries, other_queries, rows, router_weight)
    return kernel_call(
        pack_queries_kernel, "pack_queries", out, (), 12, *operands, moved=4 * MIB
    )


def log_sigmoid(x):
    small = jnp.exp(-jnp.abs(x))
    near = 1.0 + small
    tiny = near == 1.0
    log1p = jnp.where(tiny, small, jnp.log(near) * (small / jnp.where(tiny, 1.0, near - 1.0)))
    return jnp.minimum(x, 0.0) - log1p


WIDTH = 512


def project_parts(row_refs, decay_ref, bias_ref, outs, key_ref, value_ref, held, ready):
    count = len(row_refs)
    unit_out, value_out, decay_out = outs
    lives = []
    for at in range(count):
        rows = slice(at * CAP, (at + 1) * CAP)
        head = row_refs[at][:, :HEAD_DIM].astype(F32)
        lives.append(head[:, :1] < EMPTY / 2)
        held[rows, :HEAD_DIM] = jnp.where(lives[at], head, 0.0).astype(BF16)
        held[rows, HEAD_DIM:] = row_refs[at][:, HEAD_DIM:D]
    decay = log_sigmoid(dot_rows(held[...], decay_ref[...]) + bias_ref[...])
    decay_out[...] = jnp.zeros_like(decay_out)
    for at in range(count):
        decay_out[at, :, :HEADS] = jnp.where(lives[at], decay[at * CAP : (at + 1) * CAP], 0.0)
    for start in range(0, HALF, WIDTH):
        ready(start // WIDTH)
        columns = slice(start, start + WIDTH)
        keys = dot(held[...], key_ref[:, columns]).astype(BF16).astype(F32)
        for head in range(0, WIDTH, HEAD_DIM):
            key = keys[:, head : head + HEAD_DIM]
            unit = key * lax.rsqrt(jnp.sum(key * key, axis=1, keepdims=True) + 1e-06)
            unit_out[:, :, start + head : start + head + HEAD_DIM] = unit.astype(BF16).reshape(
                count, CAP, HEAD_DIM
            )
        values = dot(held[...], value_ref[:, columns]).astype(BF16)
        value_out[:, :, columns] = values.reshape(count, CAP, WIDTH)


def project_first_kernel(count, *refs):
    key_hbm, value_hbm, decay_ref, bias_ref = refs[count : count + 4]
    outs, (key_ref, value_ref, held, sems) = refs[count + 4 : count + 7], refs[count + 7 :]
    copies = []
    for at, start in enumerate(range(0, HALF, WIDTH)):
        columns = slice(start, start + WIDTH)
        for side, (far, near) in enumerate(((key_hbm, key_ref), (value_hbm, value_ref))):
            copies.append(
                pltpu.make_async_copy(far.at[:, columns], near.at[:, columns], sems.at[side, at])
            )
    for copy in copies:
        copy.start()

    def ready(at):
        copies[2 * at].wait()
        copies[2 * at + 1].wait()

    project_parts(refs[:count], decay_ref, bias_ref, outs, key_ref, value_ref, held, ready)


def project_next_kernel(count, *refs):
    key_ref, value_ref, decay_ref, bias_ref = refs[count : count + 4]
    outs, held = refs[count + 4 : count + 7], refs[count + 7]
    project_parts(
        refs[:count], decay_ref, bias_ref, outs, key_ref, value_ref, held, lambda at: None
    )


def project(row_parts, key_weight, value_weight, decay_weight, decay_bias, first=False):
    count = len(row_parts)
    out = [near((count, CAP, HALF), BF16)] * 2
    out = out + [near((count, CAP, 128), F32)]
    scratch = [pltpu.VMEM((count * CAP, D), BF16)]
    kernel = project_first_kernel if first else project_next_kernel
    if first:
        out = out + [near((D, HALF), BF16)] * 2
        scratch = scratch + [pltpu.SemaphoreType.DMA((2, HALF // WIDTH))]
    return kernel_call(
        functools.partial(kernel, count),
        f"project_{count}",
        out,
        scratch,
        40 if first else 12,
        *row_parts,
        key_weight,
        value_weight,
        decay_weight,
        decay_bias,
        hbm=(count, count + 1) if first else (),
    )


GROUPS = (((0, 0), (0, 1)), ((1, 0), (1, 1), (3, 0), (3, 1)), ((2, 0), (2, 1)))


def token_order(refs, held):
    owner, core = lax.axis_index("memory"), lax.axis_index("dp")
    for group, ref in zip(GROUPS, refs):
        for at, (shift, partner) in enumerate(group):
            held[position(shift, partner, owner, core)] = ref[at]


def head_columns(head):
    return slice(head * HEAD_DIM, (head + 1) * HEAD_DIM)


def place_in_context():
    context = lax.axis_index("context")
    return context >> 2, context & (RING - 1)


def two_parts(number):
    wide = jnp.broadcast_to(number, (TAIL, 128))
    high = wide.astype(BF16).astype(F32)
    return jnp.where(iota((TAIL, 128), 0) < TAIL // 2, high, wide - high).astype(BF16)


def from_parts(rows):
    return rows[:1].astype(F32) + rows[TAIL // 2 : TAIL // 2 + 1].astype(F32)


def state_kernel(*refs):
    unit_refs, value_refs, decay_refs = refs[0:3], refs[3:6], refs[6:9]
    messages = refs[9:13]
    column_out, row_out, units, values, decays, quarters = refs[13:]
    token_order(decay_refs, decays)
    total = decays[...].reshape(SLOTS, 128).T[:HEADS]
    lane = iota((HEADS, SLOTS), 1)
    reach = 1
    while reach < SLOTS:
        total = total + jnp.where(lane >= reach, pltpu.roll(total, reach, 1), 0.0)
        reach *= 2
    row_out[...] = total
    running = jnp.concatenate([total, jnp.zeros((128 - HEADS, SLOTS), F32)], axis=0).T
    column_out[...] = running
    token_order(unit_refs, units)
    token_order(value_refs, values)
    last = running[SLOTS - 1 : SLOTS]
    fade = jnp.exp(last - running)
    for head in range(HEADS):
        unit = units[:, :, head_columns(head)].reshape(SLOTS, HEAD_DIM).astype(F32)
        faded = (unit * fade[:, head : head + 1]).astype(BF16)
        value = values[:, :, head_columns(head)].reshape(SLOTS, HEAD_DIM)
        state = dot_columns(faded, value).astype(BF16)
        at = head % 2 * HEAD_DIM
        quarters[head // 2, at : at + HEAD_DIM] = state
        tail = PIECE + head % 2 * TAIL
        quarters[head // 2, tail : tail + TAIL] = two_parts(last[:, head : head + 1])
    _, column = place_in_context()
    for shift in range(RING):
        messages[shift][...] = quarters[column ^ shift]


def block_state(units, values, decays):
    out = [near((PIECE + 2 * TAIL, 128), BF16)] * RING + [
        near((SLOTS, 128), F32),
        near((HEADS, SLOTS), F32),
        near((CHUNKS, CAP, HALF), BF16),
        near((CHUNKS, CAP, HALF), BF16),
    ]
    scratch = [
        pltpu.VMEM((CHUNKS, CAP, 128), F32),
        pltpu.VMEM((RING, PIECE + 2 * TAIL, 128), BF16),
    ]
    return kernel_call(
        state_kernel, "block_state", out, scratch, 12, *units, *values, *decays
    )


def ring_order(refs, held, me):
    for shift in range(RING):
        held[me ^ shift] = refs[shift][...]


def row_prefix_kernel(*refs):
    pieces, (whole, before, faded, held) = refs[:RING], refs[RING:]
    ring_order(pieces, held, place_in_context()[1])
    for head in range(2):
        rows = slice(head * HEAD_DIM, (head + 1) * HEAD_DIM)
        tail = slice(PIECE + head * TAIL, PIECE + (head + 1) * TAIL)
        state, total = jnp.zeros((HEAD_DIM, 128), F32), jnp.zeros((1, 128), F32)
        for column in range(RING):
            before[column, rows] = state
            faded[column, head * 8 : head * 8 + 8] = jnp.broadcast_to(jnp.exp(total), (8, 128))
            ended = from_parts(held[column, tail])
            state = jnp.exp(ended) * state + held[column, rows].astype(F32)
            total = total + ended
        whole[rows] = state.astype(BF16)
        whole[tail] = two_parts(total)


def row_prefix(pieces):
    out = [
        near((PIECE + 2 * TAIL, 128), BF16),
        near((RING, PIECE, 128), F32),
        near((RING, 16, 128), F32),
    ]
    scratch = [pltpu.VMEM((RING, PIECE + 2 * TAIL, 128), BF16)]
    return kernel_call(row_prefix_kernel, "row_prefix", out, scratch, 8, *pieces)


def entry_kernel(*refs):
    pieces, (before, faded) = refs[:RING], refs[RING : RING + 2]
    out_refs, (held, entries) = refs[RING + 2 : 2 * RING + 2], refs[2 * RING + 2 :]
    row, mine = place_in_context()
    ring_order(pieces, held, row)
    for head in range(2):
        rows = slice(head * HEAD_DIM, (head + 1) * HEAD_DIM)
        tail = slice(PIECE + head * TAIL, PIECE + (head + 1) * TAIL)
        state = jnp.zeros((HEAD_DIM, 128), F32)
        for earlier in range(RING - 1):
            kept = jnp.exp(from_parts(held[earlier, tail])) * state
            kept = kept + held[earlier, rows].astype(F32)
            state = jnp.where(earlier < row, kept, state)
        for column in range(RING):
            fade = faded[column, head * 8 : head * 8 + 1]
            entries[column, rows] = (before[column, rows] + fade * state).astype(BF16)
    for shift in range(RING):
        out_refs[shift][...] = entries[mine ^ shift]


def entry_states(pieces, before, faded):
    out = [near((PIECE, 128), BF16)] * RING
    scratch = [
        pltpu.VMEM((RING, PIECE + 2 * TAIL, 128), BF16),
        pltpu.VMEM((RING, PIECE, 128), BF16),
    ]
    return kernel_call(entry_kernel, "entry_states", out, scratch, 8, *pieces, before, faded)


def order_queries(query_refs, held):
    owner = lax.axis_index("memory")
    for shift in range(OWNERS):
        for core in range(2):
            held[core * OWNERS + (owner ^ shift)] = query_refs[shift][core]


def inner_kernel(start, *refs):
    units, values, column_ref, row_ref = refs[0:4]
    if start == 0:
        inner, queries = refs[8:10]
        order_queries(refs[4:8], queries)
    else:
        queries, inner = refs[4:6]
    tile = 2 * CAP
    for head in range(start, start + HEADS // 2):
        columns = head_columns(head)
        running = column_ref[:, head : head + 1]
        running_row = row_ref[head : head + 1]
        unit = units[:, :, columns].reshape(SLOTS, HEAD_DIM)
        value = values[:, :, columns].reshape(SLOTS, HEAD_DIM)
        for block in range(SLOTS // tile):
            reach = -(-((block + 1) * tile) // 128) * 128
            query = queries[2 * block : 2 * block + 2, :, columns].reshape(tile, HEAD_DIM)
            score = dot_rows(query, unit[:reach])
            spread = running[block * tile : (block + 1) * tile] - running_row[:, :reach]
            causal = iota((tile, reach), 0) + block * tile >= iota((tile, reach), 1)
            score = (score * jnp.exp(jnp.where(causal, spread, -1e30))).astype(BF16)
            result = dot(score, value[:reach])
            inner[2 * block : 2 * block + 2, :, head_columns(head - start)] = result.reshape(2, CAP, HEAD_DIM)


def inner_reads(start, units, values, column, row, *queries):
    out = [near((CHUNKS, CAP, HALF // 2), F32)]
    if start == 0:
        out = out + [near((CHUNKS, CAP, HALF), BF16)]
    kernel = functools.partial(inner_kernel, start)
    operands = (units, values, column, row, *queries)
    return kernel_call(kernel, f"inner_reads_{start}", out, (), 16, *operands)


def read_kernel(*refs):
    queries, inners, column_ref = refs[0], refs[1:3], refs[3]
    out_refs, (reads, entries) = refs[8:12], refs[12:]
    ring_order(refs[4:8], entries, place_in_context()[1])
    owner = lax.axis_index("memory")
    fade = jnp.exp(column_ref[...])
    for head in range(HEADS):
        columns = head_columns(head)
        carried = dot(queries[:, :, columns].reshape(SLOTS, HEAD_DIM), entries[head // 2, head % 2 * HEAD_DIM : (head % 2 + 1) * HEAD_DIM])
        inner = inners[head // 4][:, :, head_columns(head % 4)]
        result = inner.reshape(SLOTS, HEAD_DIM) + fade[:, head : head + 1] * carried
        reads[:, :, columns] = result.astype(BF16).reshape(CHUNKS, CAP, HEAD_DIM)
    for shift in range(OWNERS):
        for core in range(2):
            out_refs[shift][core] = reads[core * OWNERS + (owner ^ shift)]


def read_out(queries, inners, column, entry):
    out = [near((2, CAP, HALF), BF16)] * OWNERS
    scratch = [pltpu.VMEM((CHUNKS, CAP, HALF), BF16), pltpu.VMEM((RING, PIECE, 128), BF16)]
    return kernel_call(
        read_kernel, "read_out", out, scratch, 12, queries, *inners, column, *entry
    )


def mix_kernel(route_ref, gates_ref, gain_ref, *refs):
    own_refs, other_refs, out_ref = refs[0:4], refs[4:8], refs[8]
    owner, core = lax.axis_index("memory"), lax.axis_index("dp")
    place = membership(route_ref[...])[1]
    picks, gates = [], []
    lane = iota((ROWS, 128), 1)
    for shift in range(OWNERS):
        memory = owner ^ shift
        picks.append(one_hot(place, memory, 128).T.astype(BF16)[:, :CAP])
        gate = jnp.where(lane == memory, gates_ref[...], 0.0)
        gates.append(jnp.sum(gate, axis=1, keepdims=True))
    for side, reads in enumerate((own_refs, other_refs)):
        start = (core ^ side) * HALF
        mixture = jnp.zeros((ROWS, HALF), F32)
        for shift in range(OWNERS):
            mixture = mixture + gates[shift] * dot(picks[shift], reads[shift][core])
        for head in range(HEADS):
            columns = pl.ds(pl.multiple_of(start + head * HEAD_DIM, HEAD_DIM), HEAD_DIM)
            mix = mixture[:, head_columns(head)]
            scale = lax.rsqrt(jnp.mean(mix * mix, axis=1, keepdims=True) + 1e-05)
            out_ref[:, columns] = (mix * scale * gain_ref[:, columns]).astype(BF16)


def mix_reads(route, gates, gain, own, other):
    out = jax.ShapeDtypeStruct((ROWS, 2 * HALF), BF16)
    return kernel_call(
        mix_kernel, "mix_reads", out, (), 12, route, gates, gain, *own, *other
    )


def after(array, *first):
    return lax.optimization_barrier((array, *first))[0]


def hop(array, shift):
    return lax.ppermute(array, "memory", [(i, i ^ shift) for i in range(OWNERS)])


def exchange(arrays, stride):
    out = [arrays[0]]
    for shift in (1, 2, 3):
        pairs = [(i, i ^ shift * stride) for i in range(RING * RING)]
        out.append(lax.ppermute(arrays[shift], "context", pairs))
    return out


def swap(array):
    return lax.ppermute(array, "dp", [(0, 1), (1, 0)])


def shards(
    hidden,
    queries,
    route_ids,
    router_weight,
    key_weight,
    value_weight,
    decay_weight,
    decay_bias,
    norm_gain,
):
    rows, query_rows, route = hidden[0], queries[0], route_ids[0].T
    weights = (key_weight[0], value_weight[0], decay_weight[0].T, decay_bias)

    packed = pack_rows(route, rows)
    arrived = {0: packed[0]}
    for shift in (1, 3):
        arrived[shift] = hop(packed[shift], shift)
    other = {0: swap(packed[0])}
    other_route, other_query = swap(route), swap(query_rows)
    first = project([arrived[0], other[0]], *weights, first=True)
    weights = (first[3], first[4], *weights[2:])
    packed_query = pack_queries(
        after(route, first[2]), other_route, query_rows, other_query, rows, router_weight.T
    )
    gates = packed_query[OWNERS]
    for shift in (1, 3):
        arrived[shift] = after(arrived[shift], gates)
    arrived[2] = hop(after(packed[2], arrived[1], arrived[3]), 2)
    for shift in (1, 3):
        other[shift] = swap(arrived[shift])
    second = project([arrived[1], other[1], arrived[3], other[3]], *weights)
    arrived[2] = after(arrived[2], second[2])
    other[2] = swap(arrived[2])
    third = project([arrived[2], other[2]], *weights)
    units, values, decays = zip(first[:3], second, third)

    *messages, column, row, units, values = block_state(units, values, decays)
    query_in = [packed_query[0]]
    query_in += [hop(after(packed_query[shift], second[2]), shift) for shift in (1, 2, 3)]
    whole, before, faded = row_prefix(exchange(messages, 1))
    totals = exchange([whole] * RING, RING)
    inner_low, ordered = inner_reads(0, units, values, column, row, *query_in)
    totals[0] = after(totals[0], inner_low)
    entry = exchange(entry_states(totals, before, faded), 1)
    (inner_high,) = inner_reads(HEADS // 2, units, values, column, row, ordered)
    reads = read_out(ordered, (inner_low, inner_high), column, entry)

    own = [reads[0]] + [hop(reads[shift], shift) for shift in (1, 2, 3)]
    paired = [swap(part) for part in own]
    return mix_reads(route, gates, norm_gain[None], own, paired)[None]


def solution(mesh):
    in_specs = (
        P(("context", "dp"), "memory", None),
        P(("context", "dp"), "memory", None),
        P(("context", "dp"), "memory", None),
        P(),
        P("memory", None, "dp"),
        P("memory", None, "dp"),
        P("memory", None, "dp"),
        P("memory", "dp"),
        P(),
    )
    out_specs = P(("context", "dp"), "memory", None)
    return jax.shard_map(shards, mesh=mesh, in_specs=in_specs, out_specs=out_specs, check_vma=False)
```

```python
import functools

import jax
import jax.numpy as jnp
from jax import lax
from jax.experimental import pallas as pl
from jax.experimental.pallas import tpu as pltpu
from jax.sharding import PartitionSpec as P

D = 4096
HEAD_DIM = 128
CAP = 80
ROWS = 128
OWNERS = 4
CHUNKS = 8
SLOTS = CHUNKS * CAP
HALF = 1024
HEADS = HALF // HEAD_DIM
EMPTY = 64.0
PAD = 128
PACKS = 4
NEAR, FAR = (0, 1, 3), 2
RING = 4
PIECE = HALF // RING
TAIL = 16
F32 = jnp.float32
BF16 = jnp.bfloat16
MIB = 1 << 20


def iota(shape, axis):
    return lax.broadcasted_iota(jnp.int32, shape, axis)


def dot(a, b):
    return jnp.dot(a, b, preferred_element_type=F32)


def dot_rows(a, b):
    return lax.dot_general(a, b, (((1,), (1,)), ((), ())), preferred_element_type=F32)


def dot_columns(a, b):
    return lax.dot_general(a, b, (((0,), (0,)), ((), ())), preferred_element_type=F32)


def near(shape, dtype):
    return pltpu.VMEM(shape, dtype)


def position(shift, partner, owner, core):
    return (core ^ partner) * OWNERS + (owner ^ shift)


def membership(route):
    memory = iota((8, ROWS), 0)
    named = ((route[0:1] == memory) | (route[1:2] == memory)).astype(F32)
    before = (iota((ROWS, ROWS), 0) < iota((ROWS, ROWS), 1)).astype(F32).astype(BF16)
    slot = dot(named.astype(BF16), before)
    return named, jnp.where(named > 0.0, slot, -1.0)


def one_hot(place, memory, slots=CAP):
    mine = jnp.sum(jnp.where(iota(place.shape, 0) == memory, place, 0.0), axis=0, keepdims=True)
    return (iota((slots, ROWS), 0).astype(F32) == mine).astype(F32)


def kernel_call(kernel, name, out_shape, scratch, limit, *operands, hbm=(), moved=1):
    spaces = [pltpu.HBM if at in hbm else pltpu.VMEM for at in range(len(operands))]
    return pl.pallas_call(
        kernel,
        out_shape=out_shape,
        in_specs=[pl.BlockSpec(memory_space=space) for space in spaces],
        out_specs=jax.tree.map(lambda _: pl.BlockSpec(memory_space=pltpu.VMEM), out_shape),
        scratch_shapes=scratch,
        compiler_params=pltpu.CompilerParams(vmem_limit_bytes=limit * MIB),
        cost_estimate=pl.CostEstimate(flops=1, bytes_accessed=moved, transcendentals=0),
        name=name,
    )(*operands)


def pack_rows_kernel(route_hbm, rows_hbm, *refs):
    out_refs, (route_ref, rows_ref, sems) = refs[:OWNERS], refs[OWNERS:]
    owner = lax.axis_index("memory")
    width = D // PACKS
    route_copy = pltpu.make_async_copy(route_hbm, route_ref, sems.at[PACKS])
    route_copy.start()
    copies = []
    for at in range(PACKS):
        columns = slice(at * width, (at + 1) * width)
        copies.append(
            pltpu.make_async_copy(rows_hbm.at[:, columns], rows_ref.at[:, columns], sems.at[at])
        )
        copies[at].start()
    route_copy.wait()
    place = membership(route_ref[...])[1]
    pick = jnp.concatenate([one_hot(place, owner ^ shift) for shift in range(OWNERS)], axis=0)
    empty = jnp.sum(pick, axis=1, keepdims=True) == 0.0
    pick = pick.astype(BF16)
    first_lane = iota((OWNERS * CAP, HEAD_DIM), 1) == 0
    for at in range(PACKS):
        copies[at].wait()
        part = dot(pick, rows_ref[:, at * width : (at + 1) * width])
        if at == 0:
            marked = jnp.where(first_lane & empty, EMPTY, part[:, :HEAD_DIM])
            part = jnp.concatenate([marked, part[:, HEAD_DIM:]], axis=1)
        part = part.astype(BF16)
        for shift in range(OWNERS):
            out_refs[shift][:, at * width : (at + 1) * width] = part[
                shift * CAP : (shift + 1) * CAP
            ]
    out_refs[2][:, D:] = jnp.zeros((CAP, PAD), BF16)


def pack_rows(route, rows):
    out = [near((CAP, D + PAD * (shift == 2)), BF16) for shift in range(OWNERS)]
    scratch = [
        pltpu.VMEM((2, ROWS), jnp.int32),
        pltpu.VMEM((ROWS, D), BF16),
        pltpu.SemaphoreType.DMA((PACKS + 1,)),
    ]
    return kernel_call(pack_rows_kernel, "pack_rows", out, scratch, 56, route, rows, hbm=(0, 1))


def pack_queries_kernel(
    route_ref, other_route_ref, query_ref, other_query_ref, rows_ref, router_ref, *out_refs
):
    owner, core = lax.axis_index("memory"), lax.axis_index("dp")
    gates_ref, picks_ref = out_refs[OWNERS:]
    mine = pl.multiple_of(core * HALF, HALF)
    for side, (routes, queries) in enumerate(
        ((route_ref, query_ref), (other_route_ref, other_query_ref))
    ):
        named, place = membership(routes[...])
        pick = jnp.concatenate(
            [one_hot(place, owner ^ shift) for shift in range(OWNERS)], axis=0
        ).astype(BF16)
        part = dot(pick, queries[:, pl.ds(mine, HALF)]).astype(BF16)
        for shift in range(OWNERS):
            out_refs[shift][core ^ side] = part[shift * CAP : (shift + 1) * CAP]
        if side == 0:
            for shift in range(OWNERS):
                picks_ref[shift] = one_hot(place, owner ^ shift, 128).T.astype(BF16)
            score = dot_rows(router_ref[...], rows_ref[...])
            chosen = jax.nn.sigmoid(score) * named[:OWNERS]
            gates = chosen / jnp.sum(chosen, axis=0, keepdims=True)
            memory = iota((OWNERS, ROWS), 0)
            by_shift = [
                jnp.sum(jnp.where(memory == owner ^ shift, gates, 0.0), axis=0, keepdims=True)
                for shift in range(OWNERS)
            ]
            by_shift.append(jnp.zeros((128 - OWNERS, ROWS), F32))
            gates_ref[...] = jnp.concatenate(by_shift, axis=0).T


def pack_queries(route, other_route, queries, other_queries, rows, router_weight):
    out = [near((2, CAP, HALF), BF16)] * OWNERS
    out = out + [near((ROWS, 128), F32), near((OWNERS, ROWS, 128), BF16)]
    operands = (route, other_route, queries, other_queries, rows, router_weight)
    return kernel_call(
        pack_queries_kernel, "pack_queries", out, (), 12, *operands, moved=4 * MIB
    )


def log_sigmoid(x):
    small = jnp.exp(-jnp.abs(x))
    near = 1.0 + small
    tiny = near == 1.0
    log1p = jnp.where(tiny, small, jnp.log(near) * (small / jnp.where(tiny, 1.0, near - 1.0)))
    return jnp.minimum(x, 0.0) - log1p


WIDTH = 512


def project_parts(row_refs, decay_ref, bias_ref, outs, key_ref, value_ref, held, ready):
    count = len(row_refs)
    unit_out, value_out, decay_out = outs
    lives = []
    for at in range(count):
        rows = slice(at * CAP, (at + 1) * CAP)
        head = row_refs[at][:, :HEAD_DIM].astype(F32)
        lives.append(head[:, :1] < EMPTY / 2)
        held[rows, :HEAD_DIM] = jnp.where(lives[at], head, 0.0).astype(BF16)
        held[rows, HEAD_DIM:] = row_refs[at][:, HEAD_DIM:D]
    decay = log_sigmoid(dot_rows(held[...], decay_ref[...]) + bias_ref[...])
    decay_out[...] = jnp.zeros_like(decay_out)
    for at in range(count):
        decay_out[at, :, :HEADS] = jnp.where(lives[at], decay[at * CAP : (at + 1) * CAP], 0.0)
    for start in range(0, HALF, WIDTH):
        ready(start // WIDTH)
        columns = slice(start, start + WIDTH)
        keys = dot(held[...], key_ref[:, columns]).astype(BF16).astype(F32)
        for head in range(0, WIDTH, HEAD_DIM):
            key = keys[:, head : head + HEAD_DIM]
            unit = key * lax.rsqrt(jnp.sum(key * key, axis=1, keepdims=True) + 1e-06)
            unit_out[:, :, start + head : start + head + HEAD_DIM] = unit.astype(BF16).reshape(
                count, CAP, HEAD_DIM
            )
        values = dot(held[...], value_ref[:, columns]).astype(BF16)
        value_out[:, :, columns] = values.reshape(count, CAP, WIDTH)


def project_first_kernel(count, *refs):
    key_hbm, value_hbm, decay_ref, bias_ref = refs[count : count + 4]
    outs, (key_ref, value_ref, held, sems) = refs[count + 4 : count + 7], refs[count + 7 :]
    copies = []
    for at, start in enumerate(range(0, HALF, WIDTH)):
        columns = slice(start, start + WIDTH)
        for side, (far, near) in enumerate(((key_hbm, key_ref), (value_hbm, value_ref))):
            copies.append(
                pltpu.make_async_copy(far.at[:, columns], near.at[:, columns], sems.at[side, at])
            )
    for copy in copies:
        copy.start()

    def ready(at):
        copies[2 * at].wait()
        copies[2 * at + 1].wait()

    project_parts(refs[:count], decay_ref, bias_ref, outs, key_ref, value_ref, held, ready)


def project_next_kernel(count, *refs):
    key_ref, value_ref, decay_ref, bias_ref = refs[count : count + 4]
    outs, held = refs[count + 4 : count + 7], refs[count + 7]
    project_parts(
        refs[:count], decay_ref, bias_ref, outs, key_ref, value_ref, held, lambda at: None
    )


def project(row_parts, key_weight, value_weight, decay_weight, decay_bias, first=False):
    count = len(row_parts)
    out = [near((count, CAP, HALF), BF16)] * 2
    out = out + [near((count, CAP, 128), F32)]
    scratch = [pltpu.VMEM((count * CAP, D), BF16)]
    kernel = project_first_kernel if first else project_next_kernel
    if first:
        out = out + [near((D, HALF), BF16)] * 2
        scratch = scratch + [pltpu.SemaphoreType.DMA((2, HALF // WIDTH))]
    return kernel_call(
        functools.partial(kernel, count),
        f"project_{count}",
        out,
        scratch,
        40 if first else 12,
        *row_parts,
        key_weight,
        value_weight,
        decay_weight,
        decay_bias,
        hbm=(count, count + 1) if first else (),
    )


GROUPS = (((0, 0), (0, 1)), ((1, 0), (1, 1), (3, 0), (3, 1)), ((2, 0), (2, 1)))


def token_order(refs, held):
    owner, core = lax.axis_index("memory"), lax.axis_index("dp")
    for group, ref in zip(GROUPS, refs):
        for at, (shift, partner) in enumerate(group):
            held[position(shift, partner, owner, core)] = ref[at]


def head_columns(head):
    return slice(head * HEAD_DIM, (head + 1) * HEAD_DIM)


def place_in_context():
    context = lax.axis_index("context")
    return context >> 2, context & (RING - 1)


def two_parts(number):
    wide = jnp.broadcast_to(number, (TAIL, 128))
    high = wide.astype(BF16).astype(F32)
    return jnp.where(iota((TAIL, 128), 0) < TAIL // 2, high, wide - high).astype(BF16)


def from_parts(rows):
    return rows[:1].astype(F32) + rows[TAIL // 2 : TAIL // 2 + 1].astype(F32)


def state_kernel(*refs):
    unit_refs, value_refs, decay_refs = refs[0:3], refs[3:6], refs[6:9]
    messages = refs[9:13]
    column_out, row_out, units, values, decays, quarters = refs[13:]
    token_order(decay_refs, decays)
    total = decays[...].reshape(SLOTS, 128).T[:HEADS]
    lane = iota((HEADS, SLOTS), 1)
    reach = 1
    while reach < SLOTS:
        total = total + jnp.where(lane >= reach, pltpu.roll(total, reach, 1), 0.0)
        reach *= 2
    row_out[...] = total
    running = jnp.concatenate([total, jnp.zeros((128 - HEADS, SLOTS), F32)], axis=0).T
    column_out[...] = running.reshape(CHUNKS, CAP, 128)
    token_order(unit_refs, units)
    token_order(value_refs, values)
    last = running[SLOTS - 1 : SLOTS]
    fade = jnp.exp(last - running)
    for head in range(HEADS):
        unit = units[:, :, head_columns(head)].reshape(SLOTS, HEAD_DIM).astype(F32)
        faded = (unit * fade[:, head : head + 1]).astype(BF16)
        value = values[:, :, head_columns(head)].reshape(SLOTS, HEAD_DIM)
        state = dot_columns(faded, value).astype(BF16)
        at = head % 2 * HEAD_DIM
        quarters[head // 2, at : at + HEAD_DIM] = state
        tail = PIECE + head % 2 * TAIL
        quarters[head // 2, tail : tail + TAIL] = two_parts(last[:, head : head + 1])
    _, column = place_in_context()
    for shift in range(RING):
        messages[shift][...] = quarters[column ^ shift]


def block_state(units, values, decays):
    out = [near((PIECE + 2 * TAIL, 128), BF16)] * RING + [
        near((CHUNKS, CAP, 128), F32),
        near((HEADS, SLOTS), F32),
        near((CHUNKS, CAP, HALF), BF16),
        near((CHUNKS, CAP, HALF), BF16),
    ]
    scratch = [
        pltpu.VMEM((CHUNKS, CAP, 128), F32),
        pltpu.VMEM((RING, PIECE + 2 * TAIL, 128), BF16),
    ]
    return kernel_call(
        state_kernel, "block_state", out, scratch, 12, *units, *values, *decays
    )


def ring_order(refs, held, me):
    for shift in range(RING):
        held[me ^ shift] = refs[shift][...]


def row_prefix_kernel(*refs):
    pieces, (whole, before, faded, held) = refs[:RING], refs[RING:]
    ring_order(pieces, held, place_in_context()[1])
    for head in range(2):
        rows = slice(head * HEAD_DIM, (head + 1) * HEAD_DIM)
        tail = slice(PIECE + head * TAIL, PIECE + (head + 1) * TAIL)
        state, total = jnp.zeros((HEAD_DIM, 128), F32), jnp.zeros((1, 128), F32)
        for column in range(RING):
            before[column, rows] = state
            faded[column, head * 8 : head * 8 + 8] = jnp.broadcast_to(jnp.exp(total), (8, 128))
            ended = from_parts(held[column, tail])
            state = jnp.exp(ended) * state + held[column, rows].astype(F32)
            total = total + ended
        whole[rows] = state.astype(BF16)
        whole[tail] = two_parts(total)


def row_prefix(pieces):
    out = [
        near((PIECE + 2 * TAIL, 128), BF16),
        near((RING, PIECE, 128), F32),
        near((RING, 16, 128), F32),
    ]
    scratch = [pltpu.VMEM((RING, PIECE + 2 * TAIL, 128), BF16)]
    return kernel_call(row_prefix_kernel, "row_prefix", out, scratch, 8, *pieces)


def entry_kernel(*refs):
    pieces, (before, faded) = refs[:RING], refs[RING : RING + 2]
    out_refs, (held, entries) = refs[RING + 2 : 2 * RING + 2], refs[2 * RING + 2 :]
    row, mine = place_in_context()
    ring_order(pieces, held, row)
    for head in range(2):
        rows = slice(head * HEAD_DIM, (head + 1) * HEAD_DIM)
        tail = slice(PIECE + head * TAIL, PIECE + (head + 1) * TAIL)
        state = jnp.zeros((HEAD_DIM, 128), F32)
        for earlier in range(RING - 1):
            kept = jnp.exp(from_parts(held[earlier, tail])) * state
            kept = kept + held[earlier, rows].astype(F32)
            state = jnp.where(earlier < row, kept, state)
        for column in range(RING):
            fade = faded[column, head * 8 : head * 8 + 1]
            entries[column, rows] = (before[column, rows] + fade * state).astype(BF16)
    for shift in range(RING):
        out_refs[shift][...] = entries[mine ^ shift]


def entry_states(pieces, before, faded):
    out = [near((PIECE, 128), BF16)] * RING
    scratch = [
        pltpu.VMEM((RING, PIECE + 2 * TAIL, 128), BF16),
        pltpu.VMEM((RING, PIECE, 128), BF16),
    ]
    return kernel_call(entry_kernel, "entry_states", out, scratch, 8, *pieces, before, faded)


def inner_kernel(shifts, *refs):
    units, values, column_ref, row_ref = refs[0:4]
    query_refs, inner = refs[4:-1], refs[-1]
    owner = lax.axis_index("memory")
    count = len(shifts) * CAP
    for core in range(2):
        reach = -(-(core + 1) * OWNERS * CAP // 128) * 128
        chunks = [core * OWNERS + (owner ^ shift) for shift in shifts]
        running = jnp.concatenate([column_ref[chunk] for chunk in chunks], axis=0)
        place = jnp.concatenate([iota((CAP, reach), 0) + chunk * CAP for chunk in chunks], axis=0)
        causal = place >= iota((count, reach), 1)
        for head in range(HEADS):
            columns = head_columns(head)
            query = jnp.concatenate([query[core, :, columns] for query in query_refs], axis=0)
            unit = units[:, :, columns].reshape(SLOTS, HEAD_DIM)[:reach]
            value = values[:, :, columns].reshape(SLOTS, HEAD_DIM)[:reach]
            spread = running[:, head : head + 1] - row_ref[head : head + 1, :reach]
            weight = jnp.exp(jnp.where(causal, spread, -1e30))
            score = (dot_rows(query, unit) * weight).astype(BF16)
            inner[:, core, :, columns] = dot(score, value).reshape(len(shifts), CAP, HEAD_DIM)


def inner_reads(shifts, units, values, column, row, *queries):
    out = near((len(shifts), 2, CAP, HALF), F32)
    kernel = functools.partial(inner_kernel, shifts)
    name = f"inner_reads_{len(shifts)}"
    return kernel_call(kernel, name, out, (), 16, units, values, column, row, *queries)


def read_kernel(*refs):
    query_refs, inner_near, inner_far, column_ref = refs[0:4], refs[4], refs[5], refs[6]
    out_refs, entries = refs[11:15], refs[15]
    ring_order(refs[7:11], entries, place_in_context()[1])
    owner = lax.axis_index("memory")
    inners = {shift: inner_near.at[at] for at, shift in enumerate(NEAR)}
    inners[FAR] = inner_far.at[0]
    pairs = [(shift, core) for shift in range(OWNERS) for core in range(2)]
    fade = jnp.concatenate([column_ref[c * OWNERS + (owner ^ s)] for s, c in pairs], axis=0)
    fade = jnp.exp(fade)
    for head in range(HEADS):
        columns = head_columns(head)
        query = jnp.concatenate([query_refs[s][c, :, columns] for s, c in pairs], axis=0)
        entry = entries[head // 2, head % 2 * HEAD_DIM : (head % 2 + 1) * HEAD_DIM]
        carried = fade[:, head : head + 1] * dot(query, entry)
        for at, (s, c) in enumerate(pairs):
            read = inners[s][c, :, columns] + carried[at * CAP : (at + 1) * CAP]
            out_refs[s][c, :, columns] = read.astype(BF16)


def read_out(queries, inner_near, inner_far, column, entry):
    out = [near((2, CAP, HALF), BF16)] * OWNERS
    scratch = [pltpu.VMEM((RING, PIECE, 128), BF16)]
    operands = (*queries, inner_near, inner_far, column, *entry)
    return kernel_call(read_kernel, "read_out", out, scratch, 12, *operands)


def mix_near_kernel(gates_ref, picks_ref, *refs):
    partial = refs[-1]
    core = lax.axis_index("dp")
    for side in range(2):
        total = jnp.zeros((ROWS, HALF), F32)
        for at, shift in enumerate(NEAR):
            reads = refs[side * len(NEAR) + at][core]
            total = total + gates_ref[:, shift : shift + 1] * dot(picks_ref[shift, :, :CAP], reads)
        partial[side] = total


def mix_near(gates, picks, own, other):
    out = near((2, ROWS, HALF), F32)
    return kernel_call(mix_near_kernel, "mix_near", out, (), 12, gates, picks, *own, *other)


def mix_kernel(gates_ref, picks_ref, gain_ref, partial, own, other, out_ref):
    core = lax.axis_index("dp")
    for side, reads in enumerate((own, other)):
        start = (core ^ side) * HALF
        far = dot(picks_ref[FAR, :, :CAP], reads[core])
        mixture = partial[side] + gates_ref[:, FAR : FAR + 1] * far
        for head in range(HEADS):
            columns = pl.ds(pl.multiple_of(start + head * HEAD_DIM, HEAD_DIM), HEAD_DIM)
            mix = mixture[:, head_columns(head)]
            scale = lax.rsqrt(jnp.mean(mix * mix, axis=1, keepdims=True) + 1e-05)
            out_ref[:, columns] = (mix * scale * gain_ref[:, columns]).astype(BF16)


def mix_reads(gates, picks, gain, partial, own, other):
    out = jax.ShapeDtypeStruct((ROWS, 2 * HALF), BF16)
    return kernel_call(
        mix_kernel, "mix_reads", out, (), 12, gates, picks, gain, partial, own, other
    )


def after(array, *first):
    return lax.optimization_barrier((array, *first))[0]


def hop(array, shift):
    return lax.ppermute(array, "memory", [(i, i ^ shift) for i in range(OWNERS)])


def exchange(arrays, stride):
    out = [arrays[0]]
    for shift in (1, 2, 3):
        pairs = [(i, i ^ shift * stride) for i in range(RING * RING)]
        out.append(lax.ppermute(arrays[shift], "context", pairs))
    return out


def swap(array):
    return lax.ppermute(array, "dp", [(0, 1), (1, 0)])


def shards(
    hidden,
    queries,
    route_ids,
    router_weight,
    key_weight,
    value_weight,
    decay_weight,
    decay_bias,
    norm_gain,
):
    rows, query_rows, route = hidden[0], queries[0], route_ids[0].T
    weights = (key_weight[0], value_weight[0], decay_weight[0].T, decay_bias)

    packed = pack_rows(route, rows)
    arrived = {0: packed[0]}
    for shift in (1, 3):
        arrived[shift] = hop(packed[shift], shift)
    other = {0: swap(packed[0])}
    other_route, other_query = swap(route), swap(query_rows)
    first = project([arrived[0], other[0]], *weights, first=True)
    weights = (first[3], first[4], *weights[2:])
    packed_query = pack_queries(
        after(route, first[2]), other_route, query_rows, other_query, rows, router_weight.T
    )
    gates, picks = packed_query[OWNERS:]
    for shift in (1, 3):
        arrived[shift] = after(arrived[shift], gates)
    arrived[2] = hop(after(packed[2], arrived[1], arrived[3]), 2)
    for shift in (1, 3):
        other[shift] = swap(arrived[shift])
    second = project([arrived[1], other[1], arrived[3], other[3]], *weights)
    arrived[2] = after(arrived[2], second[2])
    other[2] = swap(arrived[2])
    query_in = {0: packed_query[0]}
    for shift in (1, 3):
        query_in[shift] = hop(after(packed_query[shift], arrived[2]), shift)
    third = project([arrived[2], other[2]], *weights)
    units, values, decays = zip(first[:3], second, third)

    *messages, column, row, units, values = block_state(units, values, decays)
    pieces = exchange(messages, 1)
    blocks = (units, values, column, row)
    inner_near = inner_reads(NEAR, *blocks, *[query_in[shift] for shift in NEAR])
    pieces[0] = after(pieces[0], inner_near)
    whole, before, faded = row_prefix(pieces)
    query_in[FAR] = hop(after(packed_query[FAR], whole), FAR)
    totals = exchange([whole] * RING, RING)
    entry = exchange(entry_states(totals, before, faded), 1)
    inner_far = inner_reads((FAR,), *blocks, query_in[FAR])
    queries = [query_in[shift] for shift in range(OWNERS)]
    reads = read_out(queries, inner_near, inner_far, column, entry)

    own = [reads[0]] + [hop(reads[shift], shift) for shift in (1, 2, 3)]
    paired = [swap(part) for part in own]
    partial = mix_near(gates, picks, [own[i] for i in NEAR], [paired[i] for i in NEAR])
    return mix_reads(gates, picks, norm_gain[None], partial, own[FAR], paired[FAR])[None]


def solution(mesh):
    in_specs = (
        P(("context", "dp"), "memory", None),
        P(("context", "dp"), "memory", None),
        P(("context", "dp"), "memory", None),
        P(),
        P("memory", None, "dp"),
        P("memory", None, "dp"),
        P("memory", None, "dp"),
        P("memory", "dp"),
        P(),
    )
    out_specs = P(("context", "dp"), "memory", None)
    return jax.shard_map(shards, mesh=mesh, in_specs=in_specs, out_specs=out_specs, check_vma=False)
```

```python
import functools

import jax
import jax.numpy as jnp
from jax import lax
from jax.experimental import pallas as pl
from jax.experimental.pallas import tpu as pltpu
from jax.sharding import PartitionSpec as P

D = 4096
HEAD_DIM = 128
CAP = 80
ROWS = 128
OWNERS = 4
CHUNKS = 8
SLOTS = CHUNKS * CAP
HALF = 1024
HEADS = HALF // HEAD_DIM
EMPTY = 64.0
PAD = 128
PACKS = 4
NEAR, FAR = (0, 1, 3), 2
AWAY = (1, 3, 2)
RING = 4
PIECE = HALF // RING
TAIL = 16
F32 = jnp.float32
BF16 = jnp.bfloat16
MIB = 1 << 20


def iota(shape, axis):
    return lax.broadcasted_iota(jnp.int32, shape, axis)


def dot(a, b):
    return jnp.dot(a, b, preferred_element_type=F32)


def dot_rows(a, b):
    return lax.dot_general(a, b, (((1,), (1,)), ((), ())), preferred_element_type=F32)


def dot_columns(a, b):
    return lax.dot_general(a, b, (((0,), (0,)), ((), ())), preferred_element_type=F32)


def near(shape, dtype):
    return pltpu.VMEM(shape, dtype)


def position(shift, partner, owner, core):
    return (core ^ partner) * OWNERS + (owner ^ shift)


def membership(route):
    memory = iota((8, ROWS), 0)
    named = ((route[0:1] == memory) | (route[1:2] == memory)).astype(F32)
    before = (iota((ROWS, ROWS), 0) < iota((ROWS, ROWS), 1)).astype(F32).astype(BF16)
    slot = dot(named.astype(BF16), before)
    return named, jnp.where(named > 0.0, slot, -1.0)


def one_hot(place, memory, slots=CAP):
    mine = jnp.sum(jnp.where(iota(place.shape, 0) == memory, place, 0.0), axis=0, keepdims=True)
    return (iota((slots, ROWS), 0).astype(F32) == mine).astype(F32)


def kernel_call(kernel, name, out_shape, scratch, limit, *operands, hbm=(), moved=1):
    spaces = [pltpu.HBM if at in hbm else pltpu.VMEM for at in range(len(operands))]
    return pl.pallas_call(
        kernel,
        out_shape=out_shape,
        in_specs=[pl.BlockSpec(memory_space=space) for space in spaces],
        out_specs=jax.tree.map(lambda _: pl.BlockSpec(memory_space=pltpu.VMEM), out_shape),
        scratch_shapes=scratch,
        compiler_params=pltpu.CompilerParams(vmem_limit_bytes=limit * MIB),
        cost_estimate=pl.CostEstimate(flops=1, bytes_accessed=moved, transcendentals=0),
        name=name,
    )(*operands)


def select_columns(pick, rows_ref, columns, out_refs):
    part = dot(pick.astype(BF16), rows_ref[:, columns])
    if columns.start == 0:
        empty = jnp.sum(pick, axis=1, keepdims=True) == 0.0
        first_lane = iota((part.shape[0], HEAD_DIM), 1) == 0
        marked = jnp.where(first_lane & empty, EMPTY, part[:, :HEAD_DIM])
        part = jnp.concatenate([marked, part[:, HEAD_DIM:]], axis=1)
    part = part.astype(BF16)
    for to, out_ref in enumerate(out_refs):
        out_ref[:, columns] = part[to * CAP : (to + 1) * CAP]


def pack_rows_kernel(route_hbm, rows_hbm, *refs):
    out_refs, (route_ref, rows_ref, sems) = refs[: len(AWAY)], refs[len(AWAY) :]
    owner = lax.axis_index("memory")
    width = D // PACKS
    route_copy = pltpu.make_async_copy(route_hbm, route_ref, sems.at[PACKS])
    route_copy.start()
    parts, copies = [slice(at * width, (at + 1) * width) for at in range(PACKS)], []
    for at, columns in enumerate(parts):
        copies.append(
            pltpu.make_async_copy(rows_hbm.at[:, columns], rows_ref.at[:, columns], sems.at[at])
        )
        copies[at].start()
    route_copy.wait()
    place = membership(route_ref[...])[1]
    pick = jnp.concatenate([one_hot(place, owner ^ shift) for shift in AWAY], axis=0)
    for copy, columns in zip(copies, parts):
        copy.wait()
        select_columns(pick, rows_ref, columns, out_refs)
    out_refs[AWAY.index(FAR)][:, D:] = jnp.zeros((CAP, PAD), BF16)


def pack_rows(route, rows):
    out = [near((CAP, D + PAD * (shift == FAR)), BF16) for shift in AWAY]
    scratch = [
        pltpu.VMEM((2, ROWS), jnp.int32),
        pltpu.VMEM((ROWS, D), BF16),
        pltpu.SemaphoreType.DMA((PACKS + 1,)),
    ]
    return kernel_call(pack_rows_kernel, "pack_rows", out, scratch, 56, route, rows, hbm=(0, 1))


def pack_queries_kernel(
    route_ref, other_route_ref, query_ref, other_query_ref, rows_ref, router_ref, *out_refs
):
    owner, core = lax.axis_index("memory"), lax.axis_index("dp")
    gates_ref, picks_ref = out_refs[OWNERS:]
    mine = pl.multiple_of(core * HALF, HALF)
    for side, (routes, queries) in enumerate(
        ((route_ref, query_ref), (other_route_ref, other_query_ref))
    ):
        named, place = membership(routes[...])
        pick = jnp.concatenate(
            [one_hot(place, owner ^ shift) for shift in range(OWNERS)], axis=0
        ).astype(BF16)
        part = dot(pick, queries[:, pl.ds(mine, HALF)]).astype(BF16)
        for shift in range(OWNERS):
            out_refs[shift][core ^ side] = part[shift * CAP : (shift + 1) * CAP]
        if side == 0:
            for shift in range(OWNERS):
                picks_ref[shift] = one_hot(place, owner ^ shift, 128).T.astype(BF16)
            score = dot_rows(router_ref[...], rows_ref[...])
            chosen = jax.nn.sigmoid(score) * named[:OWNERS]
            gates = chosen / jnp.sum(chosen, axis=0, keepdims=True)
            memory = iota((OWNERS, ROWS), 0)
            by_shift = [
                jnp.sum(jnp.where(memory == owner ^ shift, gates, 0.0), axis=0, keepdims=True)
                for shift in range(OWNERS)
            ]
            by_shift.append(jnp.zeros((128 - OWNERS, ROWS), F32))
            gates_ref[...] = jnp.concatenate(by_shift, axis=0).T


def pack_queries(route, other_route, queries, other_queries, rows, router_weight):
    out = [near((2, CAP, HALF), BF16)] * OWNERS
    out = out + [near((ROWS, 128), F32), near((OWNERS, ROWS, 128), BF16)]
    operands = (route, other_route, queries, other_queries, rows, router_weight)
    return kernel_call(
        pack_queries_kernel, "pack_queries", out, (), 12, *operands, moved=4 * MIB
    )


def log_sigmoid(x):
    small = jnp.exp(-jnp.abs(x))
    near = 1.0 + small
    tiny = near == 1.0
    log1p = jnp.where(tiny, small, jnp.log(near) * (small / jnp.where(tiny, 1.0, near - 1.0)))
    return jnp.minimum(x, 0.0) - log1p


WIDTH = 512


def project_parts(row_refs, decay_ref, bias_ref, outs, key_ref, value_ref, held, ready):
    count = len(row_refs)
    unit_out, value_out, decay_out = outs
    lives = []
    for at in range(count):
        rows = slice(at * CAP, (at + 1) * CAP)
        head = row_refs[at][:, :HEAD_DIM].astype(F32)
        lives.append(head[:, :1] < EMPTY / 2)
        held[rows, :HEAD_DIM] = jnp.where(lives[at], head, 0.0).astype(BF16)
        held[rows, HEAD_DIM:] = row_refs[at][:, HEAD_DIM:D]
    decay = log_sigmoid(dot_rows(held[...], decay_ref[...]) + bias_ref[...])
    upto = (iota((CAP, CAP), 0) >= iota((CAP, CAP), 1)).astype(F32).astype(BF16)
    for at in range(count):
        kept = jnp.where(lives[at], decay[at * CAP : (at + 1) * CAP], 0.0)
        kept = jnp.concatenate([kept, jnp.zeros((CAP, 128 - HEADS), F32)], axis=1)
        total = jnp.zeros((CAP, 128), F32)
        for _ in range(3):
            part = kept.astype(BF16)
            kept = kept - part.astype(F32)
            total = total + dot(upto, part)
        decay_out[at] = total
    for start in range(0, HALF, WIDTH):
        ready(start // WIDTH)
        columns = slice(start, start + WIDTH)
        keys = dot(held[...], key_ref[:, columns]).astype(BF16).astype(F32)
        for head in range(0, WIDTH, HEAD_DIM):
            key = keys[:, head : head + HEAD_DIM]
            unit = key * lax.rsqrt(jnp.sum(key * key, axis=1, keepdims=True) + 1e-06)
            unit_out[:, :, start + head : start + head + HEAD_DIM] = unit.astype(BF16).reshape(
                count, CAP, HEAD_DIM
            )
        values = dot(held[...], value_ref[:, columns]).astype(BF16)
        value_out[:, :, columns] = values.reshape(count, CAP, WIDTH)


def project_first_kernel(*refs):
    route_ref, rows_ref, key_hbm, value_hbm, decay_ref, bias_ref = refs[:6]
    outs, (key_ref, value_ref, packed, held, sems) = refs[6:9], refs[9:]
    copies = []
    for at, start in enumerate(range(0, HALF, WIDTH)):
        columns = slice(start, start + WIDTH)
        for side, (far, close) in enumerate(((key_hbm, key_ref), (value_hbm, value_ref))):
            copies.append(
                pltpu.make_async_copy(far.at[:, columns], close.at[:, columns], sems.at[side, at])
            )
    for copy in copies:
        copy.start()
    pick = one_hot(membership(route_ref[...])[1], lax.axis_index("memory"))
    for start in range(0, D, WIDTH):
        select_columns(pick, rows_ref, slice(start, start + WIDTH), [packed])

    def ready(at):
        copies[2 * at].wait()
        copies[2 * at + 1].wait()

    project_parts([packed], decay_ref, bias_ref, outs, key_ref, value_ref, held, ready)


def project_next_kernel(count, *refs):
    key_ref, value_ref, decay_ref, bias_ref = refs[count : count + 4]
    outs, held = refs[count + 4 : count + 7], refs[count + 7]
    project_parts(
        refs[:count], decay_ref, bias_ref, outs, key_ref, value_ref, held, lambda at: None
    )


def projected(count):
    out = [near((count, CAP, HALF), BF16)] * 2 + [near((count, CAP, 128), F32)]
    return out, [pltpu.VMEM((count * CAP, D), BF16)]


def project_first(route, rows, *weights):
    out, scratch = projected(1)
    out = out + [near((D, HALF), BF16)] * 2 + [near((CAP, D), BF16)]
    scratch = scratch + [pltpu.SemaphoreType.DMA((2, HALF // WIDTH))]
    operands = (route, rows, *weights)
    return kernel_call(project_first_kernel, "project_first", out, scratch, 40, *operands, hbm=(2, 3))


def project(row_parts, *weights):
    count = len(row_parts)
    out, scratch = projected(count)
    kernel = functools.partial(project_next_kernel, count)
    return kernel_call(kernel, f"project_{count}", out, scratch, 12, *row_parts, *weights)


GROUPS = (((0, 0),), ((0, 1), (1, 0), (1, 1), (3, 0), (3, 1)), ((2, 0), (2, 1)))


def token_order(refs, held):
    owner, core = lax.axis_index("memory"), lax.axis_index("dp")
    for group, ref in zip(GROUPS, refs):
        for at, (shift, partner) in enumerate(group):
            held[position(shift, partner, owner, core)] = ref[at]


def head_columns(head):
    return slice(head * HEAD_DIM, (head + 1) * HEAD_DIM)


def place_in_context():
    context = lax.axis_index("context")
    return context >> 2, context & (RING - 1)


def two_parts(number):
    wide = jnp.broadcast_to(number, (TAIL, 128))
    high = wide.astype(BF16).astype(F32)
    return jnp.where(iota((TAIL, 128), 0) < TAIL // 2, high, wide - high).astype(BF16)


def from_parts(rows):
    return rows[:1].astype(F32) + rows[TAIL // 2 : TAIL // 2 + 1].astype(F32)


def state_kernel(*refs):
    unit_refs, value_refs, decay_refs = refs[0:3], refs[3:6], refs[6:9]
    messages = refs[9:13]
    column_out, row_out, units, values, decays, quarters = refs[13:]
    token_order(decay_refs, decays)
    offset, chunks = jnp.zeros((1, 128), F32), []
    for chunk in range(CHUNKS):
        chunks.append(decays[chunk] + offset)
        offset = chunks[chunk][CAP - 1 :]
    running = jnp.concatenate(chunks, axis=0)
    column_out[...] = running.reshape(CHUNKS, CAP, 128)
    row_out[...] = running.T[:HEADS]
    token_order(unit_refs, units)
    token_order(value_refs, values)
    last = running[SLOTS - 1 : SLOTS]
    fade = jnp.exp(last - running)
    for head in range(HEADS):
        unit = units[:, :, head_columns(head)].reshape(SLOTS, HEAD_DIM).astype(F32)
        faded = (unit * fade[:, head : head + 1]).astype(BF16)
        value = values[:, :, head_columns(head)].reshape(SLOTS, HEAD_DIM)
        state = dot_columns(faded, value).astype(BF16)
        at = head % 2 * HEAD_DIM
        quarters[head // 2, at : at + HEAD_DIM] = state
        tail = PIECE + head % 2 * TAIL
        quarters[head // 2, tail : tail + TAIL] = two_parts(last[:, head : head + 1])
    _, column = place_in_context()
    for shift in range(RING):
        messages[shift][...] = quarters[column ^ shift]


def block_state(units, values, decays):
    out = [near((PIECE + 2 * TAIL, 128), BF16)] * RING + [
        near((CHUNKS, CAP, 128), F32),
        near((HEADS, SLOTS), F32),
        near((CHUNKS, CAP, HALF), BF16),
        near((CHUNKS, CAP, HALF), BF16),
    ]
    scratch = [
        pltpu.VMEM((CHUNKS, CAP, 128), F32),
        pltpu.VMEM((RING, PIECE + 2 * TAIL, 128), BF16),
    ]
    return kernel_call(
        state_kernel, "block_state", out, scratch, 12, *units, *values, *decays
    )


def ring_order(refs, held, me):
    for shift in range(RING):
        held[me ^ shift] = refs[shift][...]


def row_prefix_kernel(*refs):
    pieces, (whole, before, faded, held) = refs[:RING], refs[RING:]
    ring_order(pieces, held, place_in_context()[1])
    for head in range(2):
        rows = slice(head * HEAD_DIM, (head + 1) * HEAD_DIM)
        tail = slice(PIECE + head * TAIL, PIECE + (head + 1) * TAIL)
        state, total = jnp.zeros((HEAD_DIM, 128), F32), jnp.zeros((1, 128), F32)
        for column in range(RING):
            before[column, rows] = state
            faded[column, head * 8 : head * 8 + 8] = jnp.broadcast_to(jnp.exp(total), (8, 128))
            ended = from_parts(held[column, tail])
            state = jnp.exp(ended) * state + held[column, rows].astype(F32)
            total = total + ended
        whole[rows] = state.astype(BF16)
        whole[tail] = two_parts(total)


def row_prefix(pieces):
    out = [
        near((PIECE + 2 * TAIL, 128), BF16),
        near((RING, PIECE, 128), F32),
        near((RING, 16, 128), F32),
    ]
    scratch = [pltpu.VMEM((RING, PIECE + 2 * TAIL, 128), BF16)]
    return kernel_call(row_prefix_kernel, "row_prefix", out, scratch, 8, *pieces)


def entry_kernel(*refs):
    pieces, (before, faded) = refs[:RING], refs[RING : RING + 2]
    out_refs, (held, entries) = refs[RING + 2 : 2 * RING + 2], refs[2 * RING + 2 :]
    row, mine = place_in_context()
    ring_order(pieces, held, row)
    for head in range(2):
        rows = slice(head * HEAD_DIM, (head + 1) * HEAD_DIM)
        tail = slice(PIECE + head * TAIL, PIECE + (head + 1) * TAIL)
        state = jnp.zeros((HEAD_DIM, 128), F32)
        for earlier in range(RING - 1):
            kept = jnp.exp(from_parts(held[earlier, tail])) * state
            kept = kept + held[earlier, rows].astype(F32)
            state = jnp.where(earlier < row, kept, state)
        for column in range(RING):
            fade = faded[column, head * 8 : head * 8 + 1]
            entries[column, rows] = (before[column, rows] + fade * state).astype(BF16)
    for shift in range(RING):
        out_refs[shift][...] = entries[mine ^ shift]


def entry_states(pieces, before, faded):
    out = [near((PIECE, 128), BF16)] * RING
    scratch = [
        pltpu.VMEM((RING, PIECE + 2 * TAIL, 128), BF16),
        pltpu.VMEM((RING, PIECE, 128), BF16),
    ]
    return kernel_call(entry_kernel, "entry_states", out, scratch, 8, *pieces, before, faded)


def inner_kernel(shifts, *refs):
    units, values, column_ref, row_ref = refs[0:4]
    query_refs, inner = refs[4:-1], refs[-1]
    owner = lax.axis_index("memory")
    count = len(shifts) * CAP
    for core in range(2):
        reach = -(-(core + 1) * OWNERS * CAP // 128) * 128
        chunks = [core * OWNERS + (owner ^ shift) for shift in shifts]
        running = jnp.concatenate([column_ref[chunk] for chunk in chunks], axis=0)
        place = jnp.concatenate([iota((CAP, reach), 0) + chunk * CAP for chunk in chunks], axis=0)
        causal = place >= iota((count, reach), 1)
        for head in range(HEADS):
            columns = head_columns(head)
            query = jnp.concatenate([query[core, :, columns] for query in query_refs], axis=0)
            unit = units[:, :, columns].reshape(SLOTS, HEAD_DIM)[:reach]
            value = values[:, :, columns].reshape(SLOTS, HEAD_DIM)[:reach]
            spread = running[:, head : head + 1] - row_ref[head : head + 1, :reach]
            weight = jnp.exp(jnp.where(causal, spread, -1e30))
            score = (dot_rows(query, unit) * weight).astype(BF16)
            inner[:, core, :, columns] = dot(score, value).reshape(len(shifts), CAP, HEAD_DIM)


def inner_reads(shifts, units, values, column, row, *queries):
    out = near((len(shifts), 2, CAP, HALF), F32)
    kernel = functools.partial(inner_kernel, shifts)
    name = f"inner_reads_{len(shifts)}"
    return kernel_call(kernel, name, out, (), 16, units, values, column, row, *queries)


def read_kernel(*refs):
    query_refs, inner_near, inner_far, column_ref = refs[0:4], refs[4], refs[5], refs[6]
    out_refs, entries = refs[11:15], refs[15]
    ring_order(refs[7:11], entries, place_in_context()[1])
    owner = lax.axis_index("memory")
    inners = {shift: inner_near.at[at] for at, shift in enumerate(NEAR)}
    inners[FAR] = inner_far.at[0]
    pairs = [(shift, core) for shift in range(OWNERS) for core in range(2)]
    fade = jnp.concatenate([column_ref[c * OWNERS + (owner ^ s)] for s, c in pairs], axis=0)
    fade = jnp.exp(fade)
    for head in range(HEADS):
        columns = head_columns(head)
        query = jnp.concatenate([query_refs[s][c, :, columns] for s, c in pairs], axis=0)
        entry = entries[head // 2, head % 2 * HEAD_DIM : (head % 2 + 1) * HEAD_DIM]
        carried = fade[:, head : head + 1] * dot(query, entry)
        for at, (s, c) in enumerate(pairs):
            read = inners[s][c, :, columns] + carried[at * CAP : (at + 1) * CAP]
            out_refs[s][c, :, columns] = read.astype(BF16)


def read_out(queries, inner_near, inner_far, column, entry):
    out = [near((2, CAP, HALF), BF16)] * OWNERS
    scratch = [pltpu.VMEM((RING, PIECE, 128), BF16)]
    operands = (*queries, inner_near, inner_far, column, *entry)
    return kernel_call(read_kernel, "read_out", out, scratch, 12, *operands)


def mix_near_kernel(gates_ref, picks_ref, *refs):
    partial = refs[-1]
    core = lax.axis_index("dp")
    for side in range(2):
        total = jnp.zeros((ROWS, HALF), F32)
        for at, shift in enumerate(NEAR):
            reads = refs[side * len(NEAR) + at][core]
            total = total + gates_ref[:, shift : shift + 1] * dot(picks_ref[shift, :, :CAP], reads)
        partial[side] = total


def mix_near(gates, picks, own, other):
    out = near((2, ROWS, HALF), F32)
    return kernel_call(mix_near_kernel, "mix_near", out, (), 12, gates, picks, *own, *other)


def mix_kernel(gates_ref, picks_ref, gain_ref, partial, own, other, out_ref):
    core = lax.axis_index("dp")
    for side, reads in enumerate((own, other)):
        start = (core ^ side) * HALF
        far = dot(picks_ref[FAR, :, :CAP], reads[core])
        mixture = partial[side] + gates_ref[:, FAR : FAR + 1] * far
        for head in range(HEADS):
            columns = pl.ds(pl.multiple_of(start + head * HEAD_DIM, HEAD_DIM), HEAD_DIM)
            mix = mixture[:, head_columns(head)]
            scale = lax.rsqrt(jnp.mean(mix * mix, axis=1, keepdims=True) + 1e-05)
            out_ref[:, columns] = (mix * scale * gain_ref[:, columns]).astype(BF16)


def mix_reads(gates, picks, gain, partial, own, other):
    out = jax.ShapeDtypeStruct((ROWS, 2 * HALF), BF16)
    return kernel_call(
        mix_kernel, "mix_reads", out, (), 12, gates, picks, gain, partial, own, other
    )


def after(array, *first):
    return lax.optimization_barrier((array, *first))[0]


def hop(array, shift):
    return lax.ppermute(array, "memory", [(i, i ^ shift) for i in range(OWNERS)])


def exchange(arrays, stride):
    out = [arrays[0]]
    for shift in (1, 2, 3):
        pairs = [(i, i ^ shift * stride) for i in range(RING * RING)]
        out.append(lax.ppermute(arrays[shift], "context", pairs))
    return out


def swap(array):
    return lax.ppermute(array, "dp", [(0, 1), (1, 0)])


def shards(
    hidden,
    queries,
    route_ids,
    router_weight,
    key_weight,
    value_weight,
    decay_weight,
    decay_bias,
    norm_gain,
):
    rows, query_rows, route = hidden[0], queries[0], route_ids[0].T
    weights = (key_weight[0], value_weight[0], decay_weight[0].T, decay_bias)

    packed = dict(zip(AWAY, pack_rows(route, rows)))
    arrived = {shift: hop(packed[shift], shift) for shift in (1, 3)}
    other_route, other_query = swap(route), swap(query_rows)
    first = project_first(route, rows, *weights)
    other = {0: swap(first[5])}
    weights = (first[3], first[4], *weights[2:])
    packed_query = pack_queries(
        after(route, first[2]), other_route, query_rows, other_query, rows, router_weight.T
    )
    gates, picks = packed_query[OWNERS:]
    for shift in (1, 3):
        arrived[shift] = after(arrived[shift], gates)
    arrived[2] = hop(after(packed[2], arrived[1], arrived[3]), 2)
    for shift in (1, 3):
        other[shift] = swap(arrived[shift])
    near_rows = [other[0], arrived[1], other[1], arrived[3], other[3]]
    second = project(near_rows, *weights)
    arrived[2] = after(arrived[2], second[2])
    other[2] = swap(arrived[2])
    query_in = {0: packed_query[0]}
    for shift in (1, 3):
        query_in[shift] = hop(after(packed_query[shift], arrived[2]), shift)
    third = project([arrived[2], other[2]], *weights)
    units, values, decays = zip(first[:3], second, third)

    *messages, column, row, units, values = block_state(units, values, decays)
    pieces = exchange(messages, 1)
    blocks = (units, values, column, row)
    inner_near = inner_reads(NEAR, *blocks, *[query_in[shift] for shift in NEAR])
    pieces[0] = after(pieces[0], inner_near)
    whole, before, faded = row_prefix(pieces)
    query_in[FAR] = hop(after(packed_query[FAR], whole), FAR)
    totals = exchange([whole] * RING, RING)
    entry = exchange(entry_states(totals, before, faded), 1)
    inner_far = inner_reads((FAR,), *blocks, query_in[FAR])
    queries = [query_in[shift] for shift in range(OWNERS)]
    reads = read_out(queries, inner_near, inner_far, column, entry)

    own = [reads[0]] + [hop(reads[shift], shift) for shift in (1, 2, 3)]
    paired = [swap(part) for part in own]
    partial = mix_near(gates, picks, [own[i] for i in NEAR], [paired[i] for i in NEAR])
    return mix_reads(gates, picks, norm_gain[None], partial, own[FAR], paired[FAR])[None]


def solution(mesh):
    in_specs = (
        P(("context", "dp"), "memory", None),
        P(("context", "dp"), "memory", None),
        P(("context", "dp"), "memory", None),
        P(),
        P("memory", None, "dp"),
        P("memory", None, "dp"),
        P("memory", None, "dp"),
        P("memory", "dp"),
        P(),
    )
    out_specs = P(("context", "dp"), "memory", None)
    return jax.shard_map(shards, mesh=mesh, in_specs=in_specs, out_specs=out_specs, check_vma=False)
```

```python
import functools

import jax
import jax.numpy as jnp
from jax import lax
from jax.experimental import pallas as pl
from jax.experimental.pallas import tpu as pltpu
from jax.sharding import PartitionSpec as P

D = 4096
HEAD_DIM = 128
CAP = 80
ROWS = 128
OWNERS = 4
CHUNKS = 8
SLOTS = CHUNKS * CAP
HALF = 1024
HEADS = HALF // HEAD_DIM
EMPTY = 64.0
PAD = 128
PACKS = 4
NEAR, FAR = (0, 1, 3), 2
AWAY = (1, 3, 2)
RING = 4
PIECE = HALF // RING
TAIL = 16
F32 = jnp.float32
BF16 = jnp.bfloat16
MIB = 1 << 20


def iota(shape, axis):
    return lax.broadcasted_iota(jnp.int32, shape, axis)


def dot(a, b):
    return jnp.dot(a, b, preferred_element_type=F32)


def dot_rows(a, b):
    return lax.dot_general(a, b, (((1,), (1,)), ((), ())), preferred_element_type=F32)


def dot_columns(a, b):
    return lax.dot_general(a, b, (((0,), (0,)), ((), ())), preferred_element_type=F32)


def near(shape, dtype):
    return pltpu.VMEM(shape, dtype)


def position(shift, partner, owner, core):
    return (core ^ partner) * OWNERS + (owner ^ shift)


def membership(route):
    memory = iota((8, ROWS), 0)
    named = ((route[0:1] == memory) | (route[1:2] == memory)).astype(F32)
    before = (iota((ROWS, ROWS), 0) < iota((ROWS, ROWS), 1)).astype(F32).astype(BF16)
    slot = dot(named.astype(BF16), before)
    return named, jnp.where(named > 0.0, slot, -1.0)


def one_hot(place, memory, slots=CAP):
    mine = jnp.sum(jnp.where(iota(place.shape, 0) == memory, place, 0.0), axis=0, keepdims=True)
    return (iota((slots, ROWS), 0).astype(F32) == mine).astype(F32)


def kernel_call(kernel, name, out_shape, scratch, limit, *operands, hbm=(), moved=1):
    spaces = [pltpu.HBM if at in hbm else pltpu.VMEM for at in range(len(operands))]
    return pl.pallas_call(
        kernel,
        out_shape=out_shape,
        in_specs=[pl.BlockSpec(memory_space=space) for space in spaces],
        out_specs=jax.tree.map(lambda _: pl.BlockSpec(memory_space=pltpu.VMEM), out_shape),
        scratch_shapes=scratch,
        compiler_params=pltpu.CompilerParams(vmem_limit_bytes=limit * MIB),
        cost_estimate=pl.CostEstimate(flops=1, bytes_accessed=moved, transcendentals=0),
        name=name,
    )(*operands)


def select_columns(pick, rows_ref, columns, out_refs):
    part = dot(pick.astype(BF16), rows_ref[:, columns])
    if columns.start == 0:
        empty = jnp.sum(pick, axis=1, keepdims=True) == 0.0
        first_lane = iota((part.shape[0], HEAD_DIM), 1) == 0
        marked = jnp.where(first_lane & empty, EMPTY, part[:, :HEAD_DIM])
        part = jnp.concatenate([marked, part[:, HEAD_DIM:]], axis=1)
    part = part.astype(BF16)
    for to, out_ref in enumerate(out_refs):
        out_ref[:, columns] = part[to * CAP : (to + 1) * CAP]


def pack_rows_kernel(route_hbm, rows_hbm, *refs):
    out_refs, (route_ref, rows_ref, sems) = refs[: len(AWAY)], refs[len(AWAY) :]
    owner = lax.axis_index("memory")
    width = D // PACKS
    route_copy = pltpu.make_async_copy(route_hbm, route_ref, sems.at[PACKS])
    route_copy.start()
    parts, copies = [slice(at * width, (at + 1) * width) for at in range(PACKS)], []
    for at, columns in enumerate(parts):
        copies.append(
            pltpu.make_async_copy(rows_hbm.at[:, columns], rows_ref.at[:, columns], sems.at[at])
        )
        copies[at].start()
    route_copy.wait()
    place = membership(route_ref[...])[1]
    pick = jnp.concatenate([one_hot(place, owner ^ shift) for shift in AWAY], axis=0)
    for copy, columns in zip(copies, parts):
        copy.wait()
        select_columns(pick, rows_ref, columns, out_refs)
    out_refs[AWAY.index(FAR)][:, D:] = jnp.zeros((CAP, PAD), BF16)


def pack_rows(route, rows):
    out = [near((CAP, D + PAD * (shift == FAR)), BF16) for shift in AWAY]
    scratch = [
        pltpu.VMEM((2, ROWS), jnp.int32),
        pltpu.VMEM((ROWS, D), BF16),
        pltpu.SemaphoreType.DMA((PACKS + 1,)),
    ]
    return kernel_call(pack_rows_kernel, "pack_rows", out, scratch, 56, route, rows, hbm=(0, 1))


def pack_queries_kernel(
    route_ref, other_route_ref, query_ref, other_query_ref, rows_ref, router_ref, *out_refs
):
    owner, core = lax.axis_index("memory"), lax.axis_index("dp")
    gates_ref, picks_ref = out_refs[OWNERS:]
    mine = pl.multiple_of(core * HALF, HALF)
    for side, (routes, queries) in enumerate(
        ((route_ref, query_ref), (other_route_ref, other_query_ref))
    ):
        named, place = membership(routes[...])
        pick = jnp.concatenate(
            [one_hot(place, owner ^ shift) for shift in range(OWNERS)], axis=0
        ).astype(BF16)
        part = dot(pick, queries[:, pl.ds(mine, HALF)]).astype(BF16)
        for shift in range(OWNERS):
            out_refs[shift][core ^ side] = part[shift * CAP : (shift + 1) * CAP]
        if side == 0:
            for shift in range(OWNERS):
                picks_ref[shift] = one_hot(place, owner ^ shift, 128).T.astype(BF16)
            score = dot_rows(router_ref[...], rows_ref[...])
            chosen = jax.nn.sigmoid(score) * named[:OWNERS]
            gates = chosen / jnp.sum(chosen, axis=0, keepdims=True)
            memory = iota((OWNERS, ROWS), 0)
            by_shift = [
                jnp.sum(jnp.where(memory == owner ^ shift, gates, 0.0), axis=0, keepdims=True)
                for shift in range(OWNERS)
            ]
            by_shift.append(jnp.zeros((128 - OWNERS, ROWS), F32))
            gates_ref[...] = jnp.concatenate(by_shift, axis=0).T


def pack_queries(route, other_route, queries, other_queries, rows, router_weight):
    out = [near((2, CAP, HALF), BF16)] * OWNERS
    out = out + [near((ROWS, 128), F32), near((OWNERS, ROWS, 128), BF16)]
    operands = (route, other_route, queries, other_queries, rows, router_weight)
    return kernel_call(
        pack_queries_kernel, "pack_queries", out, (), 12, *operands, moved=4 * MIB
    )


def log_sigmoid(x):
    small = jnp.exp(-jnp.abs(x))
    near = 1.0 + small
    tiny = near == 1.0
    log1p = jnp.where(tiny, small, jnp.log(near) * (small / jnp.where(tiny, 1.0, near - 1.0)))
    return jnp.minimum(x, 0.0) - log1p


WIDTH = 512
LONGEST = -128.0


def project_parts(row_refs, decay_ref, bias_ref, outs, key_ref, value_ref, held, ready):
    count = len(row_refs)
    unit_out, value_out, decay_out = outs
    lives = []
    for at in range(count):
        rows = slice(at * CAP, (at + 1) * CAP)
        head = row_refs[at][:, :HEAD_DIM].astype(F32)
        lives.append(head[:, :1] < EMPTY / 2)
        held[rows, :HEAD_DIM] = jnp.where(lives[at], head, 0.0).astype(BF16)
        held[rows, HEAD_DIM:] = row_refs[at][:, HEAD_DIM:D]
    decay = log_sigmoid(dot_rows(held[...], decay_ref[...]) + bias_ref[...])
    upto = (iota((CAP, CAP), 0) >= iota((CAP, CAP), 1)).astype(F32).astype(BF16)
    for at in range(count):
        kept = jnp.maximum(decay[at * CAP : (at + 1) * CAP], LONGEST)
        kept = jnp.where(lives[at], kept, 0.0)
        kept = jnp.concatenate([kept, jnp.zeros((CAP, 128 - HEADS), F32)], axis=1)
        total = jnp.zeros((CAP, 128), F32)
        for _ in range(3):
            part = kept.astype(BF16)
            kept = kept - part.astype(F32)
            total = total + dot(upto, part)
        decay_out[at] = total
    for start in range(0, HALF, WIDTH):
        ready(start // WIDTH)
        columns = slice(start, start + WIDTH)
        keys = dot(held[...], key_ref[:, columns]).astype(BF16).astype(F32)
        for head in range(0, WIDTH, HEAD_DIM):
            key = keys[:, head : head + HEAD_DIM]
            unit = key * lax.rsqrt(jnp.sum(key * key, axis=1, keepdims=True) + 1e-06)
            unit_out[:, :, start + head : start + head + HEAD_DIM] = unit.astype(BF16).reshape(
                count, CAP, HEAD_DIM
            )
        values = dot(held[...], value_ref[:, columns]).astype(BF16)
        value_out[:, :, columns] = values.reshape(count, CAP, WIDTH)


def project_first_kernel(*refs):
    route_ref, rows_ref, key_hbm, value_hbm, decay_ref, bias_ref = refs[:6]
    outs, (key_ref, value_ref, packed, held, sems) = refs[6:9], refs[9:]
    copies = []
    for at, start in enumerate(range(0, HALF, WIDTH)):
        columns = slice(start, start + WIDTH)
        for side, (far, close) in enumerate(((key_hbm, key_ref), (value_hbm, value_ref))):
            copies.append(
                pltpu.make_async_copy(far.at[:, columns], close.at[:, columns], sems.at[side, at])
            )
    for copy in copies:
        copy.start()
    pick = one_hot(membership(route_ref[...])[1], lax.axis_index("memory"))
    for start in range(0, D, WIDTH):
        select_columns(pick, rows_ref, slice(start, start + WIDTH), [packed])

    def ready(at):
        copies[2 * at].wait()
        copies[2 * at + 1].wait()

    project_parts([packed], decay_ref, bias_ref, outs, key_ref, value_ref, held, ready)


def project_next_kernel(count, *refs):
    key_ref, value_ref, decay_ref, bias_ref = refs[count : count + 4]
    outs, held = refs[count + 4 : count + 7], refs[count + 7]
    project_parts(
        refs[:count], decay_ref, bias_ref, outs, key_ref, value_ref, held, lambda at: None
    )


def projected(count):
    out = [near((count, CAP, HALF), BF16)] * 2 + [near((count, CAP, 128), F32)]
    return out, [pltpu.VMEM((count * CAP, D), BF16)]


def project_first(route, rows, *weights):
    out, scratch = projected(1)
    out = out + [near((D, HALF), BF16)] * 2 + [near((CAP, D), BF16)]
    scratch = scratch + [pltpu.SemaphoreType.DMA((2, HALF // WIDTH))]
    operands = (route, rows, *weights)
    return kernel_call(project_first_kernel, "project_first", out, scratch, 40, *operands, hbm=(2, 3))


def project(row_parts, *weights):
    count = len(row_parts)
    out, scratch = projected(count)
    kernel = functools.partial(project_next_kernel, count)
    return kernel_call(kernel, f"project_{count}", out, scratch, 12, *row_parts, *weights)


GROUPS = (((0, 0),), ((0, 1), (1, 0), (1, 1), (3, 0), (3, 1)), ((2, 0), (2, 1)))


def token_order(refs, held):
    owner, core = lax.axis_index("memory"), lax.axis_index("dp")
    for group, ref in zip(GROUPS, refs):
        for at, (shift, partner) in enumerate(group):
            held[position(shift, partner, owner, core)] = ref[at]


def head_columns(head):
    return slice(head * HEAD_DIM, (head + 1) * HEAD_DIM)


def place_in_context():
    context = lax.axis_index("context")
    return context >> 2, context & (RING - 1)


def two_parts(number):
    wide = jnp.broadcast_to(number, (TAIL, 128))
    high = wide.astype(BF16).astype(F32)
    return jnp.where(iota((TAIL, 128), 0) < TAIL // 2, high, wide - high).astype(BF16)


def from_parts(rows):
    wide = rows.astype(F32)
    return wide[:1] + wide[TAIL // 2 : TAIL // 2 + 1]


def state_kernel(*refs):
    unit_refs, value_refs, decay_refs = refs[0:3], refs[3:6], refs[6:9]
    messages = refs[9:13]
    column_out, row_out, units, values, decays, quarters = refs[13:]
    token_order(decay_refs, decays)
    offset, chunks = jnp.zeros((1, 128), F32), []
    for chunk in range(CHUNKS):
        chunks.append(decays[chunk] + offset)
        offset = chunks[chunk][CAP - 1 :]
    running = jnp.concatenate(chunks, axis=0)
    column_out[...] = running.reshape(CHUNKS, CAP, 128)
    row_out[...] = running.T[:HEADS]
    token_order(unit_refs, units)
    token_order(value_refs, values)
    last = running[SLOTS - 1 : SLOTS]
    fade = jnp.exp(last - running)
    for head in range(HEADS):
        unit = units[:, :, head_columns(head)].reshape(SLOTS, HEAD_DIM).astype(F32)
        faded = (unit * fade[:, head : head + 1]).astype(BF16)
        value = values[:, :, head_columns(head)].reshape(SLOTS, HEAD_DIM)
        state = dot_columns(faded, value).astype(BF16)
        at = head % 2 * HEAD_DIM
        quarters[head // 2, at : at + HEAD_DIM] = state
        tail = PIECE + head % 2 * TAIL
        quarters[head // 2, tail : tail + TAIL] = two_parts(last[:, head : head + 1])
    _, column = place_in_context()
    for shift in range(RING):
        messages[shift][...] = quarters[column ^ shift]


def block_state(units, values, decays):
    out = [near((PIECE + 2 * TAIL, 128), BF16)] * RING + [
        near((CHUNKS, CAP, 128), F32),
        near((HEADS, SLOTS), F32),
        near((CHUNKS, CAP, HALF), BF16),
        near((CHUNKS, CAP, HALF), BF16),
    ]
    scratch = [
        pltpu.VMEM((CHUNKS, CAP, 128), F32),
        pltpu.VMEM((RING, PIECE + 2 * TAIL, 128), BF16),
    ]
    return kernel_call(
        state_kernel, "block_state", out, scratch, 12, *units, *values, *decays
    )


def ring_order(refs, held, me):
    for shift in range(RING):
        held[me ^ shift] = refs[shift][...]


def row_prefix_kernel(*refs):
    pieces, (whole, before, faded, held) = refs[:RING], refs[RING:]
    ring_order(pieces, held, place_in_context()[1])
    for head in range(2):
        rows = slice(head * HEAD_DIM, (head + 1) * HEAD_DIM)
        tail = slice(PIECE + head * TAIL, PIECE + (head + 1) * TAIL)
        state, total = jnp.zeros((HEAD_DIM, 128), F32), jnp.zeros((1, 128), F32)
        for column in range(RING):
            before[column, rows] = state
            faded[column, head * 8 : head * 8 + 8] = jnp.broadcast_to(jnp.exp(total), (8, 128))
            ended = from_parts(held[column, tail])
            state = jnp.exp(ended) * state + held[column, rows].astype(F32)
            total = total + ended
        whole[rows] = state.astype(BF16)
        whole[tail] = two_parts(total)


def row_prefix(pieces):
    out = [
        near((PIECE + 2 * TAIL, 128), BF16),
        near((RING, PIECE, 128), F32),
        near((RING, 16, 128), F32),
    ]
    scratch = [pltpu.VMEM((RING, PIECE + 2 * TAIL, 128), BF16)]
    return kernel_call(row_prefix_kernel, "row_prefix", out, scratch, 8, *pieces)


def entry_kernel(*refs):
    pieces, (before, faded) = refs[:RING], refs[RING : RING + 2]
    out_refs, (held, entries) = refs[RING + 2 : 2 * RING + 2], refs[2 * RING + 2 :]
    row, mine = place_in_context()
    ring_order(pieces, held, row)
    for head in range(2):
        rows = slice(head * HEAD_DIM, (head + 1) * HEAD_DIM)
        tail = slice(PIECE + head * TAIL, PIECE + (head + 1) * TAIL)
        state = jnp.zeros((HEAD_DIM, 128), F32)
        for earlier in range(RING - 1):
            kept = jnp.exp(from_parts(held[earlier, tail])) * state
            kept = kept + held[earlier, rows].astype(F32)
            state = jnp.where(earlier < row, kept, state)
        for column in range(RING):
            fade = faded[column, head * 8 : head * 8 + 1]
            entries[column, rows] = (before[column, rows] + fade * state).astype(BF16)
    for shift in range(RING):
        out_refs[shift][...] = entries[mine ^ shift]


def entry_states(pieces, before, faded):
    out = [near((PIECE, 128), BF16)] * RING
    scratch = [
        pltpu.VMEM((RING, PIECE + 2 * TAIL, 128), BF16),
        pltpu.VMEM((RING, PIECE, 128), BF16),
    ]
    return kernel_call(entry_kernel, "entry_states", out, scratch, 8, *pieces, before, faded)


def inner_kernel(shifts, *refs):
    units, values, column_ref, row_ref = refs[0:4]
    query_refs, inner = refs[4:-1], refs[-1]
    owner = lax.axis_index("memory")
    count = len(shifts) * CAP
    for core in range(2):
        reach = -(-(core + 1) * OWNERS * CAP // 128) * 128
        chunks = [core * OWNERS + (owner ^ shift) for shift in shifts]
        running = jnp.concatenate([column_ref[chunk] for chunk in chunks], axis=0)
        place = jnp.concatenate([iota((CAP, reach), 0) + chunk * CAP for chunk in chunks], axis=0)
        causal = place >= iota((count, reach), 1)
        for head in range(HEADS):
            columns = head_columns(head)
            query = jnp.concatenate([query[core, :, columns] for query in query_refs], axis=0)
            unit = units[:, :, columns].reshape(SLOTS, HEAD_DIM)[:reach]
            value = values[:, :, columns].reshape(SLOTS, HEAD_DIM)[:reach]
            spread = running[:, head : head + 1] - row_ref[head : head + 1, :reach]
            weight = jnp.exp(jnp.where(causal, spread, -1e30))
            score = (dot_rows(query, unit) * weight).astype(BF16)
            inner[:, core, :, columns] = dot(score, value).reshape(len(shifts), CAP, HEAD_DIM)


def inner_reads(shifts, units, values, column, row, *queries):
    out = near((len(shifts), 2, CAP, HALF), F32)
    kernel = functools.partial(inner_kernel, shifts)
    name = f"inner_reads_{len(shifts)}"
    return kernel_call(kernel, name, out, (), 16, units, values, column, row, *queries)


def read_kernel(*refs):
    query_refs, inner_near, inner_far, column_ref = refs[0:4], refs[4], refs[5], refs[6]
    out_refs, entries = refs[11:15], refs[15]
    ring_order(refs[7:11], entries, place_in_context()[1])
    owner = lax.axis_index("memory")
    inners = {shift: inner_near.at[at] for at, shift in enumerate(NEAR)}
    inners[FAR] = inner_far.at[0]
    pairs = [(shift, core) for shift in range(OWNERS) for core in range(2)]
    fade = jnp.concatenate([column_ref[c * OWNERS + (owner ^ s)] for s, c in pairs], axis=0)
    fade = jnp.exp(fade)
    for head in range(HEADS):
        columns = head_columns(head)
        query = jnp.concatenate([query_refs[s][c, :, columns] for s, c in pairs], axis=0)
        entry = entries[head // 2, head % 2 * HEAD_DIM : (head % 2 + 1) * HEAD_DIM]
        carried = fade[:, head : head + 1] * dot(query, entry)
        for at, (s, c) in enumerate(pairs):
            read = inners[s][c, :, columns] + carried[at * CAP : (at + 1) * CAP]
            out_refs[s][c, :, columns] = read.astype(BF16)


def read_out(queries, inner_near, inner_far, column, entry):
    out = [near((2, CAP, HALF), BF16)] * OWNERS
    scratch = [pltpu.VMEM((RING, PIECE, 128), BF16)]
    operands = (*queries, inner_near, inner_far, column, *entry)
    return kernel_call(read_kernel, "read_out", out, scratch, 12, *operands)


def mix_near_kernel(gates_ref, picks_ref, *refs):
    partial = refs[-1]
    core = lax.axis_index("dp")
    for side in range(2):
        total = jnp.zeros((ROWS, HALF), F32)
        for at, shift in enumerate(NEAR):
            reads = refs[side * len(NEAR) + at][core]
            total = total + gates_ref[:, shift : shift + 1] * dot(picks_ref[shift, :, :CAP], reads)
        partial[side] = total


def mix_near(gates, picks, own, other):
    out = near((2, ROWS, HALF), F32)
    return kernel_call(mix_near_kernel, "mix_near", out, (), 12, gates, picks, *own, *other)


def mix_kernel(gates_ref, picks_ref, gain_ref, partial, own, other, out_ref):
    core = lax.axis_index("dp")
    for side, reads in enumerate((own, other)):
        start = (core ^ side) * HALF
        far = dot(picks_ref[FAR, :, :CAP], reads[core])
        mixture = partial[side] + gates_ref[:, FAR : FAR + 1] * far
        for head in range(HEADS):
            columns = pl.ds(pl.multiple_of(start + head * HEAD_DIM, HEAD_DIM), HEAD_DIM)
            mix = mixture[:, head_columns(head)]
            scale = lax.rsqrt(jnp.mean(mix * mix, axis=1, keepdims=True) + 1e-05)
            out_ref[:, columns] = (mix * scale * gain_ref[:, columns]).astype(BF16)


def mix_reads(gates, picks, gain, partial, own, other):
    out = jax.ShapeDtypeStruct((ROWS, 2 * HALF), BF16)
    return kernel_call(
        mix_kernel, "mix_reads", out, (), 12, gates, picks, gain, partial, own, other
    )


def after(array, *first):
    return lax.optimization_barrier((array, *first))[0]


def hop(array, shift):
    return lax.ppermute(array, "memory", [(i, i ^ shift) for i in range(OWNERS)])


def exchange(arrays, stride):
    out = [arrays[0]]
    for shift in (1, 2, 3):
        pairs = [(i, i ^ shift * stride) for i in range(RING * RING)]
        out.append(lax.ppermute(arrays[shift], "context", pairs))
    return out


def swap(array):
    return lax.ppermute(array, "dp", [(0, 1), (1, 0)])


def shards(
    hidden,
    queries,
    route_ids,
    router_weight,
    key_weight,
    value_weight,
    decay_weight,
    decay_bias,
    norm_gain,
):
    rows, query_rows, route = hidden[0], queries[0], route_ids[0].T
    weights = (key_weight[0], value_weight[0], decay_weight[0].T, decay_bias)

    packed = dict(zip(AWAY, pack_rows(route, rows)))
    arrived = {shift: hop(packed[shift], shift) for shift in (1, 3)}
    other_route, other_query = swap(route), swap(query_rows)
    first = project_first(route, rows, *weights)
    other = {0: swap(first[5])}
    weights = (first[3], first[4], *weights[2:])
    packed_query = pack_queries(
        after(route, first[2]), other_route, query_rows, other_query, rows, router_weight.T
    )
    gates, picks = packed_query[OWNERS:]
    for shift in (1, 3):
        arrived[shift] = after(arrived[shift], gates)
    arrived[2] = hop(after(packed[2], arrived[1], arrived[3]), 2)
    for shift in (1, 3):
        other[shift] = swap(arrived[shift])
    near_rows = [other[0], arrived[1], other[1], arrived[3], other[3]]
    second = project(near_rows, *weights)
    arrived[2] = after(arrived[2], second[2])
    other[2] = swap(arrived[2])
    query_in = {0: packed_query[0]}
    for shift in (1, 3):
        query_in[shift] = hop(after(packed_query[shift], arrived[2]), shift)
    third = project([arrived[2], other[2]], *weights)
    units, values, decays = zip(first[:3], second, third)

    *messages, column, row, units, values = block_state(units, values, decays)
    pieces = exchange(messages, 1)
    blocks = (units, values, column, row)
    inner_near = inner_reads(NEAR, *blocks, *[query_in[shift] for shift in NEAR])
    pieces[0] = after(pieces[0], inner_near)
    whole, before, faded = row_prefix(pieces)
    query_in[FAR] = hop(after(packed_query[FAR], whole), FAR)
    totals = exchange([whole] * RING, RING)
    entry = exchange(entry_states(totals, before, faded), 1)
    inner_far = inner_reads((FAR,), *blocks, query_in[FAR])
    queries = [query_in[shift] for shift in range(OWNERS)]
    reads = read_out(queries, inner_near, inner_far, column, entry)

    own = [reads[0]] + [hop(reads[shift], shift) for shift in (1, 2, 3)]
    paired = [swap(part) for part in own]
    partial = mix_near(gates, picks, [own[i] for i in NEAR], [paired[i] for i in NEAR])
    return mix_reads(gates, picks, norm_gain[None], partial, own[FAR], paired[FAR])[None]


def solution(mesh):
    in_specs = (
        P(("context", "dp"), "memory", None),
        P(("context", "dp"), "memory", None),
        P(("context", "dp"), "memory", None),
        P(),
        P("memory", None, "dp"),
        P("memory", None, "dp"),
        P("memory", None, "dp"),
        P("memory", "dp"),
        P(),
    )
    out_specs = P(("context", "dp"), "memory", None)
    return jax.shard_map(shards, mesh=mesh, in_specs=in_specs, out_specs=out_specs, check_vma=False)
```

```python
import functools

import jax
import jax.numpy as jnp
from jax import lax
from jax.experimental import pallas as pl
from jax.experimental.pallas import tpu as pltpu
from jax.sharding import PartitionSpec as P

D = 4096
HEAD_DIM = 128
CAP = 80
ROWS = 128
OWNERS = 4
CHUNKS = 8
SLOTS = CHUNKS * CAP
HALF = 1024
HEADS = HALF // HEAD_DIM
EMPTY = 64.0
PAD = 128
PACKS = 4
NEAR, FAR = (0, 1, 3), 2
AWAY = (1, 3, 2)
RING = 4
PIECE = HALF // RING
TAIL = 16
F32 = jnp.float32
BF16 = jnp.bfloat16
MIB = 1 << 20


def iota(shape, axis):
    return lax.broadcasted_iota(jnp.int32, shape, axis)


def dot(a, b):
    return jnp.dot(a, b, preferred_element_type=F32)


def dot_rows(a, b):
    return lax.dot_general(a, b, (((1,), (1,)), ((), ())), preferred_element_type=F32)


def dot_columns(a, b):
    return lax.dot_general(a, b, (((0,), (0,)), ((), ())), preferred_element_type=F32)


def near(shape, dtype):
    return pltpu.VMEM(shape, dtype)


def position(shift, partner, owner, core):
    return (core ^ partner) * OWNERS + (owner ^ shift)


def membership(route):
    memory = iota((8, ROWS), 0)
    named = ((route[0:1] == memory) | (route[1:2] == memory)).astype(F32)
    before = (iota((ROWS, ROWS), 0) < iota((ROWS, ROWS), 1)).astype(F32).astype(BF16)
    slot = dot(named.astype(BF16), before)
    return named, jnp.where(named > 0.0, slot, -1.0)


def one_hot(place, memory, slots=CAP):
    mine = jnp.sum(jnp.where(iota(place.shape, 0) == memory, place, 0.0), axis=0, keepdims=True)
    return (iota((slots, ROWS), 0).astype(F32) == mine).astype(F32)


def kernel_call(kernel, name, out_shape, scratch, limit, *operands, hbm=(), moved=1):
    spaces = [pltpu.HBM if at in hbm else pltpu.VMEM for at in range(len(operands))]
    return pl.pallas_call(
        kernel,
        out_shape=out_shape,
        in_specs=[pl.BlockSpec(memory_space=space) for space in spaces],
        out_specs=jax.tree.map(lambda _: pl.BlockSpec(memory_space=pltpu.VMEM), out_shape),
        scratch_shapes=scratch,
        compiler_params=pltpu.CompilerParams(vmem_limit_bytes=limit * MIB),
        cost_estimate=pl.CostEstimate(flops=1, bytes_accessed=moved, transcendentals=0),
        name=name,
    )(*operands)


def select_columns(pick, rows_ref, columns, out_refs):
    part = dot(pick.astype(BF16), rows_ref[:, columns])
    if columns.start == 0:
        empty = jnp.sum(pick, axis=1, keepdims=True) == 0.0
        first_lane = iota((part.shape[0], HEAD_DIM), 1) == 0
        marked = jnp.where(first_lane & empty, EMPTY, part[:, :HEAD_DIM])
        part = jnp.concatenate([marked, part[:, HEAD_DIM:]], axis=1)
    part = part.astype(BF16)
    for to, out_ref in enumerate(out_refs):
        out_ref[:, columns] = part[to * CAP : (to + 1) * CAP]


def pack_rows_kernel(route_hbm, rows_hbm, *refs):
    out_refs, (route_ref, rows_ref, sems) = refs[: len(AWAY)], refs[len(AWAY) :]
    owner = lax.axis_index("memory")
    width = D // PACKS
    route_copy = pltpu.make_async_copy(route_hbm, route_ref, sems.at[PACKS])
    route_copy.start()
    parts, copies = [slice(at * width, (at + 1) * width) for at in range(PACKS)], []
    for at, columns in enumerate(parts):
        copies.append(
            pltpu.make_async_copy(rows_hbm.at[:, columns], rows_ref.at[:, columns], sems.at[at])
        )
        copies[at].start()
    route_copy.wait()
    place = membership(route_ref[...])[1]
    pick = jnp.concatenate([one_hot(place, owner ^ shift) for shift in AWAY], axis=0)
    for copy, columns in zip(copies, parts):
        copy.wait()
        select_columns(pick, rows_ref, columns, out_refs)
    out_refs[AWAY.index(FAR)][:, D:] = jnp.zeros((CAP, PAD), BF16)


def pack_rows(route, rows):
    out = [near((CAP, D + PAD * (shift == FAR)), BF16) for shift in AWAY]
    scratch = [
        pltpu.VMEM((2, ROWS), jnp.int32),
        pltpu.VMEM((ROWS, D), BF16),
        pltpu.SemaphoreType.DMA((PACKS + 1,)),
    ]
    return kernel_call(pack_rows_kernel, "pack_rows", out, scratch, 56, route, rows, hbm=(0, 1))


def pack_queries_kernel(
    route_ref, other_route_ref, query_ref, other_query_ref, rows_ref, router_ref, *out_refs
):
    owner, core = lax.axis_index("memory"), lax.axis_index("dp")
    gates_ref, picks_ref = out_refs[OWNERS:]
    mine = pl.multiple_of(core * HALF, HALF)
    for side, (routes, queries) in enumerate(
        ((route_ref, query_ref), (other_route_ref, other_query_ref))
    ):
        named, place = membership(routes[...])
        pick = jnp.concatenate(
            [one_hot(place, owner ^ shift) for shift in range(OWNERS)], axis=0
        ).astype(BF16)
        part = dot(pick, queries[:, pl.ds(mine, HALF)]).astype(BF16)
        for shift in range(OWNERS):
            out_refs[shift][core ^ side] = part[shift * CAP : (shift + 1) * CAP]
        if side == 0:
            for shift in range(OWNERS):
                picks_ref[shift] = one_hot(place, owner ^ shift, 128).T.astype(BF16)
            score = dot_rows(router_ref[...], rows_ref[...])
            chosen = jax.nn.sigmoid(score) * named[:OWNERS]
            gates = chosen / jnp.sum(chosen, axis=0, keepdims=True)
            memory = iota((OWNERS, ROWS), 0)
            by_shift = [
                jnp.sum(jnp.where(memory == owner ^ shift, gates, 0.0), axis=0, keepdims=True)
                for shift in range(OWNERS)
            ]
            by_shift.append(jnp.zeros((128 - OWNERS, ROWS), F32))
            gates_ref[...] = jnp.concatenate(by_shift, axis=0).T


def pack_queries(route, other_route, queries, other_queries, rows, router_weight):
    out = [near((2, CAP, HALF), BF16)] * OWNERS
    out = out + [near((ROWS, 128), F32), near((OWNERS, ROWS, 128), BF16)]
    operands = (route, other_route, queries, other_queries, rows, router_weight)
    return kernel_call(
        pack_queries_kernel, "pack_queries", out, (), 12, *operands, moved=4 * MIB
    )


def log_sigmoid(x):
    small = jnp.exp(-jnp.abs(x))
    near = 1.0 + small
    tiny = near == 1.0
    log1p = jnp.where(tiny, small, jnp.log(near) * (small / jnp.where(tiny, 1.0, near - 1.0)))
    return jnp.minimum(x, 0.0) - log1p


WIDTH = 512
LONGEST = -128.0


def project_parts(row_refs, decay_ref, bias_ref, outs, key_ref, value_ref, held, ready):
    count = len(row_refs)
    unit_out, value_out, decay_out = outs
    lives = []
    for at in range(count):
        rows = slice(at * CAP, (at + 1) * CAP)
        head = row_refs[at][:, :HEAD_DIM].astype(F32)
        lives.append(head[:, :1] < EMPTY / 2)
        held[rows, :HEAD_DIM] = jnp.where(lives[at], head, 0.0).astype(BF16)
        held[rows, HEAD_DIM:] = row_refs[at][:, HEAD_DIM:D]
    decay = log_sigmoid(dot_rows(held[...], decay_ref[...]) + bias_ref[...])
    upto = (iota((CAP, CAP), 0) >= iota((CAP, CAP), 1)).astype(F32).astype(BF16)
    for at in range(count):
        kept = jnp.maximum(decay[at * CAP : (at + 1) * CAP], LONGEST)
        kept = jnp.where(lives[at], kept, 0.0)
        kept = jnp.concatenate([kept, jnp.zeros((CAP, 128 - HEADS), F32)], axis=1)
        total = jnp.zeros((CAP, 128), F32)
        for _ in range(3):
            part = kept.astype(BF16)
            kept = kept - part.astype(F32)
            total = total + dot(upto, part)
        decay_out[at] = total
    for start in range(0, HALF, WIDTH):
        ready(start // WIDTH)
        columns = slice(start, start + WIDTH)
        keys = dot(held[...], key_ref[:, columns]).astype(BF16).astype(F32)
        for head in range(0, WIDTH, HEAD_DIM):
            key = keys[:, head : head + HEAD_DIM]
            unit = key * lax.rsqrt(jnp.sum(key * key, axis=1, keepdims=True) + 1e-06)
            unit_out[:, :, start + head : start + head + HEAD_DIM] = unit.astype(BF16).reshape(
                count, CAP, HEAD_DIM
            )
        values = dot(held[...], value_ref[:, columns]).astype(BF16)
        value_out[:, :, columns] = values.reshape(count, CAP, WIDTH)


def project_first_kernel(*refs):
    route_ref, rows_ref, key_hbm, value_hbm, decay_ref, bias_ref = refs[:6]
    outs, (key_ref, value_ref, packed, held, sems) = refs[6:9], refs[9:]
    copies = []
    for at, start in enumerate(range(0, HALF, WIDTH)):
        columns = slice(start, start + WIDTH)
        for side, (far, close) in enumerate(((key_hbm, key_ref), (value_hbm, value_ref))):
            copies.append(
                pltpu.make_async_copy(far.at[:, columns], close.at[:, columns], sems.at[side, at])
            )
    for copy in copies:
        copy.start()
    pick = one_hot(membership(route_ref[...])[1], lax.axis_index("memory"))
    for start in range(0, D, WIDTH):
        select_columns(pick, rows_ref, slice(start, start + WIDTH), [packed])

    def ready(at):
        copies[2 * at].wait()
        copies[2 * at + 1].wait()

    project_parts([packed], decay_ref, bias_ref, outs, key_ref, value_ref, held, ready)


def project_next_kernel(count, *refs):
    key_ref, value_ref, decay_ref, bias_ref = refs[count : count + 4]
    outs, held = refs[count + 4 : count + 7], refs[count + 7]
    project_parts(
        refs[:count], decay_ref, bias_ref, outs, key_ref, value_ref, held, lambda at: None
    )


def projected(count):
    out = [near((count, CAP, HALF), BF16)] * 2 + [near((count, CAP, 128), F32)]
    return out, [pltpu.VMEM((count * CAP, D), BF16)]


def project_first(route, rows, *weights):
    out, scratch = projected(1)
    out = out + [near((D, HALF), BF16)] * 2 + [near((CAP, D), BF16)]
    scratch = scratch + [pltpu.SemaphoreType.DMA((2, HALF // WIDTH))]
    operands = (route, rows, *weights)
    return kernel_call(project_first_kernel, "project_first", out, scratch, 40, *operands, hbm=(2, 3))


def project(row_parts, *weights):
    count = len(row_parts)
    out, scratch = projected(count)
    kernel = functools.partial(project_next_kernel, count)
    return kernel_call(kernel, f"project_{count}", out, scratch, 12, *row_parts, *weights)


GROUPS = (((0, 0),), ((0, 1), (1, 0), (1, 1), (3, 0), (3, 1)), ((2, 0), (2, 1)))


def token_order(refs, held):
    owner, core = lax.axis_index("memory"), lax.axis_index("dp")
    for group, ref in zip(GROUPS, refs):
        for at, (shift, partner) in enumerate(group):
            held[position(shift, partner, owner, core)] = ref[at]


def head_columns(head):
    return slice(head * HEAD_DIM, (head + 1) * HEAD_DIM)


def place_in_context():
    context = lax.axis_index("context")
    return context >> 2, context & (RING - 1)


def two_parts(number):
    wide = jnp.broadcast_to(number, (TAIL, 128))
    high = wide.astype(BF16).astype(F32)
    return jnp.where(iota((TAIL, 128), 0) < TAIL // 2, high, wide - high).astype(BF16)


def from_parts(rows):
    wide = rows.astype(F32)
    return wide[:1] + wide[TAIL // 2 : TAIL // 2 + 1]


def state_kernel(*refs):
    unit_refs, value_refs, decay_refs = refs[0:3], refs[3:6], refs[6:9]
    messages = refs[9:13]
    column_out, row_out, units, values, decays, quarters = refs[13:]
    token_order(decay_refs, decays)
    offset, chunks = jnp.zeros((1, 128), F32), []
    for chunk in range(CHUNKS):
        chunks.append(decays[chunk] + offset)
        offset = chunks[chunk][CAP - 1 :]
    running = jnp.concatenate(chunks, axis=0)
    column_out[...] = running.reshape(CHUNKS, CAP, 128)
    row_out[...] = running.T[:HEADS]
    token_order(unit_refs, units)
    token_order(value_refs, values)
    last = running[SLOTS - 1 : SLOTS]
    fade = jnp.exp(last - running)
    for head in range(HEADS):
        unit = units[:, :, head_columns(head)].reshape(SLOTS, HEAD_DIM).astype(F32)
        faded = (unit * fade[:, head : head + 1]).astype(BF16)
        value = values[:, :, head_columns(head)].reshape(SLOTS, HEAD_DIM)
        state = dot_columns(faded, value).astype(BF16)
        at = head % 2 * HEAD_DIM
        quarters[head // 2, at : at + HEAD_DIM] = state
        tail = PIECE + head % 2 * TAIL
        quarters[head // 2, tail : tail + TAIL] = two_parts(last[:, head : head + 1])
    _, column = place_in_context()
    for shift in range(RING):
        messages[shift][...] = quarters[column ^ shift]


def block_state(units, values, decays):
    out = [near((PIECE + 2 * TAIL, 128), BF16)] * RING + [
        near((CHUNKS, CAP, 128), F32),
        near((HEADS, SLOTS), F32),
        near((CHUNKS, CAP, HALF), BF16),
        near((CHUNKS, CAP, HALF), BF16),
    ]
    scratch = [
        pltpu.VMEM((CHUNKS, CAP, 128), F32),
        pltpu.VMEM((RING, PIECE + 2 * TAIL, 128), BF16),
    ]
    return kernel_call(
        state_kernel, "block_state", out, scratch, 12, *units, *values, *decays
    )


def ring_order(refs, held, me):
    for shift in range(RING):
        held[me ^ shift] = refs[shift][...]


def row_prefix_kernel(*refs):
    pieces, (whole, before, faded, held) = refs[:RING], refs[RING:]
    ring_order(pieces, held, place_in_context()[1])
    for head in range(2):
        rows = slice(head * HEAD_DIM, (head + 1) * HEAD_DIM)
        tail = slice(PIECE + head * TAIL, PIECE + (head + 1) * TAIL)
        state, total = jnp.zeros((HEAD_DIM, 128), F32), jnp.zeros((1, 128), F32)
        for column in range(RING):
            before[column, rows] = state
            faded[column, head * 8 : head * 8 + 8] = jnp.broadcast_to(jnp.exp(total), (8, 128))
            ended = from_parts(held[column, tail])
            state = jnp.exp(ended) * state + held[column, rows].astype(F32)
            total = total + ended
        whole[rows] = state.astype(BF16)
        whole[tail] = two_parts(total)


def row_prefix(pieces):
    out = [
        near((PIECE + 2 * TAIL, 128), BF16),
        near((RING, PIECE, 128), F32),
        near((RING, 16, 128), F32),
    ]
    scratch = [pltpu.VMEM((RING, PIECE + 2 * TAIL, 128), BF16)]
    return kernel_call(row_prefix_kernel, "row_prefix", out, scratch, 8, *pieces)


def entry_kernel(*refs):
    pieces, (before, faded) = refs[:RING], refs[RING : RING + 2]
    out_refs, (held, entries) = refs[RING + 2 : 2 * RING + 2], refs[2 * RING + 2 :]
    row, mine = place_in_context()
    ring_order(pieces, held, row)
    for head in range(2):
        rows = slice(head * HEAD_DIM, (head + 1) * HEAD_DIM)
        tail = slice(PIECE + head * TAIL, PIECE + (head + 1) * TAIL)
        state = jnp.zeros((HEAD_DIM, 128), F32)
        for earlier in range(RING - 1):
            kept = jnp.exp(from_parts(held[earlier, tail])) * state
            kept = kept + held[earlier, rows].astype(F32)
            state = jnp.where(earlier < row, kept, state)
        for column in range(RING):
            fade = faded[column, head * 8 : head * 8 + 1]
            entries[column, rows] = (before[column, rows] + fade * state).astype(BF16)
    for shift in range(RING):
        out_refs[shift][...] = entries[mine ^ shift]


def entry_states(pieces, before, faded):
    out = [near((PIECE, 128), BF16)] * RING
    scratch = [
        pltpu.VMEM((RING, PIECE + 2 * TAIL, 128), BF16),
        pltpu.VMEM((RING, PIECE, 128), BF16),
    ]
    return kernel_call(entry_kernel, "entry_states", out, scratch, 8, *pieces, before, faded)


def inner_kernel(shifts, *refs):
    units, values, column_ref, row_ref = refs[0:4]
    query_refs, inner = refs[4:-1], refs[-1]
    owner = lax.axis_index("memory")
    cores = [(0, 1)] if shifts == (FAR,) else [(0,), (1,)]
    for group in cores:
        reach = -(-(group[-1] + 1) * OWNERS * CAP // 128) * 128
        tiles = [(at, shift, core) for core in group for at, shift in enumerate(shifts)]
        chunks = [core * OWNERS + (owner ^ shift) for _, shift, core in tiles]
        running = jnp.concatenate([column_ref[chunk] for chunk in chunks], axis=0)
        place = jnp.concatenate([iota((CAP, reach), 0) + chunk * CAP for chunk in chunks], axis=0)
        causal = place >= iota(place.shape, 1)
        for head in range(HEADS):
            columns = head_columns(head)
            query = jnp.concatenate([query_refs[at][c, :, columns] for at, _, c in tiles], axis=0)
            unit = units[:, :, columns].reshape(SLOTS, HEAD_DIM)[:reach]
            value = values[:, :, columns].reshape(SLOTS, HEAD_DIM)[:reach]
            spread = running[:, head : head + 1] - row_ref[head : head + 1, :reach]
            weight = jnp.exp(jnp.where(causal, spread, -1e30))
            score = (dot_rows(query, unit) * weight).astype(BF16)
            result = dot(score, value)
            for row, (at, _, core) in enumerate(tiles):
                inner[at, core, :, columns] = result[row * CAP : (row + 1) * CAP]


def inner_reads(shifts, units, values, column, row, *queries):
    out = near((len(shifts), 2, CAP, HALF), F32)
    kernel = functools.partial(inner_kernel, shifts)
    name = f"inner_reads_{len(shifts)}"
    return kernel_call(kernel, name, out, (), 16, units, values, column, row, *queries)


def read_kernel(*refs):
    query_refs, inner_near, inner_far, column_ref = refs[0:4], refs[4], refs[5], refs[6]
    out_refs, entries = refs[11:15], refs[15]
    ring_order(refs[7:11], entries, place_in_context()[1])
    owner = lax.axis_index("memory")
    inners = {shift: inner_near.at[at] for at, shift in enumerate(NEAR)}
    inners[FAR] = inner_far.at[0]
    pairs = [(shift, core) for shift in range(OWNERS) for core in range(2)]
    fade = jnp.concatenate([column_ref[c * OWNERS + (owner ^ s)] for s, c in pairs], axis=0)
    fade = jnp.exp(fade)
    for head in range(HEADS):
        columns = head_columns(head)
        query = jnp.concatenate([query_refs[s][c, :, columns] for s, c in pairs], axis=0)
        entry = entries[head // 2, head % 2 * HEAD_DIM : (head % 2 + 1) * HEAD_DIM]
        carried = fade[:, head : head + 1] * dot(query, entry)
        for at, (s, c) in enumerate(pairs):
            read = inners[s][c, :, columns] + carried[at * CAP : (at + 1) * CAP]
            out_refs[s][c, :, columns] = read.astype(BF16)


def read_out(queries, inner_near, inner_far, column, entry):
    out = [near((2, CAP, HALF), BF16)] * OWNERS
    scratch = [pltpu.VMEM((RING, PIECE, 128), BF16)]
    operands = (*queries, inner_near, inner_far, column, *entry)
    return kernel_call(read_kernel, "read_out", out, scratch, 12, *operands)


def mix_near_kernel(gates_ref, picks_ref, *refs):
    partial = refs[-1]
    core = lax.axis_index("dp")
    for side in range(2):
        total = jnp.zeros((ROWS, HALF), F32)
        for at, shift in enumerate(NEAR):
            reads = refs[side * len(NEAR) + at][core]
            total = total + gates_ref[:, shift : shift + 1] * dot(picks_ref[shift, :, :CAP], reads)
        partial[side] = total


def mix_near(gates, picks, own, other):
    out = near((2, ROWS, HALF), F32)
    return kernel_call(mix_near_kernel, "mix_near", out, (), 12, gates, picks, *own, *other)


def mix_kernel(gates_ref, picks_ref, gain_ref, partial, own, other, out_ref):
    core = lax.axis_index("dp")
    for side, reads in enumerate((own, other)):
        start = (core ^ side) * HALF
        far = dot(picks_ref[FAR, :, :CAP], reads[core])
        mixture = partial[side] + gates_ref[:, FAR : FAR + 1] * far
        for head in range(HEADS):
            columns = pl.ds(pl.multiple_of(start + head * HEAD_DIM, HEAD_DIM), HEAD_DIM)
            mix = mixture[:, head_columns(head)]
            scale = lax.rsqrt(jnp.mean(mix * mix, axis=1, keepdims=True) + 1e-05)
            out_ref[:, columns] = (mix * scale * gain_ref[:, columns]).astype(BF16)


def mix_reads(gates, picks, gain, partial, own, other):
    out = jax.ShapeDtypeStruct((ROWS, 2 * HALF), BF16)
    return kernel_call(
        mix_kernel, "mix_reads", out, (), 12, gates, picks, gain, partial, own, other
    )


def after(array, *first):
    return lax.optimization_barrier((array, *first))[0]


def hop(array, shift):
    return lax.ppermute(array, "memory", [(i, i ^ shift) for i in range(OWNERS)])


def exchange(arrays, stride):
    out = [arrays[0]]
    for shift in (1, 2, 3):
        pairs = [(i, i ^ shift * stride) for i in range(RING * RING)]
        out.append(lax.ppermute(arrays[shift], "context", pairs))
    return out


def swap(array):
    return lax.ppermute(array, "dp", [(0, 1), (1, 0)])


def shards(
    hidden,
    queries,
    route_ids,
    router_weight,
    key_weight,
    value_weight,
    decay_weight,
    decay_bias,
    norm_gain,
):
    rows, query_rows, route = hidden[0], queries[0], route_ids[0].T
    weights = (key_weight[0], value_weight[0], decay_weight[0].T, decay_bias)

    packed = dict(zip(AWAY, pack_rows(route, rows)))
    arrived = {shift: hop(packed[shift], shift) for shift in (1, 3)}
    other_route, other_query = swap(route), swap(query_rows)
    first = project_first(route, rows, *weights)
    other = {0: swap(first[5])}
    weights = (first[3], first[4], *weights[2:])
    packed_query = pack_queries(
        after(route, first[2]), other_route, query_rows, other_query, rows, router_weight.T
    )
    gates, picks = packed_query[OWNERS:]
    for shift in (1, 3):
        arrived[shift] = after(arrived[shift], gates)
    arrived[2] = hop(after(packed[2], arrived[1], arrived[3]), 2)
    for shift in (1, 3):
        other[shift] = swap(arrived[shift])
    near_rows = [other[0], arrived[1], other[1], arrived[3], other[3]]
    second = project(near_rows, *weights)
    arrived[2] = after(arrived[2], second[2])
    other[2] = swap(arrived[2])
    query_in = {0: packed_query[0]}
    for shift in (1, 3):
        query_in[shift] = hop(after(packed_query[shift], arrived[2]), shift)
    third = project([arrived[2], other[2]], *weights)
    units, values, decays = zip(first[:3], second, third)

    *messages, column, row, units, values = block_state(units, values, decays)
    pieces = exchange(messages, 1)
    blocks = (units, values, column, row)
    inner_near = inner_reads(NEAR, *blocks, *[query_in[shift] for shift in NEAR])
    pieces[0] = after(pieces[0], inner_near)
    whole, before, faded = row_prefix(pieces)
    query_in[FAR] = hop(after(packed_query[FAR], whole), FAR)
    totals = exchange([whole] * RING, RING)
    entry = exchange(entry_states(totals, before, faded), 1)
    inner_far = inner_reads((FAR,), *blocks, query_in[FAR])
    queries = [query_in[shift] for shift in range(OWNERS)]
    reads = read_out(queries, inner_near, inner_far, column, entry)

    own = [reads[0]] + [hop(reads[shift], shift) for shift in (1, 2, 3)]
    paired = [swap(part) for part in own]
    partial = mix_near(gates, picks, [own[i] for i in NEAR], [paired[i] for i in NEAR])
    return mix_reads(gates, picks, norm_gain[None], partial, own[FAR], paired[FAR])[None]


def solution(mesh):
    in_specs = (
        P(("context", "dp"), "memory", None),
        P(("context", "dp"), "memory", None),
        P(("context", "dp"), "memory", None),
        P(),
        P("memory", None, "dp"),
        P("memory", None, "dp"),
        P("memory", None, "dp"),
        P("memory", "dp"),
        P(),
    )
    out_specs = P(("context", "dp"), "memory", None)
    return jax.shard_map(shards, mesh=mesh, in_specs=in_specs, out_specs=out_specs, check_vma=False)
```
